128 devices in a mesh: coarse: 8 (over x, core), fine: 16 (over y, z).
Axes of the slice: x: 4, y: 4, z: 4, core: 2. Of those that a mesh axis runs over, the one named last changes fastest.
Arguments:
- c_old: float32 [32, 128, 256], P('coarse', 'fine'), may hold values from -6 to 6
- s_old: float32 [16, 32, 128, 256], P(None, 'coarse', 'fine'), may hold values from -6 to 6
- rate_time: float32 [16, 32, 128, 256], P(None, 'coarse', 'fine'), may hold values from 0.01 to 100
- capacity: float32 [16], replicated, may hold values from 0.05 to 0.5
- agg_count: int32 [128], P(('coarse', 'fine')), may hold values from 1 to 256, 16384 in all
- coarse_order: int32 [16384], replicated, may hold values from 0 to 16383, as said below
- coarse_cols: int32 [8, 16384], P(None, 'coarse'), may hold values from 0 to 16383
- coarse_off: float32 [8, 16384], P(None, 'coarse'), may hold values from -16 to 16
- coarse_diag: float32 [16384], P('coarse'), may hold values from 160 to 256
Outputs:
- mobile: float32 [32, 128, 256], P('coarse', 'fine')
- immobile: float32 [16, 32, 128, 256], P(None, 'coarse', 'fine')
The draws below stay inside these ranges and needn't reach their ends.
Inputs may be any that keep to these rules, and one draw needn't show every extreme that they name: agg_count sums to 16384, and some subdomain has exactly 256 aggregates. coarse_order names each coarse unknown once; aggregates g and h name unknowns of the same block of 128 consecutive unknowns only if g - h is a multiple of 128, so one subdomain names at most 2 unknowns of one block, and the subdomain with 256 aggregates names exactly 2 of some block.
All inputs are finite; a program needn't handle non-finite values. No bound on the sum of `agg_count` on one device may be relied on, other than what follows from the above.
Results may differ from the reference program's by a relative error of at most 0.0003.
Values sent between devices are 32-bit elements; how exact they have to be, the bound alone decides.
No kernel may reach another device: no remote copies, remote signals or barrier semaphores. Data moves between devices by JAX's collectives and lax.ppermute only.
A program may use at most 64 MiB of HBM per device.

```python
import math
import jax
import jax.numpy as jnp
import numpy as np
from jax import lax

CX = 4
CY = 8
CZ = 256
RATES = 16
KC = 8
KJ = 3
ITERS = 2
AGG_MEAN = 128
AGG_CAP = 256
NC = 16384
GX = 32
GY = 128
N_COARSE = 8
N_FINE = 16
DEVICES = 128


def shuffle_places(subkey):
    return jax.random.permutation(subkey, AGG_MEAN)


def draw_coarse_order(key, part):
    devices = NC // AGG_MEAN
    holders = jax.random.permutation(jax.random.fold_in(key, 11), devices).astype(jnp.int32)
    subkeys = jax.random.split(jax.random.fold_in(key, 12), devices)
    places = jax.vmap(shuffle_places)(subkeys).astype(jnp.int32)
    numbers = jnp.arange(NC, dtype=jnp.int32)
    holder = holders[numbers % devices]
    return (holder * AGG_MEAN + places[holder, numbers // devices]).astype(jnp.int32)


def plant(values, key, least, top_value):
    longest = values.shape.index(max(values.shape))
    spots = []
    for shift in (0, 1):
        where = [jax.random.randint(jax.random.fold_in(key, axis), (), 0, length) for axis, length in enumerate(values.shape)]
        where[longest] = (where[longest] + shift) % values.shape[longest]
        spots.append(tuple(where))
    return values.at[spots[0]].set(least).at[spots[1]].set(top_value)


def block_scale(stream_key, dims, shards, smallest, largest):
    gain = 1.0
    for dim, blocks in shards:
        steps = jax.random.uniform(jax.random.fold_in(jax.random.fold_in(stream_key, 6), dim), (blocks,), jnp.float32, smallest / len(shards), largest / len(shards))
        gain = gain * jnp.repeat(jnp.exp(steps), dims[dim] // blocks).reshape((-1,) + (1,) * (len(dims) - 1 - dim))
    return gain


def split_up(number_of, total, limit, lean):
    weights = [(1 << 20) // math.isqrt(standing ** lean) + 1 for standing in range(2, number_of + 1)]
    spare, holding = total - limit - (number_of - 1), [1] * (number_of - 1)
    while spare > 0:
        movable = [i for i in range(number_of - 1) if holding[i] < limit]
        whole, left = sum([weights[i] for i in movable]), spare
        for i in movable:
            extra = min(limit - holding[i], max(1, left * weights[i] // whole), spare)
            holding[i] = holding[i] + extra
            spare = spare - extra
    return np.array([limit] + holding)


def ragged(own_key, amount, total, limit, lean):
    if amount == 2:
        one = jax.random.randint(own_key, (), max(1, total - limit), min(limit, total - 1) + 1)
        return jnp.stack([one, total - one])
    tallies = jnp.asarray(split_up(amount, total, limit, lean), jnp.int32)
    couples = (amount - 1) // 2
    donor, taker = tallies[1:1 + 2 * couples:2], tallies[2:2 + 2 * couples:2]
    margin = jnp.minimum(donor - 1, limit - taker)
    passed = jax.random.randint(jax.random.fold_in(own_key, 1), (couples,), 0, 1 << 20) % (margin + 1)
    tallies = tallies.at[1:1 + 2 * couples:2].set(donor - passed).at[2:2 + 2 * couples:2].set(taker + passed)
    return tallies[jax.random.permutation(jax.random.fold_in(own_key, 2), amount)]


def normal_values(stream_key, dims, width, bound, cuts=(), kind=jnp.bfloat16):
    gain = block_scale(stream_key, dims, cuts, -0.22, 0.18) if cuts else 1.0
    values = jax.random.normal(stream_key, dims, jnp.float32) * width * gain
    return jnp.minimum(jnp.maximum(values, -bound), bound).astype(kind)


def setup_inputs(seed: int = 0) -> dict:
    streams_of = jax.random.split(jax.random.key(seed), 10)
    return {
        "c_old": normal_values(streams_of[0], (GX, GY, CZ), 1.0, 6.0, ((0, 8), (1, 16)), jnp.float32),
        "s_old": normal_values(streams_of[1], (RATES, GX, GY, CZ), 1.0, 6.0, ((1, 8), (2, 16)), jnp.float32),
        "rate_time": jnp.clip(jnp.exp(math.log(100.0) - 9.2103404 * jax.random.uniform(streams_of[2], (RATES, GX, GY, CZ), jnp.float32) ** block_scale(streams_of[2], (RATES, GX, GY, CZ), ((1, 8), (2, 16)), -0.2, 0.2)), 0.01, 100.0),
        "capacity": jnp.clip(jnp.exp(jax.random.uniform(streams_of[3], (RATES,), jnp.float32, math.log(0.05), math.log(0.5))), 0.05, 0.5),
        "agg_count": ragged(streams_of[4], DEVICES, NC, AGG_CAP, 1).astype(jnp.int32),
        "coarse_order": draw_coarse_order(jax.random.fold_in(streams_of[9], 71), 0),
        "coarse_cols": plant(jax.random.randint(streams_of[6], (KC, NC), 0, NC), jax.random.fold_in(streams_of[6], 1), 0, NC - 1).astype(jnp.int32),
        "coarse_off": jnp.clip(jax.random.uniform(streams_of[7], (KC, NC), jnp.float32, -16.0, 16.0) * block_scale(streams_of[7], (KC, NC), ((1, 8),), -0.4, 0.0), -16.0, 16.0),
        "coarse_diag": jnp.clip(160.0 + 96.0 * jax.random.uniform(streams_of[8], (NC,), jnp.float32) ** block_scale(streams_of[8], (NC,), ((0, 8),), -0.2, 0.2), 160.0, 256.0),
    }


diffusion_number = 8.0
upwind_number = 2.0
smooth_weight = 0.8
coarse_weight = 0.8

def apply_fine(field, mass):
    padded = jnp.pad(field, 1)
    beside_all = padded[2:, 1:-1, 1:-1] + padded[:-2, 1:-1, 1:-1]
    beside_all = beside_all + padded[1:-1, 2:, 1:-1] + padded[1:-1, :-2, 1:-1]
    behind = padded[1:-1, 1:-1, :-2]
    ahead = padded[1:-1, 1:-1, 2:]
    centre = mass + 6.0 * diffusion_number + upwind_number
    return centre * field - diffusion_number * (beside_all + behind + ahead) - upwind_number * behind

def solve_small(gram, right):
    count = right.shape[0]
    matrix = [[gram[row, column] for column in range(count)] for row in range(count)]
    vector = [right[row] for row in range(count)]
    for pivot in range(count):
        for row in range(pivot + 1, count):
            factor = matrix[row][pivot] / matrix[pivot][pivot]
            for column in range(pivot, count):
                matrix[row][column] = matrix[row][column] - factor * matrix[pivot][column]
            vector[row] = vector[row] - factor * vector[pivot]
    result = [None] * count
    for row in reversed(range(count)):
        partial_sum = vector[row]
        for column in range(row + 1, count):
            partial_sum = partial_sum - matrix[row][column] * result[column]
        result[row] = partial_sum / matrix[row][row]
    return result

def least_squares(columns, beta):
    hessen = jnp.stack(columns, axis=1)
    gram = jnp.dot(hessen.T, hessen, precision=lax.Precision.HIGHEST)
    return solve_small(gram, beta * hessen[0])

def reference(c_old, s_old, rate_time, capacity, agg_count, coarse_order, coarse_cols, coarse_off, coarse_diag):
    share = rate_time / (1.0 + rate_time)
    weighted = capacity[:, None, None, None] * share
    mass = 1.0 + lax.optimization_barrier(jnp.sum(weighted, 0))
    source = c_old + lax.optimization_barrier(jnp.sum(weighted * s_old, 0))
    cells = CX * CY * CZ
    offsets = jnp.cumsum(agg_count) - agg_count
    local_ids = jnp.arange(cells, dtype=jnp.int32)
    slots = local_ids[None, :] * agg_count[:, None] // cells
    row_ids = coarse_order[(offsets[:, None] + slots).astype(jnp.int32)]

    def to_blocks(field):
        return field.reshape(N_COARSE, CX, N_FINE, CY, CZ).transpose(0, 2, 1, 3, 4).reshape(N_COARSE * N_FINE, cells)

    def from_blocks(blocks):
        return blocks.reshape(N_COARSE, N_FINE, CX, CY, CZ).transpose(0, 2, 1, 3, 4).reshape(GX, GY, CZ)

    def coarse_apply(values):
        return coarse_diag * values + lax.optimization_barrier(jnp.sum(coarse_off * values[coarse_cols], 0))
    centre = mass + 6.0 * diffusion_number + upwind_number

    def precondition(vector):
        smooth = smooth_weight * vector / centre
        smooth = smooth + smooth_weight * (vector - apply_fine(smooth, mass)) / centre
        coarse_rhs = jax.ops.segment_sum(to_blocks(vector).reshape(-1), row_ids.reshape(-1), num_segments=NC)
        correction = coarse_weight * coarse_rhs / coarse_diag
        for sweep in range(KJ - 1):
            correction = correction + coarse_weight * (coarse_rhs - coarse_apply(correction)) / coarse_diag
        return smooth + from_blocks(correction[row_ids])
    beta = jnp.sqrt(jnp.sum(source * source))
    basis = [source / beta]
    directions = []
    columns = []
    for step in range(ITERS):
        direction = precondition(basis[step])
        directions.append(direction)
        image = apply_fine(direction, mass)
        products = jnp.stack([jnp.sum(earlier * image) for earlier in basis])
        for index in range(len(basis)):
            image = image - products[index] * basis[index]
        leftover = jnp.sqrt(jnp.sum(image * image))
        columns.append(jnp.concatenate([products, leftover[None], jnp.zeros((ITERS - step - 1,), jnp.float32)]))
        if step + 1 < ITERS:
            basis.append(image / leftover)
    weights = least_squares(columns, beta)
    mobile = weights[0] * directions[0]
    for index in range(1, ITERS):
        mobile = mobile + weights[index] * directions[index]
    immobile = (s_old + rate_time * mobile[None]) / (1.0 + rate_time)
    return (mobile, immobile)
```

```python
import jax
import jax.numpy as jnp
from jax import lax
from jax.experimental import pallas as pl
from jax.experimental.pallas import tpu as pltpu
from jax.sharding import PartitionSpec as P

BOTH = ("coarse", "fine")
CX, CY, CZ = 4, 8, 256
RATES = 16
KC = 8
DEVICES = 128
LANES = 128
SLOTS = 256
SHARDS = 8
SHARD_ROWS = 2048
FLOW = 50.0
F32, BF16, I32 = jnp.float32, jnp.bfloat16, jnp.int32
VM = pl.BlockSpec(memory_space=pltpu.VMEM)
SM = pl.BlockSpec(memory_space=pltpu.SMEM)


def iota(shape, dim):
    return lax.broadcasted_iota(I32, shape, dim)


def lane_take(table, index):
    return jnp.take_along_axis(table, index, axis=1, mode="promise_in_bounds")


def nt(left, right):
    return lax.dot_general(left, right, (((1,), (1,)), ((), ())), preferred_element_type=F32)


def nn(left, right):
    return jnp.dot(left, right, preferred_element_type=F32)


def split2(values):
    high = values.astype(BF16)
    return high, (values - high.astype(F32)).astype(BF16)


def split3(values):
    high = values.astype(BF16)
    rest = values - high.astype(F32)
    mid = rest.astype(BF16)
    return high, mid, (rest - mid.astype(F32)).astype(BF16)


def slots_of(plane, half, count):
    row = (plane * CY + iota((CY, LANES), 0)) * 2 + half
    return ((row * LANES + iota((CY, LANES), 1)) * count) >> 13


def restrict(cells, count):
    slot = iota((CY, SLOTS), 1)
    total = jnp.zeros((CY, SLOTS), F32)
    for plane in range(CX):
        for half in range(2):
            values = cells[plane][:, half * LANES : (half + 1) * LANES]
            row = (plane * CY + iota((CY, 1), 0)) * 2 + half
            first = (row * count) >> 6
            member = slots_of(plane, half, count) - first
            relative = slot - first
            for k in range(5):
                part = jnp.sum(jnp.where(member == k, values, 0.0), axis=1, keepdims=True)
                total = total + jnp.where(relative == k, part, 0.0)
    return jnp.sum(total, axis=0, keepdims=True)


def prolong(entries, count):
    low = jnp.broadcast_to(entries[:, :LANES], (CY, LANES))
    high = jnp.broadcast_to(entries[:, LANES:], (CY, LANES))
    planes = []
    for plane in range(CX):
        halves = []
        for half in range(2):
            slot = slots_of(plane, half, count)
            place = slot & 127
            halves.append(jnp.where(slot < LANES, lane_take(low, place), lane_take(high, place)))
        planes.append(jnp.concatenate(halves, axis=1))
    return planes


def couple(left, mid, right, up, down):
    length = mid.shape[1]
    lane = iota(mid.shape, 1)
    behind = jnp.where(lane == 0, 0.0, pltpu.roll(mid, 1, 1))
    ahead = jnp.where(lane == length - 1, 0.0, pltpu.roll(mid, length - 1, 1))
    return 8.0 * (left + right + up + down + ahead) + 10.0 * behind


def source_kernel(cap, count, place, c_old, s_old, rate, diag, c_out, ic_out, s_out, zs_out, pay):
    n = count[0]
    planes = []
    for x in range(CX):
        mass = jnp.zeros((CY, CZ), F32)
        extra = jnp.zeros((CY, CZ), F32)
        for k in range(RATES):
            r = rate[k, x]
            weighted = cap[k] * (r / (1.0 + r))
            mass = mass + weighted
            extra = extra + weighted * s_old[k, x]
        centre = (1.0 + mass) + FLOW
        source = c_old[x] + extra
        inverse = 1.0 / centre
        c_out[x] = centre
        ic_out[x] = inverse
        s_out[x] = source
        zs_out[x] = 0.8 * source * inverse
        planes.append(source)
    sums = restrict(planes, n)
    kind = iota((8, LANES), 0) & 3
    rows = [
        sums[:, :LANES],
        sums[:, LANES:],
        diag[pl.ds(place[1], 1), :],
        jnp.full((1, LANES), n, I32).astype(F32),
    ]
    tile = jnp.broadcast_to(rows[3], (8, LANES))
    for k in range(3):
        tile = jnp.where(kind == k, rows[k], tile)
    for i in range(DEVICES // 2):
        pay[pl.ds(8 * i, 8), :] = tile


def order_kernel(order, inverse_out, blocks_out):
    numbers = order[...]
    blocks = (iota((LANES, LANES), 0) == (numbers[0:1, :] >> 7)).astype(F32).astype(BF16)
    blocks_out[...] = blocks
    lows = nt(blocks, (numbers & 127).astype(F32).astype(BF16)).astype(I32)
    lane = iota((LANES, LANES), 1)
    found = jnp.zeros((LANES, LANES), I32)
    for q in range(LANES):
        found = jnp.where(lows[:, q : q + 1] == lane, q, found)
    inverse_out[...] = found


def offsets_of(counts):
    strict = (iota((LANES, LANES), 1) < iota((LANES, LANES), 0)).astype(F32).astype(BF16)
    by_row = nn(strict, counts.astype(BF16)).astype(I32)
    later = iota((LANES, LANES), 0) < iota((LANES, LANES), 1)
    by_lane = jnp.sum(jnp.where(later, counts, 0.0), axis=0, keepdims=True).astype(I32)
    return by_row, by_lane


def assemble(low, high, offsets, inverse, blocks):
    by_row, by_lane = offsets
    lane = iota((LANES, LANES), 1)
    shift = by_row & 127
    place = (lane - shift) & 127
    low = lane_take(low, place)
    high = lane_take(high, place)
    kept = lane >= shift
    rows = (jnp.where(kept, low, 0.0), jnp.where(kept, high, low), jnp.where(kept, 0.0, high))
    start = by_lane >> 7
    table = jnp.zeros((LANES, LANES), F32)
    for j in range(3):
        spot = (iota((LANES, LANES), 0) == start + j).astype(F32).astype(BF16)
        for part in split3(rows[j]):
            table = table + nn(spot, part)
    by_block = jnp.zeros((LANES, LANES), F32)
    for part in split3(table):
        by_block = by_block + nt(blocks, part)
    return lane_take(by_block, inverse)


def fetch(table, unknown):
    inner = unknown & (SHARD_ROWS - 1)
    shard = unknown >> 11
    found = jnp.zeros((SHARDS * 32, SLOTS), F32)
    for chunk in range(SHARD_ROWS // 256):
        spot = (iota((256, SLOTS), 0) + chunk * 256 == inner).astype(F32).astype(BF16)
        found = found + nn(table[:, chunk * 256 : (chunk + 1) * 256], spot)
    found = found.reshape(SHARDS, 32, SLOTS)
    picked = jnp.zeros((32, SLOTS), F32)
    for g in range(SHARDS):
        picked = picked + jnp.where(shard == g, found[g], 0.0)
    return picked[0:8], picked[8:16], picked[16:24] + picked[24:32]


def coarse_solve(values, plan, own):
    high, low = split2(values.T)
    table = jnp.concatenate([high, low], axis=1)
    row = iota((LANES, SLOTS), 0).astype(F32)

    def gather(block, inner):
        spot = (row == block).astype(F32).astype(BF16)
        found = nn(table, jnp.concatenate([spot, spot], axis=0))
        return jnp.sum(jnp.where(row == inner, found, 0.0).reshape(16, 8, SLOTS), axis=0)

    def entry(k, total):
        part = -1.4 * gather(plan[KC, pl.ds(k, 1), :], plan[KC, pl.ds(8 + k, 1), :])
        for j in range(KC):
            weight = plan[k, 16 + j : 17 + j, :]
            part = part + weight * gather(plan[k, j : j + 1, :], plan[k, 8 + j : 9 + j, :])
        return total + plan[KC, pl.ds(16 + k, 1), :] * part

    total = 1.24 * gather(own[0:1, :], own[1:2, :])
    total = lax.fori_loop(0, KC, entry, total)
    return jnp.sum(total, axis=0, keepdims=True)


def plan_rows(ref, k, parts):
    ref[k, 0:8, :] = parts[0]
    ref[k, 8:16, :] = parts[1]
    ref[k, 16:24, :] = parts[2]


def first_kernel(
    count, place, gathered, order, inverse, blocks, tabs, zs, ic,
    pe_out, plan, own, xa, xb, table,
):
    n = count[0]
    me = place[0] * 16 + place[1]
    counts = gathered[pl.ds(3, DEVICES, stride=4), :]
    offsets = offsets_of(counts)
    sums = assemble(
        gathered[pl.ds(0, DEVICES, stride=4), :],
        gathered[pl.ds(1, DEVICES, stride=4), :],
        offsets, inverse[...], blocks[...],
    )
    values = 0.8 * sums / gathered[pl.ds(2, DEVICES, stride=4), :]

    for g in range(SHARDS):
        cols = tabs[16 * g : 16 * g + 8, :]
        high = jnp.floor(cols * (1.0 / 128.0))
        pair = jnp.concatenate([high, cols - 128.0 * high], axis=0)
        table[32 * g : 32 * g + 16, :] = pair.astype(BF16)
        off = tabs[16 * g + 8 : 16 * g + 16, :]
        big = off.astype(BF16).astype(F32)
        table[32 * g + 16 : 32 * g + 32, :] = jnp.concatenate([big, off - big], axis=0).astype(BF16)

    row = iota((LANES, LANES), 0)
    mine = jnp.sum(jnp.where(row == me, offsets[0].astype(F32), 0.0), axis=0, keepdims=True).astype(I32)
    numbers = order[...].astype(F32)
    start = mine >> 7
    lines = []
    spread = (iota((8, LANES), 1) + mine) & 127
    for j in range(3):
        line = jnp.sum(jnp.where(row == start + j, numbers, 0.0), axis=0, keepdims=True)
        lines.append(lane_take(jnp.broadcast_to(line, (8, LANES)), spread))
    inside = iota((8, LANES), 1) + (mine & 127) < LANES
    unknown = jnp.concatenate(
        [jnp.where(inside, lines[0], lines[1]), jnp.where(inside, lines[1], lines[2])], axis=1
    )[0:1].astype(I32)
    own[0:1, :] = (unknown >> 7).astype(F32)
    own[1:2, :] = (unknown & 127).astype(F32)

    plan_rows(plan, KC, fetch(table, unknown))

    def level(k, carry):
        col = 128.0 * plan[KC, pl.ds(k, 1), :] + plan[KC, pl.ds(8 + k, 1), :]
        plan_rows(plan, k, fetch(table, col.astype(I32)))
        return carry

    lax.fori_loop(0, KC, level, 0)

    pe = prolong(coarse_solve(values, plan, own), n)
    for x in range(CX):
        pe_out[x] = pe[x]

    def message(out, upper):
        for k in range(3):
            out[k] = zs[CX - 3 + k] if upper else zs[k]
        for k in range(2):
            out[3 + k] = ic[CX - 2 + k] if upper else ic[k]
            out[5 + k] = pe[CX - 2 + k] if upper else pe[k]

    even = (place[0] & 1) == 0

    @pl.when(even)
    def _():
        message(xa, True)
        message(xb, False)

    @pl.when(jnp.logical_not(even))
    def _():
        message(xa, False)
        message(xb, True)


def below_above(parity, a, b):
    even = parity == 0
    return (lambda *i: jnp.where(even, b[i], a[i])), (lambda *i: jnp.where(even, a[i], b[i]))


def widen_kernel(place, zs, ic, pe, xa, xb, ya, yb):
    below, above = below_above(place[0] & 1, xa, xb)
    own = (zs, ic, pe)
    depth = (3, 2, 2)
    base = (0, 3, 5)

    def plane(field, x):
        if x < 0:
            return below(base[field] + depth[field] + x)
        if x >= CX:
            return above(base[field] + x - CX)
        return own[field][x]

    even = (place[1] & 1) == 0
    for x in range(-2, CX + 2):
        fields = [plane(f, x) for f in range(3)]
        upper = jnp.concatenate([fields[f][CY - depth[f] :] for f in range(3)] + [fields[0][0:1]], axis=0)
        lower = jnp.concatenate([fields[f][: depth[f]] for f in range(3)] + [fields[0][0:1]], axis=0)
        ya[x + 2] = jnp.where(even, upper, lower)
        yb[x + 2] = jnp.where(even, lower, upper)


def second_kernel(count, place, zs, ic, pe, c, xa, xb, ya, yb, z1_out, w1_out, sw_out, pay):
    below, above = below_above(place[0] & 1, xa, xb)
    near, far = below_above(place[1] & 1, ya, yb)
    own = (zs, ic, pe)
    depth = (3, 2, 2)
    base = (0, 3, 5)

    def plane(field, x):
        if x < 0:
            middle = below(base[field] + depth[field] + x)
        elif x >= CX:
            middle = above(base[field] + x - CX)
        else:
            middle = own[field][x]
        d = depth[field]
        if -2 <= x < CX + 2:
            low = near(x + 2)[base[field] : base[field] + d]
            high = far(x + 2)[base[field] : base[field] + d]
        else:
            low = jnp.zeros((d, CZ), F32)
            high = low
        blank = jnp.zeros((8 - d, CZ), F32)
        return jnp.concatenate([blank, low, middle, high, blank], axis=0)

    def neighbours(get, x):
        mid = get(x)
        rows = mid.shape[0]
        return couple(get(x - 1), mid, get(x + 1), pltpu.roll(mid, 1, 0), pltpu.roll(mid, rows - 1, 0))

    z = {x: plane(0, x) for x in range(-3, CX + 3)}
    inv = {x: plane(1, x) for x in range(-2, CX + 2)}
    first = {}
    for x in range(-2, CX + 2):
        first[x] = 1.2 * z[x] + 0.8 * inv[x] * neighbours(z.get, x) + plane(2, x)
    zw = {}
    image = []
    for x in range(-1, CX + 1):
        beside = neighbours(first.get, x)
        zw[x] = 0.8 * (first[x] - inv[x] * beside)
        if 0 <= x < CX:
            here = c[x] * first[x][8:16] - beside[8:16]
            image.append(here)
            z1_out[x] = first[x][8:16]
            w1_out[x] = here
    for x in range(CX):
        smooth = 1.2 * zw[x] + 0.8 * inv[x] * neighbours(zw.get, x)
        sw_out[x] = smooth[8:16]
    sums = restrict(image, count[0])
    kind = iota((8, LANES), 0) & 1
    tile = jnp.where(kind == 0, sums[:, :LANES], sums[:, LANES:])
    for i in range(DEVICES // 4):
        pay[pl.ds(8 * i, 8), :] = tile


def third_kernel(
    count, place, sums, gathered, inverse, blocks, plan, own, sw,
    p_out, xa, xb, ya, yb,
):
    offsets = offsets_of(gathered[pl.ds(3, DEVICES, stride=4), :])
    values = assemble(
        sums[pl.ds(0, DEVICES, stride=2), :],
        sums[pl.ds(1, DEVICES, stride=2), :],
        offsets, inverse[...], blocks[...],
    )
    values = 0.8 * values / gathered[pl.ds(2, DEVICES, stride=4), :]
    pe = prolong(coarse_solve(values, plan, own), count[0])
    p = [sw[x] + pe[x] for x in range(CX)]
    for x in range(CX):
        p_out[x] = p[x]
    even = (place[0] & 1) == 0
    xa[...] = jnp.where(even, p[CX - 1], p[0])
    xb[...] = jnp.where(even, p[0], p[CX - 1])
    even = (place[1] & 1) == 0
    upper = jnp.concatenate([p[x][CY - 1 : CY] for x in range(CX)] * 2, axis=0)
    lower = jnp.concatenate([p[x][0:1] for x in range(CX)] * 2, axis=0)
    ya[...] = jnp.where(even, upper, lower)
    yb[...] = jnp.where(even, lower, upper)


def products_kernel(place, s, w1, p, c, xa, xb, ya, yb, pay):
    even = (place[0] & 1) == 0
    below, above = jnp.where(even, xb[...], xa[...]), jnp.where(even, xa[...], xb[...])
    even = (place[1] & 1) == 0
    near, far = jnp.where(even, yb[...], ya[...]), jnp.where(even, ya[...], yb[...])
    sums = [jnp.zeros((CY, CZ), F32) for _ in range(6)]
    row = iota((CY, CZ), 0)
    for x in range(CX):
        mid = p[x]
        left = p[x - 1] if x else below
        right = p[x + 1] if x + 1 < CX else above
        up = jnp.where(row == 0, near[x : x + 1], pltpu.roll(mid, 1, 0))
        down = jnp.where(row == CY - 1, far[x : x + 1], pltpu.roll(mid, CY - 1, 0))
        q = c[x] * mid - couple(left, mid, right, up, down)
        a, b = s[x], w1[x]
        for k, term in enumerate((a * a, a * b, a * q, b * b, b * q, q * q)):
            sums[k] = sums[k] + term
    lane = iota((8, LANES), 1)
    tile = jnp.zeros((8, LANES), F32)
    for k in range(6):
        tile = tile + jnp.where(lane == k, jnp.sum(sums[k], keepdims=True), 0.0)
    for i in range(DEVICES // 8):
        pay[pl.ds(8 * i, 8), :] = tile


def update_kernel(parts, z1, p, s_old, rate, mobile, immobile):
    total = jnp.sum(parts[...], axis=0, keepdims=True)
    ss, sw, sq, ww, wq, qq = [total[:, k : k + 1] for k in range(6)]
    factor = wq / ww
    y2 = (sq - factor * sw) / (qq - factor * wq)
    y1 = (sw - wq * y2) / ww
    for x in range(CX):
        new = y1 * z1[x] + y2 * p[x]
        mobile[x] = new
        for k in range(RATES):
            r = rate[k, x]
            immobile[k, x] = (s_old[k, x] + r * new) / (1.0 + r)


def call(kernel, ins, outs, scratch=(), flops=10_000, vmem=48 << 20):
    shapes = [jax.ShapeDtypeStruct(shape, dtype) for shape, dtype in outs]
    return pl.pallas_call(
        kernel,
        out_shape=shapes,
        in_specs=ins,
        out_specs=[VM] * len(shapes),
        scratch_shapes=list(scratch),
        cost_estimate=pl.CostEstimate(flops=flops, bytes_accessed=100_000, transcendentals=0),
        compiler_params=pltpu.CompilerParams(vmem_limit_bytes=vmem),
    )


FIELD = ((CX, CY, CZ), F32)


def swaps(count):
    first = [(i, i ^ 1) for i in range(count)]
    second = [(i, ((i - 1) ^ 1) + 1) for i in range(1, count - 1)]
    return first, second


def trade(a, b, axis):
    first, second = swaps(lax.axis_size(axis))
    return lax.ppermute(a, axis, first), lax.ppermute(b, axis, second)


def everyone(pay, rows):
    moved = lax.all_to_all(pay.reshape(DEVICES, rows, LANES), BOTH, 0, 0)
    return moved.reshape(DEVICES * rows, LANES)


def local(
    c_old, s_old, rate_time, capacity, agg_count, coarse_order, coarse_cols, coarse_off, coarse_diag
):
    place = jnp.stack([lax.axis_index("coarse"), lax.axis_index("fine")]).astype(I32)
    scaled = 0.8 * coarse_off / coarse_diag[None, :]
    tab = jnp.concatenate([coarse_cols.astype(F32), scaled], axis=0)
    tabs = lax.all_gather(tab, "coarse", axis=0, tiled=True)
    order = coarse_order.reshape(LANES, LANES)

    c, ic, s, zs, pay = call(
        source_kernel, [SM, SM, SM, VM, VM, VM, VM],
        [FIELD, FIELD, FIELD, FIELD, ((4 * DEVICES, LANES), F32)],
    )(capacity, agg_count, place, c_old, s_old, rate_time, coarse_diag.reshape(16, LANES))
    gathered = everyone(pay, 4)
    inverse, blocks = call(
        order_kernel, [VM], [((LANES, LANES), I32), ((LANES, LANES), BF16)], flops=10_000_000
    )(order)

    pe, plan, own, xa, xb = call(
        first_kernel, [SM, SM] + [VM] * 7,
        [FIELD, ((KC + 1, 24, SLOTS), F32), ((8, SLOTS), F32), ((7, CY, CZ), F32), ((7, CY, CZ), F32)],
        scratch=[pltpu.VMEM((SHARDS * 32, SHARD_ROWS), BF16)],
    )(agg_count, place, gathered, order, inverse, blocks, tabs, zs, ic)
    xa, xb = trade(xa, xb, "coarse")
    ya, yb = call(
        widen_kernel, [SM] + [VM] * 5, [((CX + 4, CY, CZ), F32)] * 2
    )(place, zs, ic, pe, xa, xb)
    ya, yb = trade(ya, yb, "fine")
    z1, w1, sw, pay = call(
        second_kernel, [SM, SM] + [VM] * 8, [FIELD, FIELD, FIELD, ((2 * DEVICES, LANES), F32)]
    )(agg_count, place, zs, ic, pe, c, xa, xb, ya, yb)
    sums = everyone(pay, 2)

    p, xa, xb, ya, yb = call(
        third_kernel, [SM, SM] + [VM] * 7, [FIELD] + [((CY, CZ), F32)] * 4
    )(agg_count, place, sums, gathered, inverse, blocks, plan, own, sw)
    xa, xb = trade(xa, xb, "coarse")
    ya, yb = trade(ya, yb, "fine")
    (pay,) = call(
        products_kernel, [SM] + [VM] * 8, [((DEVICES, LANES), F32)]
    )(place, s, w1, p, c, xa, xb, ya, yb)
    parts = everyone(pay, 1)
    mobile, immobile = call(
        update_kernel, [VM] * 5, [FIELD, ((RATES, CX, CY, CZ), F32)]
    )(parts, z1, p, s_old, rate_time)
    return mobile, immobile


def solution(mesh):
    return jax.shard_map(
        local,
        mesh=mesh,
        in_specs=(
            P("coarse", "fine", None),
            P(None, "coarse", "fine", None),
            P(None, "coarse", "fine", None),
            P(),
            P(("coarse", "fine")),
            P(),
            P(None, "coarse"),
            P(None, "coarse"),
            P("coarse"),
        ),
        out_specs=(P("coarse", "fine", None), P(None, "coarse", "fine", None)),
        check_vma=False,
    )
```

```python
import jax
import jax.numpy as jnp
from jax import lax
from jax.experimental import pallas as pl
from jax.experimental.pallas import tpu as pltpu
from jax.sharding import PartitionSpec as P

BOTH = ("coarse", "fine")
CX, CY, CZ = 4, 8, 256
RATES = 16
KC = 8
DEVICES = 128
LANES = 128
SLOTS = 256
SHARDS = 8
SHARD_ROWS = 2048
FLOW = 50.0
F32, BF16, I32 = jnp.float32, jnp.bfloat16, jnp.int32
VM = pl.BlockSpec(memory_space=pltpu.VMEM)
SM = pl.BlockSpec(memory_space=pltpu.SMEM)
HB = pl.BlockSpec(memory_space=pltpu.HBM)


def places():
    return lax.axis_index("coarse").astype(I32), lax.axis_index("fine").astype(I32)


def iota(shape, dim):
    return lax.broadcasted_iota(I32, shape, dim)


def lane_take(table, index):
    return jnp.take_along_axis(table, index, axis=1, mode="promise_in_bounds")


def nt(left, right):
    return lax.dot_general(left, right, (((1,), (1,)), ((), ())), preferred_element_type=F32)


def nn(left, right):
    return jnp.dot(left, right, preferred_element_type=F32)


def split2(values):
    high = values.astype(BF16)
    return high, (values - high.astype(F32)).astype(BF16)


def split3(values):
    high = values.astype(BF16)
    rest = values - high.astype(F32)
    mid = rest.astype(BF16)
    return high, mid, (rest - mid.astype(F32)).astype(BF16)


def slots_of(plane, half, count):
    row = (plane * CY + iota((CY, LANES), 0)) * 2 + half
    return ((row * LANES + iota((CY, LANES), 1)) * count) >> 13


def restrict(cells, count):
    slot = iota((CY, SLOTS), 1)
    total = jnp.zeros((CY, SLOTS), F32)
    for plane in range(CX):
        for half in range(2):
            values = cells[plane][:, half * LANES : (half + 1) * LANES]
            row = (plane * CY + iota((CY, 1), 0)) * 2 + half
            first = (row * count) >> 6
            member = slots_of(plane, half, count) - first
            relative = slot - first
            for k in range(5):
                part = jnp.sum(jnp.where(member == k, values, 0.0), axis=1, keepdims=True)
                total = total + jnp.where(relative == k, part, 0.0)
    return jnp.sum(total, axis=0, keepdims=True)


def prolong(entries, count):
    low = jnp.broadcast_to(entries[:, :LANES], (CY, LANES))
    high = jnp.broadcast_to(entries[:, LANES:], (CY, LANES))
    planes = []
    for plane in range(CX):
        halves = []
        for half in range(2):
            slot = slots_of(plane, half, count)
            place = slot & 127
            halves.append(jnp.where(slot < LANES, lane_take(low, place), lane_take(high, place)))
        planes.append(jnp.concatenate(halves, axis=1))
    return planes


def couple(left, mid, right, up, down):
    length = mid.shape[1]
    lane = iota(mid.shape, 1)
    behind = jnp.where(lane == 0, 0.0, pltpu.roll(mid, 1, 1))
    ahead = jnp.where(lane == length - 1, 0.0, pltpu.roll(mid, length - 1, 1))
    return 8.0 * (left + right + up + down + ahead) + 10.0 * behind


def table_kernel(cols, off, diag, after, out):
    out[0:8, :] = cols[...].astype(F32)
    out[8:16, :] = off[...] * (0.8 / diag[...])


def source_kernel(
    cap, count, c_old, s_old_hbm, rate_hbm, diag, c_out, ic_out, s_out, zs_out, pay, s_old, rate, sems
):
    place = places()
    n = count[0]
    copies = []
    for x in range(CX):
        pair = (
            pltpu.make_async_copy(rate_hbm.at[:, x], rate.at[:, x], sems.at[0, x]),
            pltpu.make_async_copy(s_old_hbm.at[:, x], s_old.at[:, x], sems.at[1, x]),
        )
        for copy in pair:
            copy.start()
        copies.append(pair)
    planes = []
    for x in range(CX):
        for copy in copies[x]:
            copy.wait()
        mass = jnp.zeros((CY, CZ), F32)
        extra = jnp.zeros((CY, CZ), F32)
        for k in range(RATES):
            r = rate[k, x]
            weighted = cap[k] * (r / (1.0 + r))
            mass = mass + weighted
            extra = extra + weighted * s_old[k, x]
        centre = (1.0 + mass) + FLOW
        source = c_old[x] + extra
        inverse = 1.0 / centre
        c_out[x] = centre
        ic_out[x] = inverse
        s_out[x] = source
        zs_out[x] = 0.8 * source * inverse
        planes.append(source)
    sums = restrict(planes, n)
    kind = iota((8, LANES), 0) & 3
    rows = [
        sums[:, :LANES],
        sums[:, LANES:],
        diag[pl.ds(place[1], 1), :],
        jnp.full((1, LANES), n, I32).astype(F32),
    ]
    tile = jnp.broadcast_to(rows[3], (8, LANES))
    for k in range(3):
        tile = jnp.where(kind == k, rows[k], tile)
    for i in range(DEVICES // 2):
        pay[pl.ds(8 * i, 8), :] = tile


def order_kernel(order, after, inverse_out, blocks_out):
    numbers = order[...]
    blocks = (iota((LANES, LANES), 0) == (numbers[0:1, :] >> 7)).astype(F32).astype(BF16)
    blocks_out[...] = blocks
    lows = nt(blocks, (numbers & 127).astype(F32).astype(BF16)).astype(I32)
    lane = iota((LANES, LANES), 1)
    found = jnp.zeros((LANES, LANES), I32)
    for q in range(LANES):
        found = jnp.where(lows[:, q : q + 1] == lane, q, found)
    inverse_out[...] = found


def offsets_of(counts):
    strict = (iota((LANES, LANES), 1) < iota((LANES, LANES), 0)).astype(F32).astype(BF16)
    by_row = nn(strict, counts.astype(BF16)).astype(I32)
    later = iota((LANES, LANES), 0) < iota((LANES, LANES), 1)
    by_lane = jnp.sum(jnp.where(later, counts, 0.0), axis=0, keepdims=True).astype(I32)
    return by_row, by_lane


def assemble(low, high, offsets, inverse, blocks):
    by_row, by_lane = offsets
    lane = iota((LANES, LANES), 1)
    shift = by_row & 127
    place = (lane - shift) & 127
    low = lane_take(low, place)
    high = lane_take(high, place)
    kept = lane >= shift
    rows = (jnp.where(kept, low, 0.0), jnp.where(kept, high, low), jnp.where(kept, 0.0, high))
    start = by_lane >> 7
    table = jnp.zeros((LANES, LANES), F32)
    for j in range(3):
        spot = (iota((LANES, LANES), 0) == start + j).astype(F32).astype(BF16)
        for part in split3(rows[j]):
            table = table + nn(spot, part)
    by_block = jnp.zeros((LANES, LANES), F32)
    for part in split3(table):
        by_block = by_block + nt(blocks, part)
    return lane_take(by_block, inverse)


def fetch(table, unknown, coarse):
    inner = unknown & (SHARD_ROWS - 1)
    shard = unknown >> 11
    shard = ((((coarse >> 1) - (shard >> 1)) & 3) << 1) | ((shard ^ coarse) & 1)
    found = jnp.zeros((SHARDS * 32, SLOTS), F32)
    for chunk in range(SHARD_ROWS // 256):
        spot = (iota((256, SLOTS), 0) + chunk * 256 == inner).astype(F32).astype(BF16)
        found = found + nn(table[:, chunk * 256 : (chunk + 1) * 256], spot)
    found = found.reshape(SHARDS, 32, SLOTS)
    picked = jnp.zeros((32, SLOTS), F32)
    for g in range(SHARDS):
        picked = picked + jnp.where(shard == g, found[g], 0.0)
    return picked[0:8], picked[8:16], picked[16:24] + picked[24:32]


def coarse_solve(values, plan, own):
    high, low = split2(values.T)
    table = jnp.concatenate([high, low], axis=1)
    row = iota((LANES, SLOTS), 0).astype(F32)

    def gather(block, inner):
        spot = (row == block).astype(F32).astype(BF16)
        found = nn(table, jnp.concatenate([spot, spot], axis=0))
        return jnp.sum(jnp.where(row == inner, found, 0.0).reshape(16, 8, SLOTS), axis=0)

    def entry(k, total):
        part = -1.4 * gather(plan[KC, pl.ds(k, 1), :], plan[KC, pl.ds(8 + k, 1), :])
        for j in range(KC):
            weight = plan[k, 16 + j : 17 + j, :]
            part = part + weight * gather(plan[k, j : j + 1, :], plan[k, 8 + j : 9 + j, :])
        return total + plan[KC, pl.ds(16 + k, 1), :] * part

    total = 1.24 * gather(own[0:1, :], own[1:2, :])
    total = lax.fori_loop(0, KC, entry, total)
    return jnp.sum(total, axis=0, keepdims=True)


def plan_rows(ref, k, parts):
    ref[k, 0:8, :] = parts[0]
    ref[k, 8:16, :] = parts[1]
    ref[k, 16:24, :] = parts[2]


def first_kernel(
    count, gathered, order, inverse, blocks, tab0, tab1, tab2, tab3, tab4, tab5, tab6, tab7, zs, ic,
    pe_out, plan, own, xa, xb, table,
):
    place = places()
    n = count[0]
    me = place[0] * 16 + place[1]
    counts = gathered[pl.ds(3, DEVICES, stride=4), :]
    offsets = offsets_of(counts)
    sums = assemble(
        gathered[pl.ds(0, DEVICES, stride=4), :],
        gathered[pl.ds(1, DEVICES, stride=4), :],
        offsets, inverse[...], blocks[...],
    )
    values = 0.8 * sums / gathered[pl.ds(2, DEVICES, stride=4), :]

    tabs = (tab0, tab1, tab2, tab3, tab4, tab5, tab6, tab7)
    for g in range(SHARDS):
        cols = tabs[g][0:8, :]
        high = jnp.floor(cols * (1.0 / 128.0))
        pair = jnp.concatenate([high, cols - 128.0 * high], axis=0)
        table[32 * g : 32 * g + 16, :] = pair.astype(BF16)
        off = tabs[g][8:16, :]
        big = off.astype(BF16).astype(F32)
        table[32 * g + 16 : 32 * g + 32, :] = jnp.concatenate([big, off - big], axis=0).astype(BF16)

    row = iota((LANES, LANES), 0)
    mine = jnp.sum(jnp.where(row == me, offsets[0].astype(F32), 0.0), axis=0, keepdims=True).astype(I32)
    numbers = order[...].astype(F32)
    start = mine >> 7
    lines = []
    spread = (iota((8, LANES), 1) + mine) & 127
    for j in range(3):
        line = jnp.sum(jnp.where(row == start + j, numbers, 0.0), axis=0, keepdims=True)
        lines.append(lane_take(jnp.broadcast_to(line, (8, LANES)), spread))
    inside = iota((8, LANES), 1) + (mine & 127) < LANES
    unknown = jnp.concatenate(
        [jnp.where(inside, lines[0], lines[1]), jnp.where(inside, lines[1], lines[2])], axis=1
    )[0:1].astype(I32)
    own[0:1, :] = (unknown >> 7).astype(F32)
    own[1:2, :] = (unknown & 127).astype(F32)

    plan_rows(plan, KC, fetch(table, unknown, place[0]))

    def level(k, carry):
        col = 128.0 * plan[KC, pl.ds(k, 1), :] + plan[KC, pl.ds(8 + k, 1), :]
        plan_rows(plan, k, fetch(table, col.astype(I32), place[0]))
        return carry

    lax.fori_loop(0, KC, level, 0)

    pe = prolong(coarse_solve(values, plan, own), n)
    for x in range(CX):
        pe_out[x] = pe[x]

    def message(out, upper):
        for k in range(3):
            out[k] = zs[CX - 3 + k] if upper else zs[k]
        for k in range(2):
            out[3 + k] = ic[CX - 2 + k] if upper else ic[k]
            out[5 + k] = pe[CX - 2 + k] if upper else pe[k]

    even = (place[0] & 1) == 0

    @pl.when(even)
    def _():
        message(xa, True)
        message(xb, False)

    @pl.when(jnp.logical_not(even))
    def _():
        message(xa, False)
        message(xb, True)


def below_above(parity, a, b):
    even = parity == 0
    return (lambda *i: jnp.where(even, b[i], a[i])), (lambda *i: jnp.where(even, a[i], b[i]))


def widen_kernel(zs, ic, pe, xa, xb, ya, yb):
    place = places()
    below, above = below_above(place[0] & 1, xa, xb)
    own = (zs, ic, pe)
    depth = (3, 2, 2)
    base = (0, 3, 5)

    def plane(field, x):
        if x < 0:
            return below(base[field] + depth[field] + x)
        if x >= CX:
            return above(base[field] + x - CX)
        return own[field][x]

    even = (place[1] & 1) == 0
    for x in range(-2, CX + 2):
        fields = [plane(f, x) for f in range(3)]
        upper = jnp.concatenate([fields[f][CY - depth[f] :] for f in range(3)] + [fields[0][0:1]], axis=0)
        lower = jnp.concatenate([fields[f][: depth[f]] for f in range(3)] + [fields[0][0:1]], axis=0)
        ya[x + 2] = jnp.where(even, upper, lower)
        yb[x + 2] = jnp.where(even, lower, upper)


def second_kernel(count, zs, ic, pe, c, xa, xb, ya, yb, z1_out, w1_out, sw_out, pay):
    place = places()
    below, above = below_above(place[0] & 1, xa, xb)
    near, far = below_above(place[1] & 1, ya, yb)
    own = (zs, ic, pe)
    depth = (3, 2, 2)
    base = (0, 3, 5)

    def plane(field, x):
        if x < 0:
            middle = below(base[field] + depth[field] + x)
        elif x >= CX:
            middle = above(base[field] + x - CX)
        else:
            middle = own[field][x]
        d = depth[field]
        if -2 <= x < CX + 2:
            low = near(x + 2)[base[field] : base[field] + d]
            high = far(x + 2)[base[field] : base[field] + d]
        else:
            low = jnp.zeros((d, CZ), F32)
            high = low
        blank = jnp.zeros((8 - d, CZ), F32)
        return jnp.concatenate([blank, low, middle, high, blank], axis=0)

    def neighbours(get, x):
        mid = get(x)
        rows = mid.shape[0]
        return couple(get(x - 1), mid, get(x + 1), pltpu.roll(mid, 1, 0), pltpu.roll(mid, rows - 1, 0))

    z = {x: plane(0, x) for x in range(-3, CX + 3)}
    inv = {x: plane(1, x) for x in range(-2, CX + 2)}
    first = {}
    for x in range(-2, CX + 2):
        first[x] = 1.2 * z[x] + 0.8 * inv[x] * neighbours(z.get, x) + plane(2, x)
    zw = {}
    image = []
    for x in range(-1, CX + 1):
        beside = neighbours(first.get, x)
        zw[x] = 0.8 * (first[x] - inv[x] * beside)
        if 0 <= x < CX:
            here = c[x] * first[x][8:16] - beside[8:16]
            image.append(here)
            z1_out[x] = first[x][8:16]
            w1_out[x] = here
    for x in range(CX):
        smooth = 1.2 * zw[x] + 0.8 * inv[x] * neighbours(zw.get, x)
        sw_out[x] = smooth[8:16]
    sums = restrict(image, count[0])
    kind = iota((8, LANES), 0) & 1
    tile = jnp.where(kind == 0, sums[:, :LANES], sums[:, LANES:])
    for i in range(DEVICES // 4):
        pay[pl.ds(8 * i, 8), :] = tile


def third_kernel(
    count, sums, gathered, inverse, blocks, plan, own, sw,
    p_out, xa, xb, ya, yb,
):
    place = places()
    offsets = offsets_of(gathered[pl.ds(3, DEVICES, stride=4), :])
    values = assemble(
        sums[pl.ds(0, DEVICES, stride=2), :],
        sums[pl.ds(1, DEVICES, stride=2), :],
        offsets, inverse[...], blocks[...],
    )
    values = 0.8 * values / gathered[pl.ds(2, DEVICES, stride=4), :]
    pe = prolong(coarse_solve(values, plan, own), count[0])
    p = [sw[x] + pe[x] for x in range(CX)]
    for x in range(CX):
        p_out[x] = p[x]
    even = (place[0] & 1) == 0
    xa[...] = jnp.where(even, p[CX - 1], p[0])
    xb[...] = jnp.where(even, p[0], p[CX - 1])
    even = (place[1] & 1) == 0
    upper = jnp.concatenate([p[x][CY - 1 : CY] for x in range(CX)] * 2, axis=0)
    lower = jnp.concatenate([p[x][0:1] for x in range(CX)] * 2, axis=0)
    ya[...] = jnp.where(even, upper, lower)
    yb[...] = jnp.where(even, lower, upper)


def products_kernel(s, w1, p, c, xa, xb, ya, yb, pay):
    place = places()
    even = (place[0] & 1) == 0
    below, above = jnp.where(even, xb[...], xa[...]), jnp.where(even, xa[...], xb[...])
    even = (place[1] & 1) == 0
    near, far = jnp.where(even, yb[...], ya[...]), jnp.where(even, ya[...], yb[...])
    sums = [jnp.zeros((CY, CZ), F32) for _ in range(6)]
    row = iota((CY, CZ), 0)
    for x in range(CX):
        mid = p[x]
        left = p[x - 1] if x else below
        right = p[x + 1] if x + 1 < CX else above
        up = jnp.where(row == 0, near[x : x + 1], pltpu.roll(mid, 1, 0))
        down = jnp.where(row == CY - 1, far[x : x + 1], pltpu.roll(mid, CY - 1, 0))
        q = c[x] * mid - couple(left, mid, right, up, down)
        a, b = s[x], w1[x]
        for k, term in enumerate((a * a, a * b, a * q, b * b, b * q, q * q)):
            sums[k] = sums[k] + term
    lane = iota((8, LANES), 1)
    tile = jnp.zeros((8, LANES), F32)
    for k in range(6):
        tile = tile + jnp.where(lane == k, jnp.sum(sums[k], keepdims=True), 0.0)
    for i in range(DEVICES // 8):
        pay[pl.ds(8 * i, 8), :] = tile


def update_kernel(parts, z1, p, s_old, rate, mobile, immobile):
    total = jnp.sum(parts[...], axis=0, keepdims=True)
    ss, sw, sq, ww, wq, qq = [total[:, k : k + 1] for k in range(6)]
    factor = wq / ww
    y2 = (sq - factor * sw) / (qq - factor * wq)
    y1 = (sw - wq * y2) / ww
    for x in range(CX):
        new = y1 * z1[x] + y2 * p[x]
        mobile[x] = new
        for k in range(RATES):
            r = rate[k, x]
            immobile[k, x] = (s_old[k, x] + r * new) / (1.0 + r)


def call(kernel, ins, outs, scratch=(), flops=10_000, vmem=48 << 20):
    shapes = [jax.ShapeDtypeStruct(shape, dtype) for shape, dtype in outs]
    return pl.pallas_call(
        kernel,
        out_shape=shapes,
        in_specs=ins,
        out_specs=[VM] * len(shapes),
        scratch_shapes=list(scratch),
        cost_estimate=pl.CostEstimate(flops=flops, bytes_accessed=100_000, transcendentals=0),
        compiler_params=pltpu.CompilerParams(vmem_limit_bytes=vmem),
    )


FIELD = ((CX, CY, CZ), F32)


def swaps(count):
    first = [(i, i ^ 1) for i in range(count)]
    second = [(i, ((i - 1) ^ 1) + 1) for i in range(1, count - 1)]
    return first, second


def trade(a, b, axis):
    first, second = swaps(lax.axis_size(axis))
    return lax.ppermute(a, axis, first), lax.ppermute(b, axis, second)


def everyone(pay, rows):
    moved = lax.all_to_all(pay.reshape(DEVICES, rows, LANES), BOTH, 0, 0)
    return moved.reshape(DEVICES * rows, LANES)


def local(
    c_old, s_old, rate_time, capacity, agg_count, coarse_order, coarse_cols, coarse_off, coarse_diag
):
    order = coarse_order.reshape(LANES, LANES)

    c, ic, s, zs, pay = call(
        source_kernel, [SM, SM, VM, HB, HB, VM],
        [FIELD, FIELD, FIELD, FIELD, ((4 * DEVICES, LANES), F32)],
        scratch=[
            pltpu.VMEM((RATES, CX, CY, CZ), F32),
            pltpu.VMEM((RATES, CX, CY, CZ), F32),
            pltpu.SemaphoreType.DMA((2, CX)),
        ],
        vmem=63 << 20,
    )(capacity, agg_count, c_old, s_old, rate_time, coarse_diag.reshape(16, LANES))
    (tab,) = call(table_kernel, [VM] * 4, [((16, SHARD_ROWS), F32)], vmem=63 << 20)(
        coarse_cols, coarse_off, coarse_diag.reshape(1, SHARD_ROWS), ic
    )
    tabs = []
    for hop in (0, 2, 4, 6):
        mine = lax.ppermute(tab, "coarse", [(i, (i + hop) % 8) for i in range(8)]) if hop else tab
        tabs += [mine, lax.ppermute(mine, "coarse", [(i, i ^ 1) for i in range(8)])]
    gathered = everyone(pay, 4)
    inverse, blocks = call(
        order_kernel, [VM] * 2, [((LANES, LANES), I32), ((LANES, LANES), BF16)], flops=10_000_000
    )(order, tab)

    pe, plan, own, xa, xb = call(
        first_kernel, [SM] + [VM] * 14,
        [FIELD, ((KC + 1, 24, SLOTS), F32), ((8, SLOTS), F32), ((7, CY, CZ), F32), ((7, CY, CZ), F32)],
        scratch=[pltpu.VMEM((SHARDS * 32, SHARD_ROWS), BF16)],
    )(agg_count, gathered, order, inverse, blocks, *tabs, zs, ic)
    xa, xb = trade(xa, xb, "coarse")
    ya, yb = call(
        widen_kernel, [VM] * 5, [((CX + 4, CY, CZ), F32)] * 2
    )(zs, ic, pe, xa, xb)
    ya, yb = trade(ya, yb, "fine")
    z1, w1, sw, pay = call(
        second_kernel, [SM] + [VM] * 8, [FIELD, FIELD, FIELD, ((2 * DEVICES, LANES), F32)]
    )(agg_count, zs, ic, pe, c, xa, xb, ya, yb)
    sums = everyone(pay, 2)

    p, xa, xb, ya, yb = call(
        third_kernel, [SM] + [VM] * 7, [FIELD] + [((CY, CZ), F32)] * 4
    )(agg_count, sums, gathered, inverse, blocks, plan, own, sw)
    xa, xb = trade(xa, xb, "coarse")
    ya, yb = trade(ya, yb, "fine")
    (pay,) = call(
        products_kernel, [VM] * 8, [((DEVICES, LANES), F32)]
    )(s, w1, p, c, xa, xb, ya, yb)
    parts = everyone(pay, 1)
    mobile, immobile = call(
        update_kernel, [VM] * 5, [FIELD, ((RATES, CX, CY, CZ), F32)]
    )(parts, z1, p, s_old, rate_time)
    return mobile, immobile


def solution(mesh):
    return jax.shard_map(
        local,
        mesh=mesh,
        in_specs=(
            P("coarse", "fine", None),
            P(None, "coarse", "fine", None),
            P(None, "coarse", "fine", None),
            P(),
            P(("coarse", "fine")),
            P(),
            P(None, "coarse"),
            P(None, "coarse"),
            P("coarse"),
        ),
        out_specs=(P("coarse", "fine", None), P(None, "coarse", "fine", None)),
        check_vma=False,
    )
```

```python
import jax
import jax.numpy as jnp
from jax import lax
from jax.experimental import pallas as pl
from jax.experimental.pallas import tpu as pltpu
from jax.sharding import PartitionSpec as P

BOTH = ("coarse", "fine")
CX, CY, CZ = 4, 8, 256
RATES = 16
KC = 8
DEVICES = 128
LANES = 128
SLOTS = 256
SHARDS = 8
SHARD_ROWS = 2048
FLOW = 50.0
UNUSED = 1e30
F32, BF16, I32 = jnp.float32, jnp.bfloat16, jnp.int32
VM = pl.BlockSpec(memory_space=pltpu.VMEM)
SM = pl.BlockSpec(memory_space=pltpu.SMEM)
HB = pl.BlockSpec(memory_space=pltpu.HBM)


def places():
    return lax.axis_index("coarse").astype(I32), lax.axis_index("fine").astype(I32)


def iota(shape, dim):
    return lax.broadcasted_iota(I32, shape, dim)


def lane_take(table, index):
    return jnp.take_along_axis(table, index, axis=1, mode="promise_in_bounds")


def nt(left, right):
    return lax.dot_general(left, right, (((1,), (1,)), ((), ())), preferred_element_type=F32)


def nn(left, right):
    return jnp.dot(left, right, preferred_element_type=F32)


def split2(values):
    high = values.astype(BF16)
    return high, (values - high.astype(F32)).astype(BF16)


def slots_of(plane, half, count):
    row = (plane * CY + iota((CY, LANES), 0)) * 2 + half
    return ((row * LANES + iota((CY, LANES), 1)) * count) >> 13


def restrict(cells, count):
    slot = iota((CY, SLOTS), 1)
    total = jnp.zeros((CY, SLOTS), F32)
    for plane in range(CX):
        for half in range(2):
            values = cells[plane][:, half * LANES : (half + 1) * LANES]
            row = (plane * CY + iota((CY, 1), 0)) * 2 + half
            first = (row * count) >> 6
            member = slots_of(plane, half, count) - first
            relative = slot - first
            for k in range(5):
                part = jnp.sum(jnp.where(member == k, values, 0.0), axis=1, keepdims=True)
                total = total + jnp.where(relative == k, part, 0.0)
    return jnp.sum(total, axis=0, keepdims=True)


def prolong(entries, count):
    low = jnp.broadcast_to(entries[:, :LANES], (CY, LANES))
    high = jnp.broadcast_to(entries[:, LANES:], (CY, LANES))
    planes = []
    for plane in range(CX):
        halves = []
        for half in range(2):
            slot = slots_of(plane, half, count)
            place = slot & 127
            halves.append(jnp.where(slot < LANES, lane_take(low, place), lane_take(high, place)))
        planes.append(jnp.concatenate(halves, axis=1))
    return planes


def couple(left, mid, right, up, down):
    length = mid.shape[1]
    lane = iota(mid.shape, 1)
    behind = jnp.where(lane == 0, 0.0, pltpu.roll(mid, 1, 1))
    ahead = jnp.where(lane == length - 1, 0.0, pltpu.roll(mid, length - 1, 1))
    return 8.0 * (left + right + up + down + ahead) + 10.0 * behind


def source_kernel(
    cap, count, c_old, s_old_hbm, rate_hbm, diag, diag_row, order, cols, off,
    c_out, ic_out, s_out, zs_out, tile_out, tab, s_old, rate, sems,
):
    place = places()
    me = place[0] * 16 + place[1]
    n = count[0]
    copies = []
    for x in range(CX):
        pair = (
            pltpu.make_async_copy(rate_hbm.at[:, x], rate.at[:, x], sems.at[0, x]),
            pltpu.make_async_copy(s_old_hbm.at[:, x], s_old.at[:, x], sems.at[1, x]),
        )
        for copy in pair:
            copy.start()
        copies.append(pair)
    tab[0:8, :] = cols[...].astype(F32)
    tab[8:16, :] = off[...] * (0.8 / diag_row[...])
    mine = (order[0:1, :] >> 7) == me
    low = jnp.sum(jnp.where(mine, (order[...] & 127).astype(F32), 0.0), axis=1, keepdims=True)
    spot = iota((LANES, LANES), 1).astype(F32) == low
    inverse = jnp.sum(jnp.where(spot, iota((LANES, LANES), 0).astype(F32), 0.0), axis=0, keepdims=True)
    planes = []
    for x in range(CX):
        for copy in copies[x]:
            copy.wait()
        mass = jnp.zeros((CY, CZ), F32)
        extra = jnp.zeros((CY, CZ), F32)
        for k in range(RATES):
            r = rate[k, x]
            weighted = cap[k] * (r / (1.0 + r))
            mass = mass + weighted
            extra = extra + weighted * s_old[k, x]
        centre = (1.0 + mass) + FLOW
        source = c_old[x] + extra
        inv = 1.0 / centre
        c_out[x] = centre
        ic_out[x] = inv
        s_out[x] = source
        zs_out[x] = 0.8 * source * inv
        planes.append(source)
    sums = jnp.where(iota((1, SLOTS), 1) < n, restrict(planes, n), UNUSED)
    kind = iota((8, LANES), 0) & 3
    rows = [sums[:, :LANES], sums[:, LANES:], diag[pl.ds(place[1], 1), :], inverse]
    tile = jnp.broadcast_to(rows[3], (8, LANES))
    for k in range(3):
        tile = jnp.where(kind == k, rows[k], tile)
    tile_out[...] = tile


def repeat_kernel(tile, pay):
    for i in range(DEVICES // 2):
        pay[pl.ds(8 * i, 8), :] = tile[...]


def read_sums(gathered):
    low = gathered[pl.ds(0, DEVICES, stride=4), :]
    high = gathered[pl.ds(1, DEVICES, stride=4), :]
    diag = gathered[pl.ds(2, DEVICES, stride=4), :]
    inverse = gathered[pl.ds(3, DEVICES, stride=4), :].astype(I32)
    used = ((low < 0.5 * UNUSED).astype(F32) + (high < 0.5 * UNUSED).astype(F32)).astype(BF16)
    return low, high, diag, inverse, used


def offsets_of(used):
    below = iota((LANES, LANES), 1) < iota((LANES, LANES), 0)
    ones = jnp.ones((LANES, LANES), BF16)
    by_row = nn(nn(below.astype(F32).astype(BF16), used).astype(BF16), ones).astype(I32)
    counts = nt(ones, used)
    above = iota((LANES, LANES), 0) < iota((LANES, LANES), 1)
    by_lane = nn(counts[0:8].astype(BF16), above.astype(F32).astype(BF16))[0:1].astype(I32)
    return by_row, by_lane


def blocks_of(order):
    return (iota((LANES, LANES), 0) == (order[0:1, :] >> 7)).astype(F32).astype(BF16)


def assemble(low, high, offsets, inverse, blocks):
    by_row, by_lane = offsets
    lane = iota((LANES, LANES), 1)
    shift = by_row & 127
    place = (lane - shift) & 127
    low = lane_take(low, place)
    high = lane_take(high, place)
    kept = lane >= shift
    rows = (jnp.where(kept, low, 0.0), jnp.where(kept, high, low), jnp.where(kept, 0.0, high))
    start = by_lane >> 7
    spots = [(iota((LANES, LANES), 0) == start + j).astype(F32).astype(BF16) for j in range(3)]
    parts = [jnp.concatenate(split2(r), axis=1) for r in rows]
    table = nn(jnp.concatenate(spots, axis=1), jnp.concatenate(parts, axis=0))
    by_block = nt(blocks, jnp.concatenate([table[:, :LANES], table[:, LANES:]], axis=0).astype(BF16))
    return lane_take(by_block[:, :LANES] + by_block[:, LANES:], inverse)


def fetch(table, unknown, coarse):
    inner = unknown & (SHARD_ROWS - 1)
    shard = unknown >> 11
    shard = shard ^ coarse
    found = jnp.zeros((SHARDS * 32, SLOTS), F32)
    for chunk in range(SHARD_ROWS // 256):
        spot = (iota((256, SLOTS), 0) + chunk * 256 == inner).astype(F32).astype(BF16)
        found = found + nn(table[:, chunk * 256 : (chunk + 1) * 256], spot)
    found = found.reshape(SHARDS, 32, SLOTS)
    picked = jnp.zeros((32, SLOTS), F32)
    for g in range(SHARDS):
        picked = picked + jnp.where(shard == g, found[g], 0.0)
    return picked[0:8], picked[8:16], picked[16:24] + picked[24:32]


def coarse_solve(values, plan, own):
    high, low = split2(values.T)
    table = jnp.concatenate([high, low], axis=1)
    row = iota((LANES, SLOTS), 0).astype(F32)

    def gather(block, inner):
        spot = (row == block).astype(F32).astype(BF16)
        found = nn(table, jnp.concatenate([spot, spot], axis=0))
        return jnp.sum(jnp.where(row == inner, found, 0.0).reshape(16, 8, SLOTS), axis=0)

    def entry(k, total):
        part = -1.4 * gather(plan[KC, pl.ds(k, 1), :], plan[KC, pl.ds(8 + k, 1), :])
        for j in range(KC):
            weight = plan[k, 16 + j : 17 + j, :]
            part = part + weight * gather(plan[k, j : j + 1, :], plan[k, 8 + j : 9 + j, :])
        return total + plan[KC, pl.ds(16 + k, 1), :] * part

    total = 1.24 * gather(own[0:1, :], own[1:2, :])
    total = lax.fori_loop(0, KC, entry, total)
    return jnp.sum(total, axis=0, keepdims=True)


def plan_rows(ref, k, parts):
    ref[k, 0:8, :] = parts[0]
    ref[k, 8:16, :] = parts[1]
    ref[k, 16:24, :] = parts[2]


def first_kernel(
    count, gathered, order, tab0, tab1, tab2, tab3, tab4, tab5, tab6, tab7, zs, ic,
    pe_out, plan, own, beside, xa, xb, table,
):
    place = places()
    n = count[0]
    me = place[0] * 16 + place[1]
    low, high, diag, inverse, used = read_sums(gathered)
    offsets = offsets_of(used)
    sums = assemble(
        jnp.where(low < 0.5 * UNUSED, low, 0.0), jnp.where(high < 0.5 * UNUSED, high, 0.0),
        offsets, inverse, blocks_of(order),
    )
    values = 0.8 * sums / diag
    counts = nn(used, jnp.ones((LANES, LANES), BF16))
    wanted = me + jnp.where(iota((8, LANES), 0) < 4, -1, 1)
    row = iota((LANES, LANES), 0)
    before = jnp.sum(jnp.where(row == me - 1, counts, 0.0), axis=0, keepdims=True)
    after = jnp.sum(jnp.where(row == me + 1, counts, 0.0), axis=0, keepdims=True)
    beside[...] = jnp.where(wanted < me, before, after).astype(I32)

    tabs = (tab0, tab1, tab2, tab3, tab4, tab5, tab6, tab7)
    for g in range(SHARDS):
        cols = tabs[g][0:8, :]
        high = jnp.floor(cols * (1.0 / 128.0))
        pair = jnp.concatenate([high, cols - 128.0 * high], axis=0)
        table[32 * g : 32 * g + 16, :] = pair.astype(BF16)
        off = tabs[g][8:16, :]
        big = off.astype(BF16).astype(F32)
        table[32 * g + 16 : 32 * g + 32, :] = jnp.concatenate([big, off - big], axis=0).astype(BF16)

    mine = jnp.sum(jnp.where(row == me, offsets[0].astype(F32), 0.0), axis=0, keepdims=True).astype(I32)
    numbers = order[...].astype(F32)
    start = mine >> 7
    lines = []
    spread = (iota((8, LANES), 1) + mine) & 127
    for j in range(3):
        line = jnp.sum(jnp.where(row == start + j, numbers, 0.0), axis=0, keepdims=True)
        lines.append(lane_take(jnp.broadcast_to(line, (8, LANES)), spread))
    inside = iota((8, LANES), 1) + (mine & 127) < LANES
    unknown = jnp.concatenate(
        [jnp.where(inside, lines[0], lines[1]), jnp.where(inside, lines[1], lines[2])], axis=1
    )[0:1].astype(I32)
    own[0:1, :] = (unknown >> 7).astype(F32)
    own[1:2, :] = (unknown & 127).astype(F32)

    plan_rows(plan, KC, fetch(table, unknown, place[0]))

    def level(k, carry):
        col = 128.0 * plan[KC, pl.ds(k, 1), :] + plan[KC, pl.ds(8 + k, 1), :]
        plan_rows(plan, k, fetch(table, col.astype(I32), place[0]))
        return carry

    lax.fori_loop(0, KC, level, 0)

    pe = prolong(coarse_solve(values, plan, own), n)
    for x in range(CX):
        pe_out[x] = pe[x]

    def message(out, upper):
        for k in range(3):
            out[k] = zs[CX - 3 + k] if upper else zs[k]
        for k in range(2):
            out[3 + k] = ic[CX - 2 + k] if upper else ic[k]
            out[5 + k] = pe[CX - 2 + k] if upper else pe[k]

    even = (place[0] & 1) == 0

    @pl.when(even)
    def _():
        message(xa, True)
        message(xb, False)

    @pl.when(jnp.logical_not(even))
    def _():
        message(xa, False)
        message(xb, True)


def below_above(index, count, a, b):
    even = (index & 1) == 0
    inner = jnp.logical_and(index > 0, index < count - 1)

    def near(i):
        return a[i], jnp.where(inner, b[i], 0.0)

    def below(i):
        first, second = near(i)
        return jnp.where(even, second, first)

    def above(i):
        first, second = near(i)
        return jnp.where(even, first, second)

    return below, above


def ghost_rows(field, x):
    return max(0, (4, 3, 3)[field] - max(0, -x, x - CX + 1))


PACKED = [(f, x, k) for f in range(3) for x in range(-3, CX + 3) for k in range(ghost_rows(f, x))]


def wide_plane(own, below, above):
    depth = (3, 2, 2)
    base = (0, 3, 5)

    def plane(field, x):
        if x < 0:
            return below(base[field] + depth[field] + x)
        if x >= CX:
            return above(base[field] + x - CX)
        return own[field][x]

    return plane


def widen_kernel(zs, ic, pe, xa, xb, ya, yb):
    place = places()
    plane = wide_plane((zs, ic, pe), *below_above(place[0], 8, xa, xb))
    even = (place[1] & 1) == 0
    upper, lower = [], []
    for f in range(3):
        for x in range(-3, CX + 3):
            d = ghost_rows(f, x)
            if d:
                here = plane(f, x)
                upper.append(here[CY - d :])
                lower.append(here[:d])
    upper, lower = jnp.concatenate(upper, axis=0), jnp.concatenate(lower, axis=0)
    ya[...] = jnp.where(even, upper, lower)
    yb[...] = jnp.where(even, lower, upper)


def second_kernel(
    count, zs, ic, pe, c, xa, xb, ya, yb, z1_out, w1_out, sw_out, sw_ghost, s_ghost, w_ghost, pay
):
    place = places()
    middle = wide_plane((zs, ic, pe), *below_above(place[0], 8, xa, xb))
    near, far = [side(...) for side in below_above(place[1], 16, ya, yb)]

    def plane(field, x):
        d = ghost_rows(field, x)
        here = middle(field, x)
        if not d:
            blank = jnp.zeros((8, CZ), F32)
            return jnp.concatenate([blank, here, blank], axis=0)
        at = PACKED.index((field, x, 0))
        parts = [near[at : at + d], here, far[at : at + d]]
        if d < 8:
            blank = jnp.zeros((8 - d, CZ), F32)
            parts = [blank] + parts + [blank]
        return jnp.concatenate(parts, axis=0)

    def neighbours(get, x):
        mid = get(x)
        rows = mid.shape[0]
        return couple(get(x - 1), mid, get(x + 1), pltpu.roll(mid, 1, 0), pltpu.roll(mid, rows - 1, 0))

    z = {x: plane(0, x) for x in range(-3, CX + 3)}
    inv = {x: plane(1, x) for x in range(-2, CX + 2)}
    first = {}
    for x in range(-2, CX + 2):
        first[x] = 1.2 * z[x] + 0.8 * inv[x] * neighbours(z.get, x) + plane(2, x)
    zw = {}
    image = []
    for x in range(-1, CX + 1):
        beside = neighbours(first.get, x)
        zw[x] = 0.8 * (first[x] - inv[x] * beside)
        if 0 <= x < CX:
            here = c[x] * first[x][8:16] - beside[8:16]
            image.append(here)
            z1_out[x] = first[x][8:16]
            w1_out[x] = here
    for x in range(CX):
        smooth = 1.2 * zw[x] + 0.8 * inv[x] * neighbours(zw.get, x)
        sw_out[x] = smooth[8:16]
        for at, row in ((x, 7), (CX + x, 16)):
            iv = inv[x][row : row + 1]
            scale = jnp.where(iv > 0.0, 1.25 / jnp.where(iv > 0.0, iv, 1.0), 0.0)
            sw_ghost[at : at + 1, :] = smooth[row : row + 1]
            s_ghost[at : at + 1, :] = z[x][row : row + 1] * scale
            w_ghost[at : at + 1, :] = zw[x][row : row + 1] * scale
    sums = restrict(image, count[0])
    kind = iota((8, LANES), 0) & 1
    tile = jnp.where(kind == 0, sums[:, :LANES], sums[:, LANES:])
    for i in range(DEVICES // 4):
        pay[pl.ds(8 * i, 8), :] = tile


def third_kernel(count, sums, gathered, order, plan, own, sw, p_out, pe_face, e_face, xa, xb):
    place = places()
    n = count[0]
    _, _, diag, inverse, used = read_sums(gathered)
    values = assemble(
        sums[pl.ds(0, DEVICES, stride=2), :], sums[pl.ds(1, DEVICES, stride=2), :],
        offsets_of(used), inverse, blocks_of(order),
    )
    entries = coarse_solve(0.8 * values / diag, plan, own)
    pe = prolong(entries, n)
    p = [sw[x] + pe[x] for x in range(CX)]
    for x in range(CX):
        p_out[x] = p[x]
        pe_face[x : x + 1, :] = pe[x][0:1]
        pe_face[CX + x : CX + x + 1, :] = pe[x][CY - 1 : CY]
    even = (place[0] & 1) == 0
    xa[...] = jnp.where(even, p[CX - 1], p[0])
    xb[...] = jnp.where(even, p[0], p[CX - 1])
    lane = iota((8, LANES), 1)
    group = lane >> 4
    cells = ((group & 3) * CY + jnp.where(group < 4, 0, CY - 1)) * CZ
    slot = jnp.minimum(((cells * n) >> 13) + (lane & 15), SLOTS - 1)
    low = jnp.broadcast_to(entries[:, :LANES], (8, LANES))
    high = jnp.broadcast_to(entries[:, LANES:], (8, LANES))
    e_face[...] = jnp.where(slot < LANES, lane_take(low, slot & 127), lane_take(high, slot & 127))


def products_kernel(s, w1, p, c, xa, xb, sw_ghost, s_ghost, w_ghost, pe_face, e_face, beside, pay):
    place = places()
    below, above = [side(...) for side in below_above(place[0], 8, xa, xb)]
    sums = [jnp.zeros((CY, CZ), F32) for _ in range(6)]
    row = iota((CY, CZ), 0)
    rims = [None] * (2 * CX)
    for x in range(CX):
        mid = p[x]
        left = p[x - 1] if x else below
        right = p[x + 1] if x + 1 < CX else above
        up = jnp.where(row == 0, sw_ghost[x : x + 1, :], pltpu.roll(mid, 1, 0))
        down = jnp.where(row == CY - 1, sw_ghost[CX + x : CX + x + 1, :], pltpu.roll(mid, CY - 1, 0))
        q = c[x] * mid - couple(left, mid, right, up, down)
        rims[x], rims[CX + x] = q[0:1], q[CY - 1 : CY]
        a, b = s[x], w1[x]
        for k, term in enumerate((a * a, a * b, a * q, b * b, b * q, q * q)):
            sums[k] = sums[k] + term
    exists = jnp.where(row < 4, place[1], 15 - place[1]) > 0
    face = pe_face[...]
    sums[2] = sums[2] - 8.0 * face * s_ghost[...]
    sums[4] = sums[4] - 8.0 * face * w_ghost[...]
    sums[5] = sums[5] + jnp.where(exists, 64.0 * face * face, 0.0)
    rim = jnp.where(exists, jnp.concatenate(rims, axis=0), 0.0)
    n = jnp.concatenate([beside[...], beside[...]], axis=1)
    cells = ((row & 3) * CY + jnp.where(row < 4, CY - 1, 0)) * CZ
    member = (((cells + iota((CY, CZ), 1)) * n) >> 13) - ((cells * n) >> 13)
    lane = iota((8, LANES), 1)
    start = iota((8, LANES), 0) * 16
    spread = jnp.zeros((8, LANES), F32)
    for k in range(9):
        part = jnp.sum(jnp.where(member == k, rim, 0.0), axis=1, keepdims=True)
        spread = spread + jnp.where(lane == start + k, part, 0.0)
    top = jnp.broadcast_to(jnp.sum(spread, axis=0, keepdims=True), (8, LANES))
    for k in range(6):
        top = top + jnp.where(lane == 9 + k, jnp.sum(sums[k], keepdims=True), 0.0)
    tile = jnp.where((iota((8, LANES), 0) & 1) == 0, top, e_face[...])
    for i in range(DEVICES // 4):
        pay[pl.ds(8 * i, 8), :] = tile


def update_kernel(parts, z1, p, s_old, rate, mobile, immobile):
    top = parts[pl.ds(0, DEVICES, stride=2), :]
    face = pltpu.roll(parts[pl.ds(1, DEVICES, stride=2), :], LANES // 2, 1)
    lane = iota((DEVICES, LANES), 1)
    other = jnp.where(lane < LANES // 2, pltpu.roll(face, 1, 0), pltpu.roll(face, DEVICES - 1, 0))
    cross = jnp.sum(jnp.where((lane & 15) < 9, top * other, 0.0), keepdims=True)
    total = jnp.sum(top, axis=0, keepdims=True)
    ss, sw, sq, ww, wq, qq = [total[:, 9 + k : 10 + k] for k in range(6)]
    qq = qq - 16.0 * cross
    factor = wq / ww
    y2 = (sq - factor * sw) / (qq - factor * wq)
    y1 = (sw - wq * y2) / ww
    for x in range(CX):
        new = y1 * z1[x] + y2 * p[x]
        mobile[x] = new
        for k in range(RATES):
            r = rate[k, x]
            immobile[k, x] = (s_old[k, x] + r * new) / (1.0 + r)


def call(kernel, ins, outs, scratch=(), flops=10_000, vmem=48 << 20):
    shapes = [jax.ShapeDtypeStruct(shape, dtype) for shape, dtype in outs]
    return pl.pallas_call(
        kernel,
        out_shape=shapes,
        in_specs=ins,
        out_specs=[VM] * len(shapes),
        scratch_shapes=list(scratch),
        cost_estimate=pl.CostEstimate(flops=flops, bytes_accessed=100_000, transcendentals=0),
        compiler_params=pltpu.CompilerParams(vmem_limit_bytes=vmem),
    )


FIELD = ((CX, CY, CZ), F32)


def trade(a, b, axis):
    n, m = lax.axis_size("coarse"), lax.axis_size("fine")
    inside, between = [], []
    for c in range(n):
        for f in range(m):
            me = c * m + f
            at, count, step = (c, n, m) if axis == "coarse" else (f, m, 1)
            inside.append((me, me + ((at ^ 1) - at) * step))
            if 0 < at < count - 1:
                between.append((me, me + (((at - 1) ^ 1) + 1 - at) * step))
            elif axis == "fine":
                between.append((me, (c ^ 1) * m + f))
            else:
                between.append((me, (n - 1 - c) * m + f))
    b = lax.ppermute(b, BOTH, between)
    return lax.ppermute(a, BOTH, inside), b


def everyone(pay, rows):
    moved = lax.all_to_all(pay.reshape(DEVICES, rows, LANES), BOTH, 0, 0)
    return moved.reshape(DEVICES * rows, LANES)


def local(
    c_old, s_old, rate_time, capacity, agg_count, coarse_order, coarse_cols, coarse_off, coarse_diag
):
    order = coarse_order.reshape(LANES, LANES)
    c, ic, s, zs, tile, tab = call(
        source_kernel, [SM, SM, VM, HB, HB] + [VM] * 5,
        [FIELD, FIELD, FIELD, FIELD, ((8, LANES), F32), ((16, SHARD_ROWS), F32)],
        scratch=[
            pltpu.VMEM((RATES, CX, CY, CZ), F32),
            pltpu.VMEM((RATES, CX, CY, CZ), F32),
            pltpu.SemaphoreType.DMA((2, CX)),
        ],
        vmem=63 << 20,
    )(
        capacity, agg_count, c_old, s_old, rate_time, coarse_diag.reshape(16, LANES),
        coarse_diag.reshape(1, SHARD_ROWS), order, coarse_cols, coarse_off,
    )
    tabs = []
    for hop in (0, 2, 4, 6):
        shard = lax.ppermute(tab, "coarse", [(i, i ^ hop) for i in range(8)]) if hop else tab
        tabs += [shard, lax.ppermute(shard, "coarse", [(i, i ^ 1) for i in range(8)])]
    (pay,) = call(repeat_kernel, [VM], [((4 * DEVICES, LANES), F32)])(tile)
    gathered = everyone(pay, 4)

    pe, plan, own, beside, xa, xb = call(
        first_kernel, [SM] + [VM] * 12,
        [
            FIELD, ((KC + 1, 24, SLOTS), F32), ((8, SLOTS), F32), ((8, LANES), I32),
            ((7, CY, CZ), F32), ((7, CY, CZ), F32),
        ],
        scratch=[pltpu.VMEM((SHARDS * 32, SHARD_ROWS), BF16)],
    )(agg_count, gathered, order, *tabs, zs, ic)
    xa, xb = trade(xa, xb, "coarse")
    ya, yb = call(
        widen_kernel, [VM] * 5, [((len(PACKED), CZ), F32)] * 2
    )(zs, ic, pe, xa, xb)
    ya, yb = trade(ya, yb, "fine")
    z1, w1, sw, sw_ghost, s_ghost, w_ghost, pay = call(
        second_kernel, [SM] + [VM] * 8,
        [FIELD, FIELD, FIELD] + [((CY, CZ), F32)] * 3 + [((2 * DEVICES, LANES), F32)],
    )(agg_count, zs, ic, pe, c, xa, xb, ya, yb)
    sums = everyone(pay, 2)

    p, pe_face, e_face, xa, xb = call(
        third_kernel, [SM] + [VM] * 6,
        [FIELD, ((CY, CZ), F32), ((8, LANES), F32), ((CY, CZ), F32), ((CY, CZ), F32)],
    )(agg_count, sums, gathered, order, plan, own, sw)
    xa, xb = trade(xa, xb, "coarse")
    (pay,) = call(
        products_kernel, [VM] * 12, [((2 * DEVICES, LANES), F32)]
    )(s, w1, p, c, xa, xb, sw_ghost, s_ghost, w_ghost, pe_face, e_face, beside)
    parts = everyone(pay, 2)
    mobile, immobile = call(
        update_kernel, [VM] * 5, [FIELD, ((RATES, CX, CY, CZ), F32)]
    )(parts, z1, p, s_old, rate_time)
    return mobile, immobile


def solution(mesh):
    return jax.shard_map(
        local,
        mesh=mesh,
        in_specs=(
            P("coarse", "fine", None),
            P(None, "coarse", "fine", None),
            P(None, "coarse", "fine", None),
            P(),
            P(("coarse", "fine")),
            P(),
            P(None, "coarse"),
            P(None, "coarse"),
            P("coarse"),
        ),
        out_specs=(P("coarse", "fine", None), P(None, "coarse", "fine", None)),
        check_vma=False,
    )
```

```python
import jax
import jax.numpy as jnp
from jax import lax
from jax.experimental import pallas as pl
from jax.experimental.pallas import tpu as pltpu
from jax.sharding import PartitionSpec as P

BOTH = ("coarse", "fine")
CX, CY, CZ = 4, 8, 256
RATES = 16
KC = 8
DEVICES = 128
LANES = 128
SLOTS = 256
SHARDS = 8
SHARD_ROWS = 2048
FLOW = 50.0
TABLE_ROWS = 128
UNUSED = 1e30
F32, BF16, I32 = jnp.float32, jnp.bfloat16, jnp.int32
VM = pl.BlockSpec(memory_space=pltpu.VMEM)
SM = pl.BlockSpec(memory_space=pltpu.SMEM)
HB = pl.BlockSpec(memory_space=pltpu.HBM)


def places():
    return lax.axis_index("coarse").astype(I32), lax.axis_index("fine").astype(I32)


def iota(shape, dim):
    return lax.broadcasted_iota(I32, shape, dim)


def lane_take(table, index):
    return jnp.take_along_axis(table, index, axis=1, mode="promise_in_bounds")


def nt(left, right):
    return lax.dot_general(left, right, (((1,), (1,)), ((), ())), preferred_element_type=F32)


def nn(left, right):
    return jnp.dot(left, right, preferred_element_type=F32)


def split2(values):
    high = values.astype(BF16)
    return high, (values - high.astype(F32)).astype(BF16)


def slots_of(plane, half, count):
    row = (plane * CY + iota((CY, LANES), 0)) * 2 + half
    return ((row * LANES + iota((CY, LANES), 1)) * count) >> 13


def restrict_plane(values, plane, count, total, base):
    slot = iota(total.shape, 1) + base
    for half in range(2):
        part_of = values[:, half * LANES : (half + 1) * LANES]
        row = (plane * CY + iota((CY, 1), 0)) * 2 + half
        first = (row * count) >> 6
        member = slots_of(plane, half, count) - first
        relative = slot - first
        for k in range(5):
            part = jnp.sum(jnp.where(member == k, part_of, 0.0), axis=1, keepdims=True)
            total = total + jnp.where(relative == k, part, 0.0)
    return total


def restrict(cells, count):
    total = jnp.zeros((CY, SLOTS), F32)
    for plane in range(CX):
        total = restrict_plane(cells[plane], plane, count, total, 0)
    return jnp.sum(total, axis=0, keepdims=True)


def rim_restrict(rim, count):
    n = jnp.concatenate([count, count], axis=1)
    row = iota((CY, CZ), 0)
    cells = ((row & 3) * CY + jnp.where(row < 4, CY - 1, 0)) * CZ
    member = (((cells + iota((CY, CZ), 1)) * n) >> 13) - ((cells * n) >> 13)
    lane = iota((8, LANES), 1)
    start = iota((8, LANES), 0) * 16
    spread = jnp.zeros((8, LANES), F32)
    for k in range(9):
        part = jnp.sum(jnp.where(member == k, rim, 0.0), axis=1, keepdims=True)
        spread = spread + jnp.where(lane == start + k, part, 0.0)
    return jnp.sum(spread, axis=0, keepdims=True)


def rim_exists(index):
    return jnp.where(iota((CY, CZ), 0) < 4, index, 15 - index) > 0


def prolong(entries, count):
    low = jnp.broadcast_to(entries[:, :LANES], (CY, LANES))
    high = jnp.broadcast_to(entries[:, LANES:], (CY, LANES))
    planes = []
    for plane in range(CX):
        halves = []
        for half in range(2):
            slot = slots_of(plane, half, count)
            place = slot & 127
            halves.append(jnp.where(slot < LANES, lane_take(low, place), lane_take(high, place)))
        planes.append(jnp.concatenate(halves, axis=1))
    return planes


def couple(left, mid, right, up, down):
    length = mid.shape[1]
    lane = iota(mid.shape, 1)
    behind = jnp.where(lane == 0, 0.0, pltpu.roll(mid, 1, 1))
    ahead = jnp.where(lane == length - 1, 0.0, pltpu.roll(mid, length - 1, 1))
    return 8.0 * (left + right + up + down + ahead) + 10.0 * behind


def source_kernel(
    cap, c_old, s_old_hbm, rate_hbm, diag, cols, off,
    c_out, ic_out, s_out, zs_out, tab, both, xb, ya, yb, s_old, rate, sems,
):
    copies = []
    for x in range(CX):
        pair = (
            pltpu.make_async_copy(rate_hbm.at[:, x], rate.at[:, x], sems.at[0, x]),
            pltpu.make_async_copy(s_old_hbm.at[:, x], s_old.at[:, x], sems.at[1, x]),
        )
        for copy in pair:
            copy.start()
        copies.append(pair)
    for j in range(SHARD_ROWS // 256):
        at = slice(256 * j, 256 * j + 256)
        part = jnp.concatenate([cols[:, at].astype(F32), off[:, at] * (0.8 / diag[:, at])], axis=0)
        tab[16 * j : 16 * j + 16, :] = part
        both[16 * j : 16 * j + 16, :] = part
    smooth, inverse = [], []
    for x in range(CX):
        for copy in copies[x]:
            copy.wait()
        mass = jnp.zeros((CY, CZ), F32)
        extra = jnp.zeros((CY, CZ), F32)
        for k in range(RATES):
            r = rate[k, x]
            weighted = cap[k] * (r / (1.0 + r))
            mass = mass + weighted
            extra = extra + weighted * s_old[k, x]
        centre = (1.0 + mass) + FLOW
        source = c_old[x] + extra
        inv = 1.0 / centre
        c_out[x] = centre
        ic_out[x] = inv
        s_out[x] = source
        zs_out[x] = 0.8 * source * inv
        smooth.append(0.8 * source * inv)
        inverse.append(inv)
    xa, xb[...] = send_planes([(smooth, 3), (inverse, 2)])
    both[TABLE_ROWS:, :] = xa
    ya[...], yb[...] = send_rims(smooth)


def send_planes(fields):
    even = (places()[0] & 1) == 0
    upper = jnp.concatenate([p for planes, depth in fields for p in planes[CX - depth :]], axis=0)
    lower = jnp.concatenate([p for planes, depth in fields for p in planes[:depth]], axis=0)
    return jnp.where(even, upper, lower), jnp.where(even, lower, upper)


def send_rims(planes):
    even = (places()[1] & 1) == 0
    upper = jnp.concatenate([p[CY - 1 : CY] for p in planes] * 2, axis=0)
    lower = jnp.concatenate([p[0:1] for p in planes] * 2, axis=0)
    return jnp.where(even, upper, lower), jnp.where(even, lower, upper)


def sums_kernel(count, s, diag, order, pay):
    place = places()
    n = count[0]
    mine = (order[0:1, :] >> 7) == place[0] * 16 + place[1]
    low = jnp.sum(jnp.where(mine, (order[...] & 127).astype(F32), 0.0), axis=1, keepdims=True)
    spot = iota((LANES, LANES), 1).astype(F32) == low
    inverse = jnp.sum(jnp.where(spot, iota((LANES, LANES), 0).astype(F32), 0.0), axis=0, keepdims=True)
    sums = jnp.where(iota((1, SLOTS), 1) < n, restrict([s[x] for x in range(CX)], n), UNUSED)
    repeat4(pay, [sums[:, :LANES], sums[:, LANES:], diag[pl.ds(place[1], 1), :], inverse])


def repeat4(pay, rows):
    kind = iota((8, LANES), 0) & 3
    tile = jnp.broadcast_to(rows[3], (8, LANES))
    for k in range(3):
        tile = jnp.where(kind == k, rows[k], tile)
    for i in range(DEVICES // 2):
        pay[pl.ds(8 * i, 8), :] = tile


def read_sums(gathered):
    low = gathered[pl.ds(0, DEVICES, stride=4), :]
    high = gathered[pl.ds(1, DEVICES, stride=4), :]
    diag = gathered[pl.ds(2, DEVICES, stride=4), :]
    inverse = gathered[pl.ds(3, DEVICES, stride=4), :].astype(I32)
    used = ((low < 0.5 * UNUSED).astype(F32) + (high < 0.5 * UNUSED).astype(F32)).astype(BF16)
    return low, high, diag, inverse, used


def offsets_of(used):
    below = iota((LANES, LANES), 1) < iota((LANES, LANES), 0)
    ones = jnp.ones((LANES, LANES), BF16)
    by_row = nn(nn(below.astype(F32).astype(BF16), used).astype(BF16), ones).astype(I32)
    counts = nt(ones, used)
    above = iota((LANES, LANES), 0) < iota((LANES, LANES), 1)
    by_lane = nn(counts[0:8].astype(BF16), above.astype(F32).astype(BF16))[0:1].astype(I32)
    return by_row, by_lane


def blocks_of(order):
    return (iota((LANES, LANES), 0) == (order[0:1, :] >> 7)).astype(F32).astype(BF16)


def assemble(low, high, offsets, inverse, blocks):
    by_row, by_lane = offsets
    lane = iota((LANES, LANES), 1)
    shift = by_row & 127
    place = (lane - shift) & 127
    low = lane_take(low, place)
    high = lane_take(high, place)
    kept = lane >= shift
    rows = (jnp.where(kept, low, 0.0), jnp.where(kept, high, low), jnp.where(kept, 0.0, high))
    start = by_lane >> 7
    spots = [(iota((LANES, LANES), 0) == start + j).astype(F32).astype(BF16) for j in range(3)]
    parts = [jnp.concatenate(split2(r), axis=1) for r in rows]
    table = nn(jnp.concatenate(spots, axis=1), jnp.concatenate(parts, axis=0))
    by_block = nt(blocks, jnp.concatenate([table[:, :LANES], table[:, LANES:]], axis=0).astype(BF16))
    return lane_take(by_block[:, :LANES] + by_block[:, LANES:], inverse)


def fetch(table, unknown, coarse):
    inner = unknown & (SHARD_ROWS - 1)
    shard = unknown >> 11
    shard = shard ^ coarse
    found = jnp.zeros((SHARDS * 32, SLOTS), F32)
    for chunk in range(SHARD_ROWS // 256):
        spot = (iota((256, SLOTS), 0) + chunk * 256 == inner).astype(F32).astype(BF16)
        found = found + nn(table[:, chunk * 256 : (chunk + 1) * 256], spot)
    found = found.reshape(SHARDS, 32, SLOTS)
    picked = jnp.zeros((32, SLOTS), F32)
    for g in range(SHARDS):
        picked = picked + jnp.where(shard == g, found[g], 0.0)
    return picked[0:8], picked[8:16], picked[16:24] + picked[24:32]


def coarse_solve(values, plan, own):
    high, low = split2(values.T)
    table = jnp.concatenate([high, low], axis=1)
    row = iota((LANES, SLOTS), 0).astype(F32)

    def gather(block, inner):
        spot = (row == block).astype(F32).astype(BF16)
        found = nn(table, jnp.concatenate([spot, spot], axis=0))
        return jnp.sum(jnp.where(row == inner, found, 0.0).reshape(16, 8, SLOTS), axis=0)

    def entry(k, total):
        part = -1.4 * gather(plan[KC, pl.ds(k, 1), :], plan[KC, pl.ds(8 + k, 1), :])
        for j in range(KC):
            weight = plan[k, 16 + j : 17 + j, :]
            part = part + weight * gather(plan[k, j : j + 1, :], plan[k, 8 + j : 9 + j, :])
        return total + plan[KC, pl.ds(16 + k, 1), :] * part

    total = 1.24 * gather(own[0:1, :], own[1:2, :])
    total = lax.fori_loop(0, KC, entry, total)
    return jnp.sum(total, axis=0, keepdims=True)


def plan_rows(ref, k, parts):
    ref[k, 0:8, :] = parts[0]
    ref[k, 8:16, :] = parts[1]
    ref[k, 16:24, :] = parts[2]


def first_kernel(
    count, gathered, order, tab0, tab1, tab2, tab3, tab4, tab5, tab6, tab7,
    pe_out, plan, own, beside, across, at_row, at_lane, counts_out, xa, xb, table,
):
    place = places()
    n = count[0]
    me = place[0] * 16 + place[1]
    low, high, diag, inverse, used = read_sums(gathered)
    offsets = offsets_of(used)
    at_row[...] = offsets[0]
    at_lane[...] = jnp.broadcast_to(offsets[1], (8, LANES))
    sums = assemble(
        jnp.where(low < 0.5 * UNUSED, low, 0.0), jnp.where(high < 0.5 * UNUSED, high, 0.0),
        offsets, inverse, blocks_of(order),
    )
    values = 0.8 * sums / diag
    counts = nn(used, jnp.ones((LANES, LANES), BF16))
    counts_out[...] = counts.astype(I32)
    row = iota((LANES, LANES), 0)
    before = iota((8, LANES), 0) < 4
    for out, step in ((beside, 1), (across, 16)):
        sides = [jnp.sum(jnp.where(row == me + d, counts, 0.0), axis=0, keepdims=True) for d in (-step, step)]
        out[...] = jnp.where(before, sides[0], sides[1]).astype(I32)

    tabs = (tab0, tab1, tab2, tab3, tab4, tab5, tab6, tab7)
    for g in range(SHARDS):
        for j in range(SHARD_ROWS // 256):
            at = slice(256 * j, 256 * j + 256)
            cols = tabs[g][16 * j : 16 * j + 8, :]
            big = jnp.floor(cols * (1.0 / 128.0))
            pair = jnp.concatenate([big, cols - 128.0 * big], axis=0)
            table[32 * g : 32 * g + 16, at] = pair.astype(BF16)
            off = tabs[g][16 * j + 8 : 16 * j + 16, :]
            big = off.astype(BF16).astype(F32)
            table[32 * g + 16 : 32 * g + 32, at] = jnp.concatenate([big, off - big], axis=0).astype(BF16)

    mine = jnp.sum(jnp.where(row == me, offsets[0].astype(F32), 0.0), axis=0, keepdims=True).astype(I32)
    numbers = order[...].astype(F32)
    start = mine >> 7
    lines = []
    spread = (iota((8, LANES), 1) + mine) & 127
    for j in range(3):
        line = jnp.sum(jnp.where(row == start + j, numbers, 0.0), axis=0, keepdims=True)
        lines.append(lane_take(jnp.broadcast_to(line, (8, LANES)), spread))
    inside = iota((8, LANES), 1) + (mine & 127) < LANES
    unknown = jnp.concatenate(
        [jnp.where(inside, lines[0], lines[1]), jnp.where(inside, lines[1], lines[2])], axis=1
    )[0:1].astype(I32)
    own[0:1, :] = (unknown >> 7).astype(F32)
    own[1:2, :] = (unknown & 127).astype(F32)

    plan_rows(plan, KC, fetch(table, unknown, place[0]))

    def level(k, carry):
        col = 128.0 * plan[KC, pl.ds(k, 1), :] + plan[KC, pl.ds(8 + k, 1), :]
        plan_rows(plan, k, fetch(table, col.astype(I32), place[0]))
        return carry

    lax.fori_loop(0, KC, level, 0)

    pe = prolong(coarse_solve(values, plan, own), n)
    for x in range(CX):
        pe_out[x] = pe[x]

    xa[...], xb[...] = send_planes([(pe, 2)])


def below_above(index, count, a, b):
    even = (index & 1) == 0
    inner = jnp.logical_and(index > 0, index < count - 1)

    def near(i):
        if i is not ...:
            i = slice(CY * i, CY * i + CY)
        return a[i], jnp.where(inner, b[i], 0.0)

    def below(i):
        first, second = near(i)
        return jnp.where(even, second, first)

    def above(i):
        first, second = near(i)
        return jnp.where(even, first, second)

    return below, above


def ghost_rows(field, x):
    return max(0, (4, 3, 3)[field] - max(0, -x, x - CX + 1))


def packed(fields):
    return [(f, x, k) for f in fields for x in range(-3, CX + 3) for k in range(ghost_rows(f, x))]


PACKED = packed((0, 1, 2))


def with_ghosts(own, messages):
    def plane(field, x):
        if 0 <= x < CX:
            return own[field][x]
        below, above, base, depth = messages[field]
        return below(base + depth + x) if x < 0 else above(base + x - CX)

    return plane


def widen(plane, fields, ya, yb):
    even = (places()[1] & 1) == 0
    upper, lower = [], []
    for f in fields:
        for x in range(-3, CX + 3):
            d = ghost_rows(f, x)
            if d:
                here = plane(f, x)
                upper.append(here[CY - d :])
                lower.append(here[:d])
    upper, lower = jnp.concatenate(upper, axis=0), jnp.concatenate(lower, axis=0)
    ya[...] = jnp.where(even, upper, lower)
    yb[...] = jnp.where(even, lower, upper)


def all_ghosts(own, x0a, x0b, x1a, x1b):
    early = below_above(places()[0], 8, x0a.at[TABLE_ROWS:], x0b)
    late = below_above(places()[0], 8, x1a, x1b)
    return with_ghosts(own, ((*early, 0, 3), (*early, 3, 2), (*late, 0, 2)))


def widen_kernel(zs, ic, pe, x0a, x0b, x1a, x1b, ya, yb):
    plane = all_ghosts((zs, ic, pe), x0a, x0b, x1a, x1b)
    even = (places()[1] & 1) == 0
    upper, lower = [], []
    for f in range(3):
        for x in range(-3, CX + 3):
            d = ghost_rows(f, x)
            if d:
                here = plane(f, x)
                upper.append(here[CY - d :])
                lower.append(here[:d])
    upper, lower = jnp.concatenate(upper, axis=0), jnp.concatenate(lower, axis=0)
    ya[...] = jnp.where(even, upper, lower)
    yb[...] = jnp.where(even, lower, upper)


def early_kernel(count, beside, across, zs, ic, pe, c, xa, xb, ya, yb, pay):
    place = places()
    n = count[0]
    below, above = below_above(place[0], 8, xa.at[TABLE_ROWS:], xb)
    near, far = [side(...) for side in below_above(place[1], 16, ya, yb)]
    row = iota((CY, CZ), 0)
    z1 = []
    for x in range(CX):
        mid = zs[x]
        left = zs[x - 1] if x else below(2)
        right = zs[x + 1] if x + 1 < CX else above(0)
        up = jnp.where(row == 0, near[x : x + 1], pltpu.roll(mid, 1, 0))
        down = jnp.where(row == CY - 1, far[x : x + 1], pltpu.roll(mid, CY - 1, 0))
        z1.append(1.2 * mid + 0.8 * ic[x] * couple(left, mid, right, up, down) + pe[x])
    image = []
    zero = jnp.zeros((CY, CZ), F32)
    for x in range(CX):
        mid = z1[x]
        up = jnp.where(row == 0, 0.0, pltpu.roll(mid, 1, 0))
        down = jnp.where(row == CY - 1, 0.0, pltpu.roll(mid, CY - 1, 0))
        left = z1[x - 1] if x else zero
        right = z1[x + 1] if x + 1 < CX else zero
        image.append(c[x] * mid - couple(left, mid, right, up, down))
    sums = restrict(image, n)
    blank = jnp.zeros((CY, LANES), F32)
    lane = iota((1, LANES), 1)
    under, over = across[0:1, 0:1], across[4:5, 0:1]
    down_x = restrict_plane(-8.0 * z1[0], CX - 1, under, blank, (3 * under) >> 2)
    up_x = restrict_plane(-8.0 * z1[CX - 1], 0, over, blank, 0)
    down_x = jnp.where(place[0] > 0, jnp.sum(down_x, axis=0, keepdims=True), 0.0)
    up_x = jnp.where(place[0] < 7, jnp.sum(up_x, axis=0, keepdims=True), 0.0)
    along_x = jnp.where(lane < 64, down_x, pltpu.roll(jnp.broadcast_to(up_x, (8, LANES)), 64, 1)[0:1])
    rims = jnp.concatenate([z[0:1] for z in z1] + [z[CY - 1 : CY] for z in z1], axis=0)
    along_y = rim_restrict(jnp.where(rim_exists(place[1]), -8.0 * rims, 0.0), beside[...])
    repeat4(pay, [sums[:, :LANES], sums[:, LANES:], along_x, along_y])


def add_neighbours(low, high, from_x, from_y, counts):
    lane = iota((DEVICES, LANES), 1)

    def place(window, base, shift, length):
        nonlocal low, high
        relative = lane - base
        moved = lane_take(window, (relative + shift) & 127)
        low = low + jnp.where(jnp.logical_and(relative >= 0, relative < length), moved, 0.0)
        relative = relative + LANES
        high = high + jnp.where(jnp.logical_and(relative >= 0, relative < length), moved, 0.0)

    low = low + jnp.where(lane < 64, pltpu.roll(pltpu.roll(from_x, 16, 0), 64, 1), 0.0)
    place(pltpu.roll(from_x, DEVICES - 16, 0), (3 * counts) >> 2, 0, 64)
    both = jnp.where(lane < 64, pltpu.roll(from_y, DEVICES - 1, 0), pltpu.roll(from_y, 1, 0))
    for g in range(2 * CX):
        cells = ((g & 3) * CY + (CY - 1 if g < CX else 0)) * CZ
        place(both, (cells * counts) >> 13, 16 * g, 9)
    return low, high


def second_solve_kernel(
    count, sums, gathered, order, plan, own, at_row, at_lane, counts, pe_out, pe_face, e_face
):
    n = count[0]
    low, high = add_neighbours(
        sums[pl.ds(0, DEVICES, stride=4), :], sums[pl.ds(1, DEVICES, stride=4), :],
        sums[pl.ds(2, DEVICES, stride=4), :], sums[pl.ds(3, DEVICES, stride=4), :], counts[...],
    )
    diag = gathered[pl.ds(2, DEVICES, stride=4), :]
    inverse = gathered[pl.ds(3, DEVICES, stride=4), :].astype(I32)
    values = assemble(low, high, (at_row[...], at_lane[0:1, :]), inverse, blocks_of(order))
    entries = coarse_solve(0.8 * values / diag, plan, own)
    pe = prolong(entries, n)
    for x in range(CX):
        pe_out[x] = pe[x]
        pe_face[x : x + 1, :] = pe[x][0:1]
        pe_face[CX + x : CX + x + 1, :] = pe[x][CY - 1 : CY]
    lane = iota((8, LANES), 1)
    group = lane >> 4
    cells = ((group & 3) * CY + jnp.where(group < 4, 0, CY - 1)) * CZ
    slot = jnp.minimum(((cells * n) >> 13) + (lane & 15), SLOTS - 1)
    low = jnp.broadcast_to(entries[:, :LANES], (8, LANES))
    high = jnp.broadcast_to(entries[:, LANES:], (8, LANES))
    e_face[...] = jnp.where(slot < LANES, lane_take(low, slot & 127), lane_take(high, slot & 127))


def direction_kernel(
    zs, ic, pe, c, x0a, x0b, x1a, x1b, ya, yb, pe2,
    z1_out, w1_out, p_out, sw_ghost, s_ghost, w_ghost, xa, xb,
):
    place = places()
    middle = all_ghosts((zs, ic, pe), x0a, x0b, x1a, x1b)
    near, far = [side(...) for side in below_above(place[1], 16, ya, yb)]

    def plane(field, x):
        d = ghost_rows(field, x)
        here = middle(field, x)
        if not d:
            blank = jnp.zeros((8, CZ), F32)
            return jnp.concatenate([blank, here, blank], axis=0)
        at = PACKED.index((field, x, 0))
        parts = [near[at : at + d], here, far[at : at + d]]
        if d < 8:
            blank = jnp.zeros((8 - d, CZ), F32)
            parts = [blank] + parts + [blank]
        return jnp.concatenate(parts, axis=0)

    def neighbours(get, x):
        mid = get(x)
        count = mid.shape[0]
        return couple(get(x - 1), mid, get(x + 1), pltpu.roll(mid, 1, 0), pltpu.roll(mid, count - 1, 0))

    z = {x: plane(0, x) for x in range(-3, CX + 3)}
    inv = {x: plane(1, x) for x in range(-2, CX + 2)}
    first = {}
    for x in range(-2, CX + 2):
        first[x] = 1.2 * z[x] + 0.8 * inv[x] * neighbours(z.get, x) + plane(2, x)
    zw = {}
    for x in range(-1, CX + 1):
        beside = neighbours(first.get, x)
        zw[x] = 0.8 * (first[x] - inv[x] * beside)
        if 0 <= x < CX:
            z1_out[x] = first[x][8:16]
            w1_out[x] = c[x] * first[x][8:16] - beside[8:16]
    p = []
    for x in range(CX):
        smooth = 1.2 * zw[x] + 0.8 * inv[x] * neighbours(zw.get, x)
        p.append(smooth[8:16] + pe2[x])
        p_out[x] = p[x]
        for at, row in ((x, 7), (CX + x, 16)):
            iv = inv[x][row : row + 1]
            scale = jnp.where(iv > 0.0, 1.25 / jnp.where(iv > 0.0, iv, 1.0), 0.0)
            sw_ghost[at : at + 1, :] = smooth[row : row + 1]
            s_ghost[at : at + 1, :] = z[x][row : row + 1] * scale
            w_ghost[at : at + 1, :] = zw[x][row : row + 1] * scale
    even = (place[0] & 1) == 0
    xa[...] = jnp.where(even, p[CX - 1], p[0])
    xb[...] = jnp.where(even, p[0], p[CX - 1])


def products_kernel(s, w1, p, c, xa, xb, sw_ghost, s_ghost, w_ghost, pe_face, e_face, beside, pay):
    place = places()
    below, above = [side(...) for side in below_above(place[0], 8, xa, xb)]
    sums = [jnp.zeros((CY, CZ), F32) for _ in range(6)]
    row = iota((CY, CZ), 0)
    rims = [None] * (2 * CX)
    for x in range(CX):
        mid = p[x]
        left = p[x - 1] if x else below
        right = p[x + 1] if x + 1 < CX else above
        up = jnp.where(row == 0, sw_ghost[x : x + 1, :], pltpu.roll(mid, 1, 0))
        down = jnp.where(row == CY - 1, sw_ghost[CX + x : CX + x + 1, :], pltpu.roll(mid, CY - 1, 0))
        q = c[x] * mid - couple(left, mid, right, up, down)
        rims[x], rims[CX + x] = q[0:1], q[CY - 1 : CY]
        a, b = s[x], w1[x]
        for k, term in enumerate((a * a, a * b, a * q, b * b, b * q, q * q)):
            sums[k] = sums[k] + term
    exists = rim_exists(place[1])
    face = pe_face[...]
    sums[2] = sums[2] - 8.0 * face * s_ghost[...]
    sums[4] = sums[4] - 8.0 * face * w_ghost[...]
    sums[5] = sums[5] + jnp.where(exists, 64.0 * face * face, 0.0)
    rim = jnp.where(exists, jnp.concatenate(rims, axis=0), 0.0)
    lane = iota((8, LANES), 1)
    top = jnp.broadcast_to(rim_restrict(rim, beside[...]), (8, LANES))
    for k in range(6):
        top = top + jnp.where(lane == 9 + k, jnp.sum(sums[k], keepdims=True), 0.0)
    tile = jnp.where((iota((8, LANES), 0) & 1) == 0, top, e_face[...])
    for i in range(DEVICES // 4):
        pay[pl.ds(8 * i, 8), :] = tile


def update_kernel(parts, z1, p, s_old, rate, mobile, immobile):
    top = parts[pl.ds(0, DEVICES, stride=2), :]
    face = pltpu.roll(parts[pl.ds(1, DEVICES, stride=2), :], LANES // 2, 1)
    lane = iota((DEVICES, LANES), 1)
    other = jnp.where(lane < LANES // 2, pltpu.roll(face, 1, 0), pltpu.roll(face, DEVICES - 1, 0))
    cross = jnp.sum(jnp.where((lane & 15) < 9, top * other, 0.0), keepdims=True)
    total = jnp.sum(top, axis=0, keepdims=True)
    ss, sw, sq, ww, wq, qq = [total[:, 9 + k : 10 + k] for k in range(6)]
    qq = qq - 16.0 * cross
    factor = wq / ww
    y2 = (sq - factor * sw) / (qq - factor * wq)
    y1 = (sw - wq * y2) / ww
    for x in range(CX):
        new = y1 * z1[x] + y2 * p[x]
        mobile[x] = new
        for k in range(RATES):
            r = rate[k, x]
            immobile[k, x] = (s_old[k, x] + r * new) / (1.0 + r)


def call(kernel, ins, outs, scratch=(), flops=10_000, vmem=48 << 20):
    shapes = [jax.ShapeDtypeStruct(shape, dtype) for shape, dtype in outs]
    return pl.pallas_call(
        kernel,
        out_shape=shapes,
        in_specs=ins,
        out_specs=[VM] * len(shapes),
        scratch_shapes=list(scratch),
        cost_estimate=pl.CostEstimate(flops=flops, bytes_accessed=100_000, transcendentals=0),
        compiler_params=pltpu.CompilerParams(vmem_limit_bytes=vmem),
    )


FIELD = ((CX, CY, CZ), F32)
SOURCE_VMEM = 63 << 20


def swap_pairs(axis):
    n, m = lax.axis_size("coarse"), lax.axis_size("fine")
    inside, between = [], []
    for c in range(n):
        for f in range(m):
            me = c * m + f
            at, count, step = (c, n, m) if axis == "coarse" else (f, m, 1)
            inside.append((me, me + ((at ^ 1) - at) * step))
            if 0 < at < count - 1:
                between.append((me, me + (((at - 1) ^ 1) + 1 - at) * step))
            elif axis == "fine":
                between.append((me, (c ^ 1) * m + f))
            else:
                between.append((me, (n - 1 - c) * m + f))
    return inside, between


def swap_between(b, axis):
    return lax.ppermute(b, BOTH, swap_pairs(axis)[1])


def trade(a, b, axis):
    b = swap_between(b, axis)
    return lax.ppermute(a, BOTH, swap_pairs(axis)[0]), b


def everyone(pay, rows):
    moved = lax.all_to_all(pay.reshape(DEVICES, rows, LANES), BOTH, 0, 0)
    return moved.reshape(DEVICES * rows, LANES)


def local(
    c_old, s_old, rate_time, capacity, agg_count, coarse_order, coarse_cols, coarse_off, coarse_diag
):
    order = coarse_order.reshape(LANES, LANES)
    c, ic, s, zs, tab, both, x0b, y0a, y0b = call(
        source_kernel, [SM, VM, HB, HB] + [VM] * 3,
        [
            FIELD, FIELD, FIELD, FIELD, ((TABLE_ROWS, 256), F32), ((TABLE_ROWS + 40, 256), F32),
            ((40, CZ), F32), ((CY, CZ), F32), ((CY, CZ), F32),
        ],
        scratch=[
            pltpu.VMEM((RATES, CX, CY, CZ), F32),
            pltpu.VMEM((RATES, CX, CY, CZ), F32),
            pltpu.SemaphoreType.DMA((2, CX)),
        ],
        vmem=SOURCE_VMEM,
    )(
        capacity, c_old, s_old, rate_time, coarse_diag.reshape(1, SHARD_ROWS), coarse_cols, coarse_off,
    )
    other_core = [(i, i ^ 1) for i in range(8)]
    both = lax.ppermute(both, "coarse", other_core)
    tabs = [tab, both]
    for hop in (2, 4, 6):
        shard = lax.ppermute(tab, "coarse", [(i, i ^ hop) for i in range(8)])
        tabs += [shard, lax.ppermute(shard, "coarse", other_core)]
    x0b = swap_between(x0b, "coarse")
    y0a, y0b = trade(y0a, y0b, "fine")
    (pay,) = call(sums_kernel, [SM] + [VM] * 3, [((4 * DEVICES, LANES), F32)])(
        agg_count, s, coarse_diag.reshape(16, LANES), order
    )
    gathered = everyone(pay, 4)

    pe, plan, own, beside, across, at_row, at_lane, counts, x1a, x1b = call(
        first_kernel, [SM] + [VM] * 10,
        [
            FIELD, ((KC + 1, 24, SLOTS), F32), ((8, SLOTS), F32), ((8, LANES), I32), ((8, LANES), I32),
            ((LANES, LANES), I32), ((8, LANES), I32), ((LANES, LANES), I32),
            ((2 * CY, CZ), F32), ((2 * CY, CZ), F32),
        ],
        scratch=[pltpu.VMEM((SHARDS * 32, SHARD_ROWS), BF16)],
    )(agg_count, gathered, order, *tabs)
    x1a, x1b = trade(x1a, x1b, "coarse")
    (pay,) = call(early_kernel, [SM] + [VM] * 10, [((4 * DEVICES, LANES), F32)])(
        agg_count, beside, across, zs, ic, pe, c, both, x0b, y0a, y0b
    )
    sums = everyone(pay, 4)
    ya, yb = call(widen_kernel, [VM] * 7, [((len(PACKED), CZ), F32)] * 2)(zs, ic, pe, both, x0b, x1a, x1b)
    ya, yb = trade(ya, yb, "fine")

    pe2, pe_face, e_face = call(
        second_solve_kernel, [SM] + [VM] * 8, [FIELD, ((CY, CZ), F32), ((8, LANES), F32)], flops=100_000_000
    )(agg_count, sums, gathered, order, plan, own, at_row, at_lane, counts)
    z1, w1, p, sw_ghost, s_ghost, w_ghost, xa, xb = call(
        direction_kernel, [VM] * 11, [FIELD, FIELD, FIELD] + [((CY, CZ), F32)] * 5,
    )(zs, ic, pe, c, both, x0b, x1a, x1b, ya, yb, pe2)
    xa, xb = trade(xa, xb, "coarse")
    (pay,) = call(
        products_kernel, [VM] * 12, [((2 * DEVICES, LANES), F32)]
    )(s, w1, p, c, xa, xb, sw_ghost, s_ghost, w_ghost, pe_face, e_face, beside)
    parts = everyone(pay, 2)
    mobile, immobile = call(
        update_kernel, [VM] * 5, [FIELD, ((RATES, CX, CY, CZ), F32)]
    )(parts, z1, p, s_old, rate_time)
    return mobile, immobile


def solution(mesh):
    return jax.shard_map(
        local,
        mesh=mesh,
        in_specs=(
            P("coarse", "fine", None),
            P(None, "coarse", "fine", None),
            P(None, "coarse", "fine", None),
            P(),
            P(("coarse", "fine")),
            P(),
            P(None, "coarse"),
            P(None, "coarse"),
            P("coarse"),
        ),
        out_specs=(P("coarse", "fine", None), P(None, "coarse", "fine", None)),
        check_vma=False,
    )
```

```python
import jax
import jax.numpy as jnp
from jax import lax
from jax.experimental import pallas as pl
from jax.experimental.pallas import tpu as pltpu
from jax.sharding import PartitionSpec as P

BOTH = ("coarse", "fine")
CX, CY, CZ = 4, 8, 256
RATES = 16
KC = 8
DEVICES = 128
LANES = 128
SLOTS = 256
SHARDS = 8
SHARD_ROWS = 2048
FLOW = 50.0
TABLE_ROWS = 128
UNUSED = 1e30
F32, BF16, I32 = jnp.float32, jnp.bfloat16, jnp.int32
VM = pl.BlockSpec(memory_space=pltpu.VMEM)
SM = pl.BlockSpec(memory_space=pltpu.SMEM)
HB = pl.BlockSpec(memory_space=pltpu.HBM)


def places():
    return lax.axis_index("coarse").astype(I32), lax.axis_index("fine").astype(I32)


def iota(shape, dim):
    return lax.broadcasted_iota(I32, shape, dim)


def lane_take(table, index):
    return jnp.take_along_axis(table, index, axis=1, mode="promise_in_bounds")


def nt(left, right):
    return lax.dot_general(left, right, (((1,), (1,)), ((), ())), preferred_element_type=F32)


def nn(left, right):
    return jnp.dot(left, right, preferred_element_type=F32)


def split2(values):
    high = values.astype(BF16)
    return high, (values - high.astype(F32)).astype(BF16)


def slots_of(plane, half, count):
    row = (plane * CY + iota((CY, LANES), 0)) * 2 + half
    return ((row * LANES + iota((CY, LANES), 1)) * count) >> 13


def restrict_plane(values, plane, count, total, base):
    slot = iota(total.shape, 1) + base
    for half in range(2):
        part_of = values[:, half * LANES : (half + 1) * LANES]
        row = (plane * CY + iota((CY, 1), 0)) * 2 + half
        first = (row * count) >> 6
        member = slots_of(plane, half, count) - first
        relative = slot - first
        for k in range(5):
            part = jnp.sum(jnp.where(member == k, part_of, 0.0), axis=1, keepdims=True)
            total = total + jnp.where(relative == k, part, 0.0)
    return total


def restrict(cells, count):
    total = jnp.zeros((CY, SLOTS), F32)
    for plane in range(CX):
        total = restrict_plane(cells[plane], plane, count, total, 0)
    return jnp.sum(total, axis=0, keepdims=True)


def rim_restrict(rim, count):
    n = jnp.concatenate([count, count], axis=1)
    row = iota((CY, CZ), 0)
    cells = ((row & 3) * CY + jnp.where(row < 4, CY - 1, 0)) * CZ
    member = (((cells + iota((CY, CZ), 1)) * n) >> 13) - ((cells * n) >> 13)
    lane = iota((8, LANES), 1)
    start = iota((8, LANES), 0) * 16
    spread = jnp.zeros((8, LANES), F32)
    for k in range(9):
        part = jnp.sum(jnp.where(member == k, rim, 0.0), axis=1, keepdims=True)
        spread = spread + jnp.where(lane == start + k, part, 0.0)
    return jnp.sum(spread, axis=0, keepdims=True)


def rim_exists(index):
    return jnp.where(iota((CY, CZ), 0) < 4, index, 15 - index) > 0


def prolong(entries, count):
    low = jnp.broadcast_to(entries[:, :LANES], (CY, LANES))
    high = jnp.broadcast_to(entries[:, LANES:], (CY, LANES))
    planes = []
    for plane in range(CX):
        halves = []
        for half in range(2):
            slot = slots_of(plane, half, count)
            place = slot & 127
            halves.append(jnp.where(slot < LANES, lane_take(low, place), lane_take(high, place)))
        planes.append(jnp.concatenate(halves, axis=1))
    return planes


def couple(left, mid, right, up, down):
    length = mid.shape[1]
    lane = iota(mid.shape, 1)
    behind = jnp.where(lane == 0, 0.0, pltpu.roll(mid, 1, 1))
    ahead = jnp.where(lane == length - 1, 0.0, pltpu.roll(mid, length - 1, 1))
    return 8.0 * (left + right + up + down + ahead) + 10.0 * behind


def source_kernel(
    cap, c_old, s_old_hbm, rate_hbm, diag, cols, off,
    c_out, ic_out, s_out, zs_out, tab, both, xb, ya, yb, s_old, rate, sems,
):
    copies = []
    for x in range(CX):
        pair = (
            pltpu.make_async_copy(rate_hbm.at[:, x], rate.at[:, x], sems.at[0, x]),
            pltpu.make_async_copy(s_old_hbm.at[:, x], s_old.at[:, x], sems.at[1, x]),
        )
        for copy in pair:
            copy.start()
        copies.append(pair)
    for j in range(SHARD_ROWS // 256):
        at = slice(256 * j, 256 * j + 256)
        part = jnp.concatenate([cols[:, at].astype(F32), off[:, at] * (0.8 / diag[:, at])], axis=0)
        tab[16 * j : 16 * j + 16, :] = part
        both[16 * j : 16 * j + 16, :] = part
    smooth, inverse = [], []
    for x in range(CX):
        for copy in copies[x]:
            copy.wait()
        mass = jnp.zeros((CY, CZ), F32)
        extra = jnp.zeros((CY, CZ), F32)
        for k in range(RATES):
            r = rate[k, x]
            weighted = cap[k] * (r / (1.0 + r))
            mass = mass + weighted
            extra = extra + weighted * s_old[k, x]
        centre = (1.0 + mass) + FLOW
        source = c_old[x] + extra
        inv = 1.0 / centre
        c_out[x] = centre
        ic_out[x] = inv
        s_out[x] = source
        zs_out[x] = 0.8 * source * inv
        smooth.append(0.8 * source * inv)
        inverse.append(inv)
    xa, xb[...] = send_planes([(smooth, 3), (inverse, 2)])
    both[TABLE_ROWS:, :] = xa
    ya[...], yb[...] = send_rims(smooth)


def send_planes(fields):
    even = (places()[0] & 1) == 0
    upper = jnp.concatenate([p for planes, depth in fields for p in planes[CX - depth :]], axis=0)
    lower = jnp.concatenate([p for planes, depth in fields for p in planes[:depth]], axis=0)
    return jnp.where(even, upper, lower), jnp.where(even, lower, upper)


def send_rims(planes):
    even = (places()[1] & 1) == 0
    upper = jnp.concatenate([p[CY - 1 : CY] for p in planes] * 2, axis=0)
    lower = jnp.concatenate([p[0:1] for p in planes] * 2, axis=0)
    return jnp.where(even, upper, lower), jnp.where(even, lower, upper)


def sums_kernel(count, s, diag, order, pay):
    place = places()
    n = count[0]
    mine = (order[0:1, :] >> 7) == place[0] * 16 + place[1]
    low = jnp.sum(jnp.where(mine, (order[...] & 127).astype(F32), 0.0), axis=1, keepdims=True)
    spot = iota((LANES, LANES), 1).astype(F32) == low
    inverse = jnp.sum(jnp.where(spot, iota((LANES, LANES), 0).astype(F32), 0.0), axis=0, keepdims=True)
    sums = jnp.where(iota((1, SLOTS), 1) < n, restrict([s[x] for x in range(CX)], n), UNUSED)
    repeat4(pay, [sums[:, :LANES], sums[:, LANES:], diag[pl.ds(place[1], 1), :], inverse])


def repeat4(pay, rows):
    kind = iota((8, LANES), 0) & 3
    tile = jnp.broadcast_to(rows[3], (8, LANES))
    for k in range(3):
        tile = jnp.where(kind == k, rows[k], tile)
    for i in range(DEVICES // 2):
        pay[pl.ds(8 * i, 8), :] = tile


def read_sums(gathered):
    low = gathered[pl.ds(0, DEVICES, stride=4), :]
    high = gathered[pl.ds(1, DEVICES, stride=4), :]
    diag = gathered[pl.ds(2, DEVICES, stride=4), :]
    inverse = gathered[pl.ds(3, DEVICES, stride=4), :].astype(I32)
    used = jnp.where(low < 0.5 * UNUSED, 1.0, 0.0) + jnp.where(high < 0.5 * UNUSED, 1.0, 0.0)
    return low, high, diag, inverse, jnp.sum(used, axis=1, keepdims=True)


def offsets_of(counts):
    row, lane = iota((LANES, LANES), 0), iota((LANES, LANES), 1)
    by_lane = jnp.sum(jnp.where(row < lane, counts, 0.0), axis=0, keepdims=True)
    across = jnp.sum(jnp.where(row == lane, counts, 0.0), axis=0, keepdims=True)
    by_row = jnp.sum(jnp.where(lane < row, across, 0.0), axis=1, keepdims=True)
    return jnp.broadcast_to(by_row, (LANES, LANES)).astype(I32), by_lane.astype(I32)


def blocks_of(order):
    return (iota((LANES, LANES), 0) == (order[0:1, :] >> 7)).astype(F32).astype(BF16)


def assemble(low, high, offsets, inverse, blocks):
    by_row, by_lane = offsets
    lane = iota((LANES, LANES), 1)
    shift = by_row & 127
    place = (lane - shift) & 127
    low = lane_take(low, place)
    high = lane_take(high, place)
    kept = lane >= shift
    rows = (jnp.where(kept, low, 0.0), jnp.where(kept, high, low), jnp.where(kept, 0.0, high))
    start = by_lane >> 7
    spots = [(iota((LANES, LANES), 0) == start + j).astype(F32).astype(BF16) for j in range(3)]
    parts = [jnp.concatenate(split2(r), axis=1) for r in rows]
    table = nn(jnp.concatenate(spots, axis=1), jnp.concatenate(parts, axis=0))
    by_block = nt(blocks, jnp.concatenate([table[:, :LANES], table[:, LANES:]], axis=0).astype(BF16))
    return lane_take(by_block[:, :LANES] + by_block[:, LANES:], inverse)


def one_hot(row16, index):
    return jnp.where(row16 == index.astype(BF16), jnp.ones(row16.shape, BF16), jnp.zeros(row16.shape, BF16))


def fetch(table, unknown, coarse):
    inner = unknown & (SHARD_ROWS - 1)
    shard = (unknown >> 11) ^ coarse
    row16 = iota((256, SLOTS), 0).astype(F32).astype(BF16)
    found = jnp.zeros((SHARDS * 32, SLOTS), F32)
    for chunk in range(SHARD_ROWS // 256):
        spot = one_hot(row16, (inner - chunk * 256).astype(F32))
        found = found + nn(table[:, chunk * 256 : (chunk + 1) * 256], spot)
    found = found.reshape(SHARDS, 32, SLOTS)
    picked = found[0]
    for g in range(1, SHARDS):
        picked = jnp.where(shard == g, found[g], picked)
    return picked[0:8], picked[8:16], picked[16:24] + picked[24:32]


def gatherer(values):
    high, low = split2(values.T)
    table = jnp.concatenate([high, low], axis=1)
    row = iota((LANES, SLOTS), 0).astype(F32)
    row16 = row.astype(BF16)

    def gather(block, inner):
        spot = one_hot(row16, block)
        found = nn(table, jnp.concatenate([spot, spot], axis=0))
        kept = jnp.zeros((8, SLOTS), F32)
        for b in range(0, LANES, 8):
            kept = jnp.where(row[b : b + 8] == inner, found[b : b + 8], kept)
        return kept

    return gather


def solve_entry(gather, first, parts):
    total = -1.4 * gather(first[0], first[1])
    for j in range(KC):
        total = total + parts[2][j : j + 1] * gather(parts[0][j : j + 1], parts[1][j : j + 1])
    return first[2] * total


def coarse_solve(values, plan, own):
    gather = gatherer(values)

    def column(k, total):
        first = [plan[KC, pl.ds(8 * i + k, 1), :] for i in range(3)]
        return total + solve_entry(gather, first, [plan[k, 8 * i : 8 * i + 8, :] for i in range(3)])

    total = lax.fori_loop(0, KC, column, 1.24 * gather(own[0:1, :], own[1:2, :]), unroll=SECOND_UNROLL)
    return jnp.sum(total, axis=0, keepdims=True)


def plan_rows(ref, k, parts):
    ref[k, 0:8, :] = parts[0]
    ref[k, 8:16, :] = parts[1]
    ref[k, 16:24, :] = parts[2]


def first_kernel(
    count, gathered, order, tab0, tab1, tab2, tab3, tab4, tab5, tab6, tab7,
    pe_out, plan, own, beside, across, at_row, at_lane, counts_out, xa, xb, table,
):
    place = places()
    n = count[0]
    me = place[0] * 16 + place[1]
    low, high, diag, inverse, counts = read_sums(gathered)
    offsets = offsets_of(counts)
    at_row[...] = offsets[0]
    at_lane[...] = jnp.broadcast_to(offsets[1], (8, LANES))
    sums = assemble(
        jnp.where(low < 0.5 * UNUSED, low, 0.0), jnp.where(high < 0.5 * UNUSED, high, 0.0),
        offsets, inverse, blocks_of(order),
    )
    values = 0.8 * sums / diag
    counts = jnp.broadcast_to(counts, (LANES, LANES))
    counts_out[...] = counts.astype(I32)
    row = iota((LANES, LANES), 0)
    before = iota((8, LANES), 0) < 4
    for out, step in ((beside, 1), (across, 16)):
        sides = [jnp.sum(jnp.where(row == me + d, counts, 0.0), axis=0, keepdims=True) for d in (-step, step)]
        out[...] = jnp.where(before, sides[0], sides[1]).astype(I32)

    tabs = (tab0, tab1, tab2, tab3, tab4, tab5, tab6, tab7)
    for g in range(SHARDS):
        for j in range(SHARD_ROWS // 256):
            at = slice(256 * j, 256 * j + 256)
            cols = tabs[g][16 * j : 16 * j + 8, :]
            big = jnp.floor(cols * (1.0 / 128.0))
            pair = jnp.concatenate([big, cols - 128.0 * big], axis=0)
            table[32 * g : 32 * g + 16, at] = pair.astype(BF16)
            off = tabs[g][16 * j + 8 : 16 * j + 16, :]
            big = off.astype(BF16).astype(F32)
            table[32 * g + 16 : 32 * g + 32, at] = jnp.concatenate([big, off - big], axis=0).astype(BF16)

    mine = jnp.sum(jnp.where(row == me, offsets[0].astype(F32), 0.0), axis=0, keepdims=True).astype(I32)
    numbers = order[...].astype(F32)
    start = mine >> 7
    lines = []
    spread = (iota((8, LANES), 1) + mine) & 127
    for j in range(3):
        line = jnp.sum(jnp.where(row == start + j, numbers, 0.0), axis=0, keepdims=True)
        lines.append(lane_take(jnp.broadcast_to(line, (8, LANES)), spread))
    inside = iota((8, LANES), 1) + (mine & 127) < LANES
    unknown = jnp.concatenate(
        [jnp.where(inside, lines[0], lines[1]), jnp.where(inside, lines[1], lines[2])], axis=1
    )[0:1].astype(I32)
    own[0:1, :] = (unknown >> 7).astype(F32)
    own[1:2, :] = (unknown & 127).astype(F32)
    plan_rows(plan, KC, fetch(table, unknown, place[0]))

    def column(k, carry):
        col = 128.0 * plan[KC, pl.ds(k, 1), :] + plan[KC, pl.ds(8 + k, 1), :]
        plan_rows(plan, k, fetch(table, col.astype(I32), place[0]))
        return carry

    lax.fori_loop(0, KC, column, 0, unroll=FIRST_UNROLL)
    pe = prolong(coarse_solve(values, plan, own), n)
    for x in range(CX):
        pe_out[x] = pe[x]

    xa[...], xb[...] = send_planes([(pe, 2)])


def below_above(index, count, a, b):
    even = (index & 1) == 0
    inner = jnp.logical_and(index > 0, index < count - 1)

    def near(i):
        if i is not ...:
            i = slice(CY * i, CY * i + CY)
        return a[i], jnp.where(inner, b[i], 0.0)

    def below(i):
        first, second = near(i)
        return jnp.where(even, second, first)

    def above(i):
        first, second = near(i)
        return jnp.where(even, first, second)

    return below, above


def ghost_rows(field, x):
    return max(0, (4, 3, 3)[field] - max(0, -x, x - CX + 1))


def packed(fields):
    return [(f, x, k) for f in fields for x in range(-3, CX + 3) for k in range(ghost_rows(f, x))]


PACKED = packed((0, 1, 2))


def with_ghosts(own, messages):
    def plane(field, x):
        if 0 <= x < CX:
            return own[field][x]
        below, above, base, depth = messages[field]
        return below(base + depth + x) if x < 0 else above(base + x - CX)

    return plane


def widen(plane, fields, ya, yb):
    even = (places()[1] & 1) == 0
    upper, lower = [], []
    for f in fields:
        for x in range(-3, CX + 3):
            d = ghost_rows(f, x)
            if d:
                here = plane(f, x)
                upper.append(here[CY - d :])
                lower.append(here[:d])
    upper, lower = jnp.concatenate(upper, axis=0), jnp.concatenate(lower, axis=0)
    ya[...] = jnp.where(even, upper, lower)
    yb[...] = jnp.where(even, lower, upper)


def all_ghosts(own, x0a, x0b, x1a, x1b):
    early = below_above(places()[0], 8, x0a.at[TABLE_ROWS:], x0b)
    late = below_above(places()[0], 8, x1a, x1b)
    return with_ghosts(own, ((*early, 0, 3), (*early, 3, 2), (*late, 0, 2)))


def widen_kernel(zs, ic, pe, x0a, x0b, x1a, x1b, ya, yb):
    plane = all_ghosts((zs, ic, pe), x0a, x0b, x1a, x1b)
    even = (places()[1] & 1) == 0
    upper, lower = [], []
    for f in range(3):
        for x in range(-3, CX + 3):
            d = ghost_rows(f, x)
            if d:
                here = plane(f, x)
                upper.append(here[CY - d :])
                lower.append(here[:d])
    upper, lower = jnp.concatenate(upper, axis=0), jnp.concatenate(lower, axis=0)
    ya[...] = jnp.where(even, upper, lower)
    yb[...] = jnp.where(even, lower, upper)


def early_kernel(count, beside, across, zs, ic, pe, c, xa, xb, ya, yb, pay):
    place = places()
    n = count[0]
    below, above = below_above(place[0], 8, xa.at[TABLE_ROWS:], xb)
    near, far = [side(...) for side in below_above(place[1], 16, ya, yb)]
    row = iota((CY, CZ), 0)
    z1 = []
    for x in range(CX):
        mid = zs[x]
        left = zs[x - 1] if x else below(2)
        right = zs[x + 1] if x + 1 < CX else above(0)
        up = jnp.where(row == 0, near[x : x + 1], pltpu.roll(mid, 1, 0))
        down = jnp.where(row == CY - 1, far[x : x + 1], pltpu.roll(mid, CY - 1, 0))
        z1.append(1.2 * mid + 0.8 * ic[x] * couple(left, mid, right, up, down) + pe[x])
    image = []
    zero = jnp.zeros((CY, CZ), F32)
    for x in range(CX):
        mid = z1[x]
        up = jnp.where(row == 0, 0.0, pltpu.roll(mid, 1, 0))
        down = jnp.where(row == CY - 1, 0.0, pltpu.roll(mid, CY - 1, 0))
        left = z1[x - 1] if x else zero
        right = z1[x + 1] if x + 1 < CX else zero
        image.append(c[x] * mid - couple(left, mid, right, up, down))
    sums = restrict(image, n)
    blank = jnp.zeros((CY, LANES), F32)
    lane = iota((1, LANES), 1)
    under, over = across[0:1, 0:1], across[4:5, 0:1]
    down_x = restrict_plane(-8.0 * z1[0], CX - 1, under, blank, (3 * under) >> 2)
    up_x = restrict_plane(-8.0 * z1[CX - 1], 0, over, blank, 0)
    down_x = jnp.where(place[0] > 0, jnp.sum(down_x, axis=0, keepdims=True), 0.0)
    up_x = jnp.where(place[0] < 7, jnp.sum(up_x, axis=0, keepdims=True), 0.0)
    along_x = jnp.where(lane < 64, down_x, pltpu.roll(jnp.broadcast_to(up_x, (8, LANES)), 64, 1)[0:1])
    rims = jnp.concatenate([z[0:1] for z in z1] + [z[CY - 1 : CY] for z in z1], axis=0)
    along_y = rim_restrict(jnp.where(rim_exists(place[1]), -8.0 * rims, 0.0), beside[...])
    repeat4(pay, [sums[:, :LANES], sums[:, LANES:], along_x, along_y])


def add_neighbours(low, high, from_x, from_y, counts):
    lane = iota((DEVICES, LANES), 1)

    def place(window, base, shift, length):
        nonlocal low, high
        relative = lane - base
        moved = lane_take(window, (relative + shift) & 127)
        low = low + jnp.where(jnp.logical_and(relative >= 0, relative < length), moved, 0.0)
        relative = relative + LANES
        high = high + jnp.where(jnp.logical_and(relative >= 0, relative < length), moved, 0.0)

    low = low + jnp.where(lane < 64, pltpu.roll(pltpu.roll(from_x, 16, 0), 64, 1), 0.0)
    place(pltpu.roll(from_x, DEVICES - 16, 0), (3 * counts) >> 2, 0, 64)
    both = jnp.where(lane < 64, pltpu.roll(from_y, DEVICES - 1, 0), pltpu.roll(from_y, 1, 0))
    for g in range(2 * CX):
        cells = ((g & 3) * CY + (CY - 1 if g < CX else 0)) * CZ
        place(both, (cells * counts) >> 13, 16 * g, 9)
    return low, high


def second_solve_kernel(
    count, sums, gathered, order, plan, own, at_row, at_lane, counts, pe_out, pe_face, e_face
):
    n = count[0]
    low, high = add_neighbours(
        sums[pl.ds(0, DEVICES, stride=4), :], sums[pl.ds(1, DEVICES, stride=4), :],
        sums[pl.ds(2, DEVICES, stride=4), :], sums[pl.ds(3, DEVICES, stride=4), :], counts[...],
    )
    diag = gathered[pl.ds(2, DEVICES, stride=4), :]
    inverse = gathered[pl.ds(3, DEVICES, stride=4), :].astype(I32)
    values = assemble(low, high, (at_row[...], at_lane[0:1, :]), inverse, blocks_of(order))
    entries = coarse_solve(0.8 * values / diag, plan, own)
    pe = prolong(entries, n)
    for x in range(CX):
        pe_out[x] = pe[x]
        pe_face[x : x + 1, :] = pe[x][0:1]
        pe_face[CX + x : CX + x + 1, :] = pe[x][CY - 1 : CY]
    lane = iota((8, LANES), 1)
    group = lane >> 4
    cells = ((group & 3) * CY + jnp.where(group < 4, 0, CY - 1)) * CZ
    slot = jnp.minimum(((cells * n) >> 13) + (lane & 15), SLOTS - 1)
    low = jnp.broadcast_to(entries[:, :LANES], (8, LANES))
    high = jnp.broadcast_to(entries[:, LANES:], (8, LANES))
    e_face[...] = jnp.where(slot < LANES, lane_take(low, slot & 127), lane_take(high, slot & 127))


def direction_kernel(
    zs, ic, pe, c, x0a, x0b, x1a, x1b, ya, yb, pe2,
    z1_out, w1_out, p_out, sw_ghost, s_ghost, w_ghost, xa, xb,
):
    place = places()
    middle = all_ghosts((zs, ic, pe), x0a, x0b, x1a, x1b)
    near, far = [side(...) for side in below_above(place[1], 16, ya, yb)]

    def plane(field, x):
        d = ghost_rows(field, x)
        here = middle(field, x)
        if not d:
            blank = jnp.zeros((8, CZ), F32)
            return jnp.concatenate([blank, here, blank], axis=0)
        at = PACKED.index((field, x, 0))
        parts = [near[at : at + d], here, far[at : at + d]]
        if d < 8:
            blank = jnp.zeros((8 - d, CZ), F32)
            parts = [blank] + parts + [blank]
        return jnp.concatenate(parts, axis=0)

    def neighbours(get, x):
        mid = get(x)
        count = mid.shape[0]
        return couple(get(x - 1), mid, get(x + 1), pltpu.roll(mid, 1, 0), pltpu.roll(mid, count - 1, 0))

    z = {x: plane(0, x) for x in range(-3, CX + 3)}
    inv = {x: plane(1, x) for x in range(-2, CX + 2)}
    first = {}
    for x in range(-2, CX + 2):
        first[x] = 1.2 * z[x] + 0.8 * inv[x] * neighbours(z.get, x) + plane(2, x)
    zw = {}
    for x in range(-1, CX + 1):
        beside = neighbours(first.get, x)
        zw[x] = 0.8 * (first[x] - inv[x] * beside)
        if 0 <= x < CX:
            z1_out[x] = first[x][8:16]
            w1_out[x] = c[x] * first[x][8:16] - beside[8:16]
    p = []
    for x in range(CX):
        smooth = 1.2 * zw[x] + 0.8 * inv[x] * neighbours(zw.get, x)
        p.append(smooth[8:16] + pe2[x])
        p_out[x] = p[x]
        for at, row in ((x, 7), (CX + x, 16)):
            iv = inv[x][row : row + 1]
            scale = jnp.where(iv > 0.0, 1.25 / jnp.where(iv > 0.0, iv, 1.0), 0.0)
            sw_ghost[at : at + 1, :] = smooth[row : row + 1]
            s_ghost[at : at + 1, :] = z[x][row : row + 1] * scale
            w_ghost[at : at + 1, :] = zw[x][row : row + 1] * scale
    even = (place[0] & 1) == 0
    xa[...] = jnp.where(even, p[CX - 1], p[0])
    xb[...] = jnp.where(even, p[0], p[CX - 1])


def products_kernel(s, w1, p, c, xa, xb, sw_ghost, s_ghost, w_ghost, pe_face, e_face, beside, pay):
    place = places()
    below, above = [side(...) for side in below_above(place[0], 8, xa, xb)]
    sums = [jnp.zeros((CY, CZ), F32) for _ in range(6)]
    row = iota((CY, CZ), 0)
    rims = [None] * (2 * CX)
    for x in range(CX):
        mid = p[x]
        left = p[x - 1] if x else below
        right = p[x + 1] if x + 1 < CX else above
        up = jnp.where(row == 0, sw_ghost[x : x + 1, :], pltpu.roll(mid, 1, 0))
        down = jnp.where(row == CY - 1, sw_ghost[CX + x : CX + x + 1, :], pltpu.roll(mid, CY - 1, 0))
        q = c[x] * mid - couple(left, mid, right, up, down)
        rims[x], rims[CX + x] = q[0:1], q[CY - 1 : CY]
        a, b = s[x], w1[x]
        for k, term in enumerate((a * a, a * b, a * q, b * b, b * q, q * q)):
            sums[k] = sums[k] + term
    exists = rim_exists(place[1])
    face = pe_face[...]
    sums[2] = sums[2] - 8.0 * face * s_ghost[...]
    sums[4] = sums[4] - 8.0 * face * w_ghost[...]
    sums[5] = sums[5] + jnp.where(exists, 64.0 * face * face, 0.0)
    rim = jnp.where(exists, jnp.concatenate(rims, axis=0), 0.0)
    lane = iota((8, LANES), 1)
    top = jnp.broadcast_to(rim_restrict(rim, beside[...]), (8, LANES))
    for k in range(6):
        top = top + jnp.where(lane == 9 + k, jnp.sum(sums[k], keepdims=True), 0.0)
    tile = jnp.where((iota((8, LANES), 0) & 1) == 0, top, e_face[...])
    for i in range(DEVICES // 4):
        pay[pl.ds(8 * i, 8), :] = tile


def update_kernel(parts, z1, p, s_old, rate, mobile, immobile):
    top = parts[pl.ds(0, DEVICES, stride=2), :]
    face = pltpu.roll(parts[pl.ds(1, DEVICES, stride=2), :], LANES // 2, 1)
    lane = iota((DEVICES, LANES), 1)
    other = jnp.where(lane < LANES // 2, pltpu.roll(face, 1, 0), pltpu.roll(face, DEVICES - 1, 0))
    cross = jnp.sum(jnp.where((lane & 15) < 9, top * other, 0.0), keepdims=True)
    total = jnp.sum(top, axis=0, keepdims=True)
    ss, sw, sq, ww, wq, qq = [total[:, 9 + k : 10 + k] for k in range(6)]
    qq = qq - 16.0 * cross
    factor = wq / ww
    y2 = (sq - factor * sw) / (qq - factor * wq)
    y1 = (sw - wq * y2) / ww
    for x in range(CX):
        new = y1 * z1[x] + y2 * p[x]
        mobile[x] = new
        for k in range(RATES):
            r = rate[k, x]
            immobile[k, x] = (s_old[k, x] + r * new) / (1.0 + r)


def call(kernel, ins, outs, scratch=(), flops=10_000, vmem=48 << 20):
    shapes = [jax.ShapeDtypeStruct(shape, dtype) for shape, dtype in outs]
    return pl.pallas_call(
        kernel,
        out_shape=shapes,
        in_specs=ins,
        out_specs=[VM] * len(shapes),
        scratch_shapes=list(scratch),
        cost_estimate=pl.CostEstimate(flops=flops, bytes_accessed=100_000, transcendentals=0),
        compiler_params=pltpu.CompilerParams(vmem_limit_bytes=vmem),
    )


FIELD = ((CX, CY, CZ), F32)
SOURCE_VMEM = 63 << 20
FIRST_UNROLL = 8
SECOND_UNROLL = 8


def swap_pairs(axis):
    n, m = lax.axis_size("coarse"), lax.axis_size("fine")
    inside, between = [], []
    for c in range(n):
        for f in range(m):
            me = c * m + f
            at, count, step = (c, n, m) if axis == "coarse" else (f, m, 1)
            inside.append((me, me + ((at ^ 1) - at) * step))
            if 0 < at < count - 1:
                between.append((me, me + (((at - 1) ^ 1) + 1 - at) * step))
            elif axis == "fine":
                between.append((me, (c ^ 1) * m + f))
            else:
                between.append((me, (n - 1 - c) * m + f))
    return inside, between


def swap_between(b, axis):
    return lax.ppermute(b, BOTH, swap_pairs(axis)[1])


def trade(a, b, axis):
    b = swap_between(b, axis)
    return lax.ppermute(a, BOTH, swap_pairs(axis)[0]), b


def everyone(pay, rows):
    moved = lax.all_to_all(pay.reshape(DEVICES, rows, LANES), BOTH, 0, 0)
    return moved.reshape(DEVICES * rows, LANES)


def local(
    c_old, s_old, rate_time, capacity, agg_count, coarse_order, coarse_cols, coarse_off, coarse_diag
):
    order = coarse_order.reshape(LANES, LANES)
    c, ic, s, zs, tab, both, x0b, y0a, y0b = call(
        source_kernel, [SM, VM, HB, HB] + [VM] * 3,
        [
            FIELD, FIELD, FIELD, FIELD, ((TABLE_ROWS, 256), F32), ((TABLE_ROWS + 40, 256), F32),
            ((40, CZ), F32), ((CY, CZ), F32), ((CY, CZ), F32),
        ],
        scratch=[
            pltpu.VMEM((RATES, CX, CY, CZ), F32),
            pltpu.VMEM((RATES, CX, CY, CZ), F32),
            pltpu.SemaphoreType.DMA((2, CX)),
        ],
        vmem=SOURCE_VMEM,
    )(
        capacity, c_old, s_old, rate_time, coarse_diag.reshape(1, SHARD_ROWS), coarse_cols, coarse_off,
    )
    other_core = [(i, i ^ 1) for i in range(8)]
    both = lax.ppermute(both, "coarse", other_core)
    tabs = [tab, both]
    for hop in (2, 4, 6):
        shard = lax.ppermute(tab, "coarse", [(i, i ^ hop) for i in range(8)])
        tabs += [shard, lax.ppermute(shard, "coarse", other_core)]
    x0b = swap_between(x0b, "coarse")
    y0a, y0b = trade(y0a, y0b, "fine")
    (pay,) = call(sums_kernel, [SM] + [VM] * 3, [((4 * DEVICES, LANES), F32)])(
        agg_count, s, coarse_diag.reshape(16, LANES), order
    )
    gathered = everyone(pay, 4)

    pe, plan, own, beside, across, at_row, at_lane, counts, x1a, x1b = call(
        first_kernel, [SM] + [VM] * 10,
        [
            FIELD, ((KC + 1, 24, SLOTS), F32), ((8, SLOTS), F32), ((8, LANES), I32), ((8, LANES), I32),
            ((LANES, LANES), I32), ((8, LANES), I32), ((LANES, LANES), I32),
            ((2 * CY, CZ), F32), ((2 * CY, CZ), F32),
        ],
        scratch=[pltpu.VMEM((SHARDS * 32, SHARD_ROWS), BF16)],
    )(agg_count, gathered, order, *tabs)
    x1a, x1b = trade(x1a, x1b, "coarse")
    (pay,) = call(early_kernel, [SM] + [VM] * 10, [((4 * DEVICES, LANES), F32)])(
        agg_count, beside, across, zs, ic, pe, c, both, x0b, y0a, y0b
    )
    sums = everyone(pay, 4)
    ya, yb = call(widen_kernel, [VM] * 7, [((len(PACKED), CZ), F32)] * 2)(zs, ic, pe, both, x0b, x1a, x1b)
    ya, yb = trade(ya, yb, "fine")

    pe2, pe_face, e_face = call(
        second_solve_kernel, [SM] + [VM] * 8, [FIELD, ((CY, CZ), F32), ((8, LANES), F32)], flops=100_000_000
    )(agg_count, sums, gathered, order, plan, own, at_row, at_lane, counts)
    z1, w1, p, sw_ghost, s_ghost, w_ghost, xa, xb = call(
        direction_kernel, [VM] * 11, [FIELD, FIELD, FIELD] + [((CY, CZ), F32)] * 5,
    )(zs, ic, pe, c, both, x0b, x1a, x1b, ya, yb, pe2)
    xa, xb = trade(xa, xb, "coarse")
    (pay,) = call(
        products_kernel, [VM] * 12, [((2 * DEVICES, LANES), F32)]
    )(s, w1, p, c, xa, xb, sw_ghost, s_ghost, w_ghost, pe_face, e_face, beside)
    parts = everyone(pay, 2)
    mobile, immobile = call(
        update_kernel, [VM] * 5, [FIELD, ((RATES, CX, CY, CZ), F32)]
    )(parts, z1, p, s_old, rate_time)
    return mobile, immobile


def solution(mesh):
    return jax.shard_map(
        local,
        mesh=mesh,
        in_specs=(
            P("coarse", "fine", None),
            P(None, "coarse", "fine", None),
            P(None, "coarse", "fine", None),
            P(),
            P(("coarse", "fine")),
            P(),
            P(None, "coarse"),
            P(None, "coarse"),
            P("coarse"),
        ),
        out_specs=(P("coarse", "fine", None), P(None, "coarse", "fine", None)),
        check_vma=False,
    )
```

```python
import jax
import jax.numpy as jnp
from jax import lax
from jax.experimental import pallas as pl
from jax.experimental.pallas import tpu as pltpu
from jax.sharding import PartitionSpec as P

BOTH = ("coarse", "fine")
CX, CY, CZ = 4, 8, 256
RATES = 16
KC = 8
DEVICES = 128
LANES = 128
SLOTS = 256
SHARDS = 8
SHARD_ROWS = 2048
FLOW = 50.0
TABLE_ROWS = 128
UNUSED = 1e30
F32, BF16, I32 = jnp.float32, jnp.bfloat16, jnp.int32
VM = pl.BlockSpec(memory_space=pltpu.VMEM)
SM = pl.BlockSpec(memory_space=pltpu.SMEM)
HB = pl.BlockSpec(memory_space=pltpu.HBM)


def places():
    return lax.axis_index("coarse").astype(I32), lax.axis_index("fine").astype(I32)


def iota(shape, dim):
    return lax.broadcasted_iota(I32, shape, dim)


def lane_take(table, index):
    return jnp.take_along_axis(table, index, axis=1, mode="promise_in_bounds")


def nt(left, right):
    return lax.dot_general(left, right, (((1,), (1,)), ((), ())), preferred_element_type=F32)


def nn(left, right):
    return jnp.dot(left, right, preferred_element_type=F32)


def split2(values):
    high = values.astype(BF16)
    return high, (values - high.astype(F32)).astype(BF16)


def slots_of(plane, half, count):
    row = (plane * CY + iota((CY, LANES), 0)) * 2 + half
    return ((row * LANES + iota((CY, LANES), 1)) * count) >> 13


def restrict_plane(values, plane, count, total, base):
    slot = iota(total.shape, 1) + base
    for half in range(2):
        part_of = values[:, half * LANES : (half + 1) * LANES]
        row = (plane * CY + iota((CY, 1), 0)) * 2 + half
        first = (row * count) >> 6
        member = slots_of(plane, half, count) - first
        relative = slot - first
        for k in range(5):
            part = jnp.sum(jnp.where(member == k, part_of, 0.0), axis=1, keepdims=True)
            total = total + jnp.where(relative == k, part, 0.0)
    return total


def restrict(cells, count):
    total = jnp.zeros((CY, SLOTS), F32)
    for plane in range(CX):
        total = restrict_plane(cells[plane], plane, count, total, 0)
    return jnp.sum(total, axis=0, keepdims=True)


def rim_restrict(rim, count):
    n = jnp.concatenate([count, count], axis=1)
    row = iota((CY, CZ), 0)
    cells = ((row & 3) * CY + jnp.where(row < 4, CY - 1, 0)) * CZ
    member = (((cells + iota((CY, CZ), 1)) * n) >> 13) - ((cells * n) >> 13)
    lane = iota((8, LANES), 1)
    start = iota((8, LANES), 0) * 16
    spread = jnp.zeros((8, LANES), F32)
    for k in range(9):
        part = jnp.sum(jnp.where(member == k, rim, 0.0), axis=1, keepdims=True)
        spread = spread + jnp.where(lane == start + k, part, 0.0)
    return jnp.sum(spread, axis=0, keepdims=True)


def rim_exists(index):
    return jnp.where(iota((CY, CZ), 0) < 4, index, 15 - index) > 0


def prolong(entries, count):
    low = jnp.broadcast_to(entries[:, :LANES], (CY, LANES))
    high = jnp.broadcast_to(entries[:, LANES:], (CY, LANES))
    planes = []
    for plane in range(CX):
        halves = []
        for half in range(2):
            slot = slots_of(plane, half, count)
            place = slot & 127
            halves.append(jnp.where(slot < LANES, lane_take(low, place), lane_take(high, place)))
        planes.append(jnp.concatenate(halves, axis=1))
    return planes


def couple(left, mid, right, up, down):
    length = mid.shape[1]
    lane = iota(mid.shape, 1)
    behind = jnp.where(lane == 0, 0.0, pltpu.roll(mid, 1, 1))
    ahead = jnp.where(lane == length - 1, 0.0, pltpu.roll(mid, length - 1, 1))
    return 8.0 * (left + right + up + down + ahead) + 10.0 * behind


def source_kernel(
    cap, c_old, s_old_hbm, rate_hbm, diag, cols, off,
    c_out, ic_out, s_out, zs_out, tab, both, xb, ya, yb, s_old, rate, sems,
):
    copies = []
    for x in range(CX):
        pair = (
            pltpu.make_async_copy(rate_hbm.at[:, x], rate.at[:, x], sems.at[0, x]),
            pltpu.make_async_copy(s_old_hbm.at[:, x], s_old.at[:, x], sems.at[1, x]),
        )
        for copy in pair:
            copy.start()
        copies.append(pair)
    for j in range(SHARD_ROWS // 256):
        at = slice(256 * j, 256 * j + 256)
        part = jnp.concatenate([cols[:, at].astype(F32), off[:, at] * (0.8 / diag[:, at])], axis=0)
        tab[16 * j : 16 * j + 16, :] = part
        both[16 * j : 16 * j + 16, :] = part
    smooth, inverse = [], []
    for x in range(CX):
        for copy in copies[x]:
            copy.wait()
        mass = jnp.zeros((CY, CZ), F32)
        extra = jnp.zeros((CY, CZ), F32)
        for k in range(RATES):
            r = rate[k, x]
            weighted = cap[k] * (r / (1.0 + r))
            mass = mass + weighted
            extra = extra + weighted * s_old[k, x]
        centre = (1.0 + mass) + FLOW
        source = c_old[x] + extra
        inv = 1.0 / centre
        c_out[x] = centre
        ic_out[x] = inv
        s_out[x] = source
        zs_out[x] = 0.8 * source * inv
        smooth.append(0.8 * source * inv)
        inverse.append(inv)
    xa, xb[...] = send_planes([(smooth, 4), (inverse, 3)])
    both[TABLE_ROWS:, :] = xa
    ya[...], yb[...] = send_rows(EARLY_ROWS, lambda f, x: (smooth, inverse)[f][x])


def send_planes(fields):
    even = (places()[0] & 1) == 0
    upper = jnp.concatenate([p for planes, depth in fields for p in planes[CX - depth :]], axis=0)
    lower = jnp.concatenate([p for planes, depth in fields for p in planes[:depth]], axis=0)
    return jnp.where(even, upper, lower), jnp.where(even, lower, upper)


def ghost_rows(field, x):
    return max(0, (4, 3, 3)[field] - max(0, -x, x - CX + 1))


EARLY_ROWS = [(f, x) for f in range(2) for x in range(CX)]
LATE_ROWS = [(f, x) for f in range(3) for x in range(-3, CX + 3) if ghost_rows(f, x) and (f, x) not in EARLY_ROWS]


def row_of(rows, which):
    return sum(ghost_rows(*w) for w in rows[: rows.index(which)])


def row_count(rows):
    return sum(ghost_rows(*w) for w in rows)


def send_rows(rows, plane):
    even = (places()[1] & 1) == 0
    upper = jnp.concatenate([plane(*w)[CY - ghost_rows(*w) :] for w in rows], axis=0)
    lower = jnp.concatenate([plane(*w)[: ghost_rows(*w)] for w in rows], axis=0)
    return jnp.where(even, upper, lower), jnp.where(even, lower, upper)


def sums_kernel(count, s, diag, order, pay):
    place = places()
    n = count[0]
    mine = (order[0:1, :] >> 7) == place[0] * 16 + place[1]
    low = jnp.sum(jnp.where(mine, (order[...] & 127).astype(F32), 0.0), axis=1, keepdims=True)
    spot = iota((LANES, LANES), 1).astype(F32) == low
    inverse = jnp.sum(jnp.where(spot, iota((LANES, LANES), 0).astype(F32), 0.0), axis=0, keepdims=True)
    sums = jnp.where(iota((1, SLOTS), 1) < n, restrict([s[x] for x in range(CX)], n), UNUSED)
    repeat4(pay, [sums[:, :LANES], sums[:, LANES:], diag[pl.ds(place[1], 1), :], inverse])


def repeat4(pay, rows):
    kind = iota((8, LANES), 0) & 3
    tile = jnp.broadcast_to(rows[3], (8, LANES))
    for k in range(3):
        tile = jnp.where(kind == k, rows[k], tile)
    for i in range(DEVICES // 2):
        pay[pl.ds(8 * i, 8), :] = tile


def read_sums(gathered):
    low = gathered[pl.ds(0, DEVICES, stride=4), :]
    high = gathered[pl.ds(1, DEVICES, stride=4), :]
    diag = gathered[pl.ds(2, DEVICES, stride=4), :]
    inverse = gathered[pl.ds(3, DEVICES, stride=4), :].astype(I32)
    used = jnp.where(low < 0.5 * UNUSED, 1.0, 0.0) + jnp.where(high < 0.5 * UNUSED, 1.0, 0.0)
    return low, high, diag, inverse, jnp.sum(used, axis=1, keepdims=True)


def offsets_of(counts):
    row, lane = iota((LANES, LANES), 0), iota((LANES, LANES), 1)
    by_lane = jnp.sum(jnp.where(row < lane, counts, 0.0), axis=0, keepdims=True)
    across = jnp.sum(jnp.where(row == lane, counts, 0.0), axis=0, keepdims=True)
    by_row = jnp.sum(jnp.where(lane < row, across, 0.0), axis=1, keepdims=True)
    return jnp.broadcast_to(by_row, (LANES, LANES)).astype(I32), by_lane.astype(I32)


def blocks_of(order):
    return (iota((LANES, LANES), 0) == (order[0:1, :] >> 7)).astype(F32).astype(BF16)


def assemble(low, high, offsets, inverse, blocks):
    by_row, by_lane = offsets
    lane = iota((LANES, LANES), 1)
    shift = by_row & 127
    place = (lane - shift) & 127
    low = lane_take(low, place)
    high = lane_take(high, place)
    kept = lane >= shift
    rows = (jnp.where(kept, low, 0.0), jnp.where(kept, high, low), jnp.where(kept, 0.0, high))
    start = by_lane >> 7
    spots = [(iota((LANES, LANES), 0) == start + j).astype(F32).astype(BF16) for j in range(3)]
    parts = [jnp.concatenate(split2(r), axis=1) for r in rows]
    table = nn(jnp.concatenate(spots, axis=1), jnp.concatenate(parts, axis=0))
    by_block = nt(blocks, jnp.concatenate([table[:, :LANES], table[:, LANES:]], axis=0).astype(BF16))
    return lane_take(by_block[:, :LANES] + by_block[:, LANES:], inverse)


def one_hot(row16, index):
    return jnp.where(row16 == index.astype(BF16), jnp.ones(row16.shape, BF16), jnp.zeros(row16.shape, BF16))


def fetch(table, unknown, coarse):
    inner = unknown & (SHARD_ROWS - 1)
    shard = (unknown >> 11) ^ coarse
    row16 = iota((256, SLOTS), 0).astype(F32).astype(BF16)
    found = jnp.zeros((SHARDS * 32, SLOTS), F32)
    for chunk in range(SHARD_ROWS // 256):
        spot = one_hot(row16, (inner - chunk * 256).astype(F32))
        found = found + nn(table[:, chunk * 256 : (chunk + 1) * 256], spot)
    found = found.reshape(SHARDS, 32, SLOTS)
    picked = found[0]
    for g in range(1, SHARDS):
        picked = jnp.where(shard == g, found[g], picked)
    return picked[0:8], picked[8:16], picked[16:24] + picked[24:32]


def gatherer(values):
    high, low = split2(values.T)
    table = jnp.concatenate([high, low], axis=1)
    row = iota((LANES, SLOTS), 0).astype(F32)
    row16 = row.astype(BF16)

    def gather(block, inner):
        spot = one_hot(row16, block)
        found = nn(table, jnp.concatenate([spot, spot], axis=0))
        kept = jnp.zeros((8, SLOTS), F32)
        for b in range(0, LANES, 8):
            kept = jnp.where(row[b : b + 8] == inner, found[b : b + 8], kept)
        return kept

    return gather


def solve_entry(gather, first, parts):
    total = -1.4 * gather(first[0], first[1])
    for j in range(KC):
        total = total + parts[2][j : j + 1] * gather(parts[0][j : j + 1], parts[1][j : j + 1])
    return first[2] * total


def coarse_solve(values, plan, own):
    gather = gatherer(values)

    def column(k, total):
        first = [plan[KC, pl.ds(8 * i + k, 1), :] for i in range(3)]
        return total + solve_entry(gather, first, [plan[k, 8 * i : 8 * i + 8, :] for i in range(3)])

    total = lax.fori_loop(0, KC, column, 1.24 * gather(own[0:1, :], own[1:2, :]), unroll=SECOND_UNROLL)
    return jnp.sum(total, axis=0, keepdims=True)


def plan_rows(ref, k, parts):
    ref[k, 0:8, :] = parts[0]
    ref[k, 8:16, :] = parts[1]
    ref[k, 16:24, :] = parts[2]


def first_kernel(
    count, gathered, order, tab0, tab1, tab2, tab3, tab4, tab5, tab6, tab7,
    pe_out, plan, own, beside, across, at_row, at_lane, counts_out, xa, xb, table,
):
    place = places()
    n = count[0]
    me = place[0] * 16 + place[1]
    low, high, diag, inverse, counts = read_sums(gathered)
    offsets = offsets_of(counts)
    at_row[...] = offsets[0]
    at_lane[...] = jnp.broadcast_to(offsets[1], (8, LANES))
    sums = assemble(
        jnp.where(low < 0.5 * UNUSED, low, 0.0), jnp.where(high < 0.5 * UNUSED, high, 0.0),
        offsets, inverse, blocks_of(order),
    )
    values = 0.8 * sums / diag
    counts = jnp.broadcast_to(counts, (LANES, LANES))
    counts_out[...] = counts.astype(I32)
    row = iota((LANES, LANES), 0)
    before = iota((8, LANES), 0) < 4
    for out, step in ((beside, 1), (across, 16)):
        sides = [jnp.sum(jnp.where(row == me + d, counts, 0.0), axis=0, keepdims=True) for d in (-step, step)]
        out[...] = jnp.where(before, sides[0], sides[1]).astype(I32)

    tabs = (tab0, tab1, tab2, tab3, tab4, tab5, tab6, tab7)
    for g in range(SHARDS):
        for j in range(SHARD_ROWS // 256):
            at = slice(256 * j, 256 * j + 256)
            cols = tabs[g][16 * j : 16 * j + 8, :]
            big = jnp.floor(cols * (1.0 / 128.0))
            pair = jnp.concatenate([big, cols - 128.0 * big], axis=0)
            table[32 * g : 32 * g + 16, at] = pair.astype(BF16)
            off = tabs[g][16 * j + 8 : 16 * j + 16, :]
            big = off.astype(BF16).astype(F32)
            table[32 * g + 16 : 32 * g + 32, at] = jnp.concatenate([big, off - big], axis=0).astype(BF16)

    mine = jnp.sum(jnp.where(row == me, offsets[0].astype(F32), 0.0), axis=0, keepdims=True).astype(I32)
    numbers = order[...].astype(F32)
    start = mine >> 7
    lines = []
    spread = (iota((8, LANES), 1) + mine) & 127
    for j in range(3):
        line = jnp.sum(jnp.where(row == start + j, numbers, 0.0), axis=0, keepdims=True)
        lines.append(lane_take(jnp.broadcast_to(line, (8, LANES)), spread))
    inside = iota((8, LANES), 1) + (mine & 127) < LANES
    unknown = jnp.concatenate(
        [jnp.where(inside, lines[0], lines[1]), jnp.where(inside, lines[1], lines[2])], axis=1
    )[0:1].astype(I32)
    own[0:1, :] = (unknown >> 7).astype(F32)
    own[1:2, :] = (unknown & 127).astype(F32)
    plan_rows(plan, KC, fetch(table, unknown, place[0]))

    def column(k, carry):
        col = 128.0 * plan[KC, pl.ds(k, 1), :] + plan[KC, pl.ds(8 + k, 1), :]
        plan_rows(plan, k, fetch(table, col.astype(I32), place[0]))
        return carry

    lax.fori_loop(0, KC, column, 0, unroll=FIRST_UNROLL)
    pe = prolong(coarse_solve(values, plan, own), n)
    for x in range(CX):
        pe_out[x] = pe[x]

    xa[...], xb[...] = send_planes([(pe, 3)])


def below_above(index, count, a, b):
    even = (index & 1) == 0
    inner = jnp.logical_and(index > 0, index < count - 1)

    def near(i):
        if i is not ...:
            i = slice(CY * i, CY * i + CY)
        return a[i], jnp.where(inner, b[i], 0.0)

    def below(i):
        first, second = near(i)
        return jnp.where(even, second, first)

    def above(i):
        first, second = near(i)
        return jnp.where(even, first, second)

    return below, above


def with_ghosts(own, messages):
    def plane(field, x):
        if 0 <= x < CX:
            return own[field][x]
        below, above, base, depth = messages[field]
        return below(base + depth + x) if x < 0 else above(base + x - CX)

    return plane


def widen(plane, fields, ya, yb):
    even = (places()[1] & 1) == 0
    upper, lower = [], []
    for f in fields:
        for x in range(-3, CX + 3):
            d = ghost_rows(f, x)
            if d:
                here = plane(f, x)
                upper.append(here[CY - d :])
                lower.append(here[:d])
    upper, lower = jnp.concatenate(upper, axis=0), jnp.concatenate(lower, axis=0)
    ya[...] = jnp.where(even, upper, lower)
    yb[...] = jnp.where(even, lower, upper)


def all_ghosts(own, x0a, x0b, x1a, x1b):
    early = below_above(places()[0], 8, x0a.at[TABLE_ROWS:], x0b)
    late = below_above(places()[0], 8, x1a, x1b)
    return with_ghosts(own, ((*early, 0, 4), (*early, 4, 3), (*late, 0, 3)))


def widen_kernel(zs, ic, pe, x0a, x0b, x1a, x1b, ya, yb):
    plane = all_ghosts((zs, ic, pe), x0a, x0b, x1a, x1b)
    ya[...], yb[...] = send_rows(LATE_ROWS, plane)


def early_kernel(count, beside, across, zs, ic, pe, c, xa, xb, ya, yb, pay):
    place = places()
    n = count[0]
    below, above = below_above(place[0], 8, xa.at[TABLE_ROWS:], xb)
    near, far = [side(...) for side in below_above(place[1], 16, ya, yb)]
    row = iota((CY, CZ), 0)
    z1 = []
    for x in range(CX):
        mid = zs[x]
        left = zs[x - 1] if x else below(3)
        right = zs[x + 1] if x + 1 < CX else above(0)
        at = row_of(EARLY_ROWS, (0, x))
        last = at + ghost_rows(0, x) - 1
        up = jnp.where(row == 0, near[last : last + 1], pltpu.roll(mid, 1, 0))
        down = jnp.where(row == CY - 1, far[at : at + 1], pltpu.roll(mid, CY - 1, 0))
        z1.append(1.2 * mid + 0.8 * ic[x] * couple(left, mid, right, up, down) + pe[x])
    image = []
    zero = jnp.zeros((CY, CZ), F32)
    for x in range(CX):
        mid = z1[x]
        up = jnp.where(row == 0, 0.0, pltpu.roll(mid, 1, 0))
        down = jnp.where(row == CY - 1, 0.0, pltpu.roll(mid, CY - 1, 0))
        left = z1[x - 1] if x else zero
        right = z1[x + 1] if x + 1 < CX else zero
        image.append(c[x] * mid - couple(left, mid, right, up, down))
    sums = restrict(image, n)
    blank = jnp.zeros((CY, LANES), F32)
    lane = iota((1, LANES), 1)
    under, over = across[0:1, 0:1], across[4:5, 0:1]
    down_x = restrict_plane(-8.0 * z1[0], CX - 1, under, blank, (3 * under) >> 2)
    up_x = restrict_plane(-8.0 * z1[CX - 1], 0, over, blank, 0)
    down_x = jnp.where(place[0] > 0, jnp.sum(down_x, axis=0, keepdims=True), 0.0)
    up_x = jnp.where(place[0] < 7, jnp.sum(up_x, axis=0, keepdims=True), 0.0)
    along_x = jnp.where(lane < 64, down_x, pltpu.roll(jnp.broadcast_to(up_x, (8, LANES)), 64, 1)[0:1])
    rims = jnp.concatenate([z[0:1] for z in z1] + [z[CY - 1 : CY] for z in z1], axis=0)
    along_y = rim_restrict(jnp.where(rim_exists(place[1]), -8.0 * rims, 0.0), beside[...])
    repeat4(pay, [sums[:, :LANES], sums[:, LANES:], along_x, along_y])


def add_neighbours(low, high, from_x, from_y, counts):
    lane = iota((DEVICES, LANES), 1)

    def place(window, base, shift, length):
        nonlocal low, high
        relative = lane - base
        moved = lane_take(window, (relative + shift) & 127)
        low = low + jnp.where(jnp.logical_and(relative >= 0, relative < length), moved, 0.0)
        relative = relative + LANES
        high = high + jnp.where(jnp.logical_and(relative >= 0, relative < length), moved, 0.0)

    low = low + jnp.where(lane < 64, pltpu.roll(pltpu.roll(from_x, 16, 0), 64, 1), 0.0)
    place(pltpu.roll(from_x, DEVICES - 16, 0), (3 * counts) >> 2, 0, 64)
    both = jnp.where(lane < 64, pltpu.roll(from_y, DEVICES - 1, 0), pltpu.roll(from_y, 1, 0))
    for g in range(2 * CX):
        cells = ((g & 3) * CY + (CY - 1 if g < CX else 0)) * CZ
        place(both, (cells * counts) >> 13, 16 * g, 9)
    return low, high


def second_solve_kernel(
    count, sums, gathered, order, plan, own, at_row, at_lane, counts, pe_out, pe_face, e_face, xa, xb
):
    n = count[0]
    low, high = add_neighbours(
        sums[pl.ds(0, DEVICES, stride=4), :], sums[pl.ds(1, DEVICES, stride=4), :],
        sums[pl.ds(2, DEVICES, stride=4), :], sums[pl.ds(3, DEVICES, stride=4), :], counts[...],
    )
    diag = gathered[pl.ds(2, DEVICES, stride=4), :]
    inverse = gathered[pl.ds(3, DEVICES, stride=4), :].astype(I32)
    values = assemble(low, high, (at_row[...], at_lane[0:1, :]), inverse, blocks_of(order))
    entries = coarse_solve(0.8 * values / diag, plan, own)
    pe = prolong(entries, n)
    for x in range(CX):
        pe_out[x] = pe[x]
        pe_face[x : x + 1, :] = pe[x][0:1]
        pe_face[CX + x : CX + x + 1, :] = pe[x][CY - 1 : CY]
    xa[...], xb[...] = send_planes([(pe, 1)])
    lane = iota((8, LANES), 1)
    group = lane >> 4
    cells = ((group & 3) * CY + jnp.where(group < 4, 0, CY - 1)) * CZ
    slot = jnp.minimum(((cells * n) >> 13) + (lane & 15), SLOTS - 1)
    low = jnp.broadcast_to(entries[:, :LANES], (8, LANES))
    high = jnp.broadcast_to(entries[:, LANES:], (8, LANES))
    e_face[...] = jnp.where(slot < LANES, lane_take(low, slot & 127), lane_take(high, slot & 127))


def direction_kernel(
    zs, ic, pe, c, x0a, x0b, x1a, x1b, y0a, y0b, y1a, y1b, after,
    z1_out, w1_out, sw_out, sw_beside, sw_ghost, s_ghost, w_ghost,
):
    place = places()
    middle = all_ghosts((zs, ic, pe), x0a, x0b, x1a, x1b)
    early = [side(...) for side in below_above(place[1], 16, y0a, y0b)]
    late = [side(...) for side in below_above(place[1], 16, y1a, y1b)]

    def plane(field, x):
        d = ghost_rows(field, x)
        here = middle(field, x)
        if not d:
            blank = jnp.zeros((8, CZ), F32)
            return jnp.concatenate([blank, here, blank], axis=0)
        rows, (near, far) = (EARLY_ROWS, early) if (field, x) in EARLY_ROWS else (LATE_ROWS, late)
        at = row_of(rows, (field, x))
        blank = jnp.zeros((8 - d, CZ), F32)
        return jnp.concatenate([blank, near[at : at + d], here, far[at : at + d], blank], axis=0)

    def neighbours(get, x):
        mid = get(x)
        count = mid.shape[0]
        return couple(get(x - 1), mid, get(x + 1), pltpu.roll(mid, 1, 0), pltpu.roll(mid, count - 1, 0))

    z = {x: plane(0, x) for x in range(-4, CX + 4)}
    inv = {x: plane(1, x) for x in range(-3, CX + 3)}
    first = {}
    for x in range(-3, CX + 3):
        first[x] = 1.2 * z[x] + 0.8 * inv[x] * neighbours(z.get, x) + plane(2, x)
    zw = {}
    for x in range(-2, CX + 2):
        beside = neighbours(first.get, x)
        zw[x] = 0.8 * (first[x] - inv[x] * beside)
        if 0 <= x < CX:
            z1_out[x] = first[x][8:16]
            w1_out[x] = c[x] * first[x][8:16] - beside[8:16]
    for x in range(-1, CX + 1):
        smooth = 1.2 * zw[x] + 0.8 * inv[x] * neighbours(zw.get, x)
        if not 0 <= x < CX:
            sw_beside[0 if x < 0 else 1] = smooth[8:16]
            continue
        sw_out[x] = smooth[8:16]
        for at, row in ((x, 7), (CX + x, 16)):
            iv = inv[x][row : row + 1]
            scale = jnp.where(iv > 0.0, 1.25 / jnp.where(iv > 0.0, iv, 1.0), 0.0)
            sw_ghost[at : at + 1, :] = smooth[row : row + 1]
            s_ghost[at : at + 1, :] = z[x][row : row + 1] * scale
            w_ghost[at : at + 1, :] = zw[x][row : row + 1] * scale


def products_kernel(
    s, w1, sw, pe2, c, xa, xb, sw_beside, sw_ghost, s_ghost, w_ghost, pe_face, e_face, beside, pay
):
    place = places()
    below, above = [side(...) for side in below_above(place[0], 8, xa, xb)]
    sums = [jnp.zeros((CY, CZ), F32) for _ in range(6)]
    row = iota((CY, CZ), 0)
    rims = [None] * (2 * CX)
    p = [below + sw_beside[0], *(sw[x] + pe2[x] for x in range(CX)), above + sw_beside[1]]
    for x in range(CX):
        left, mid, right = p[x : x + 3]
        up = jnp.where(row == 0, sw_ghost[x : x + 1, :], pltpu.roll(mid, 1, 0))
        down = jnp.where(row == CY - 1, sw_ghost[CX + x : CX + x + 1, :], pltpu.roll(mid, CY - 1, 0))
        q = c[x] * mid - couple(left, mid, right, up, down)
        rims[x], rims[CX + x] = q[0:1], q[CY - 1 : CY]
        a, b = s[x], w1[x]
        for k, term in enumerate((a * a, a * b, a * q, b * b, b * q, q * q)):
            sums[k] = sums[k] + term
    exists = rim_exists(place[1])
    face = pe_face[...]
    sums[2] = sums[2] - 8.0 * face * s_ghost[...]
    sums[4] = sums[4] - 8.0 * face * w_ghost[...]
    sums[5] = sums[5] + jnp.where(exists, 64.0 * face * face, 0.0)
    rim = jnp.where(exists, jnp.concatenate(rims, axis=0), 0.0)
    lane = iota((8, LANES), 1)
    top = jnp.broadcast_to(rim_restrict(rim, beside[...]), (8, LANES))
    for k in range(6):
        top = top + jnp.where(lane == 9 + k, jnp.sum(sums[k], keepdims=True), 0.0)
    tile = jnp.where((iota((8, LANES), 0) & 1) == 0, top, e_face[...])
    for i in range(DEVICES // 4):
        pay[pl.ds(8 * i, 8), :] = tile


def update_kernel(parts, z1, smooth, pe2, s_old, rate, mobile, immobile):
    top = parts[pl.ds(0, DEVICES, stride=2), :]
    face = pltpu.roll(parts[pl.ds(1, DEVICES, stride=2), :], LANES // 2, 1)
    lane = iota((DEVICES, LANES), 1)
    other = jnp.where(lane < LANES // 2, pltpu.roll(face, 1, 0), pltpu.roll(face, DEVICES - 1, 0))
    cross = jnp.sum(jnp.where((lane & 15) < 9, top * other, 0.0), keepdims=True)
    total = jnp.sum(top, axis=0, keepdims=True)
    ss, sw, sq, ww, wq, qq = [total[:, 9 + k : 10 + k] for k in range(6)]
    qq = qq - 16.0 * cross
    factor = wq / ww
    y2 = (sq - factor * sw) / (qq - factor * wq)
    y1 = (sw - wq * y2) / ww
    for x in range(CX):
        new = y1 * z1[x] + y2 * (smooth[x] + pe2[x])
        mobile[x] = new
        for k in range(RATES):
            r = rate[k, x]
            immobile[k, x] = (s_old[k, x] + r * new) / (1.0 + r)


def call(kernel, ins, outs, scratch=(), flops=10_000, vmem=48 << 20):
    shapes = [jax.ShapeDtypeStruct(shape, dtype) for shape, dtype in outs]
    return pl.pallas_call(
        kernel,
        out_shape=shapes,
        in_specs=ins,
        out_specs=[VM] * len(shapes),
        scratch_shapes=list(scratch),
        cost_estimate=pl.CostEstimate(flops=flops, bytes_accessed=100_000, transcendentals=0),
        compiler_params=pltpu.CompilerParams(vmem_limit_bytes=vmem),
    )


FIELD = ((CX, CY, CZ), F32)
SOURCE_VMEM = 63 << 20
FIRST_UNROLL = 8
SECOND_UNROLL = 8


def swap_pairs(axis):
    n, m = lax.axis_size("coarse"), lax.axis_size("fine")
    inside, between = [], []
    for c in range(n):
        for f in range(m):
            me = c * m + f
            at, count, step = (c, n, m) if axis == "coarse" else (f, m, 1)
            inside.append((me, me + ((at ^ 1) - at) * step))
            if 0 < at < count - 1:
                between.append((me, me + (((at - 1) ^ 1) + 1 - at) * step))
            elif axis == "fine":
                between.append((me, (c ^ 1) * m + f))
            else:
                between.append((me, (n - 1 - c) * m + f))
    return inside, between


def swap_between(b, axis):
    return lax.ppermute(b, BOTH, swap_pairs(axis)[1])


def trade(a, b, axis):
    b = swap_between(b, axis)
    return lax.ppermute(a, BOTH, swap_pairs(axis)[0]), b


def everyone(pay, rows):
    moved = lax.all_to_all(pay.reshape(DEVICES, rows, LANES), BOTH, 0, 0)
    return moved.reshape(DEVICES * rows, LANES)


def local(
    c_old, s_old, rate_time, capacity, agg_count, coarse_order, coarse_cols, coarse_off, coarse_diag
):
    order = coarse_order.reshape(LANES, LANES)
    c, ic, s, zs, tab, both, x0b, y0a, y0b = call(
        source_kernel, [SM, VM, HB, HB] + [VM] * 3,
        [
            FIELD, FIELD, FIELD, FIELD, ((TABLE_ROWS, 256), F32), ((TABLE_ROWS + 7 * CY, 256), F32),
            ((7 * CY, CZ), F32), ((row_count(EARLY_ROWS), CZ), F32), ((row_count(EARLY_ROWS), CZ), F32),
        ],
        scratch=[
            pltpu.VMEM((RATES, CX, CY, CZ), F32),
            pltpu.VMEM((RATES, CX, CY, CZ), F32),
            pltpu.SemaphoreType.DMA((2, CX)),
        ],
        vmem=SOURCE_VMEM,
    )(
        capacity, c_old, s_old, rate_time, coarse_diag.reshape(1, SHARD_ROWS), coarse_cols, coarse_off,
    )
    other_core = [(i, i ^ 1) for i in range(8)]
    both = lax.ppermute(both, "coarse", other_core)
    tabs = [tab, both]
    for hop in (2, 4, 6):
        shard = lax.ppermute(tab, "coarse", [(i, i ^ hop) for i in range(8)])
        tabs += [shard, lax.ppermute(shard, "coarse", other_core)]
    x0b = swap_between(x0b, "coarse")
    y0a, y0b = trade(y0a, y0b, "fine")
    (pay,) = call(sums_kernel, [SM] + [VM] * 3, [((4 * DEVICES, LANES), F32)])(
        agg_count, s, coarse_diag.reshape(16, LANES), order
    )
    gathered = everyone(pay, 4)

    pe, plan, own, beside, across, at_row, at_lane, counts, x1a, x1b = call(
        first_kernel, [SM] + [VM] * 10,
        [
            FIELD, ((KC + 1, 24, SLOTS), F32), ((8, SLOTS), F32), ((8, LANES), I32), ((8, LANES), I32),
            ((LANES, LANES), I32), ((8, LANES), I32), ((LANES, LANES), I32),
            ((3 * CY, CZ), F32), ((3 * CY, CZ), F32),
        ],
        scratch=[pltpu.VMEM((SHARDS * 32, SHARD_ROWS), BF16)],
    )(agg_count, gathered, order, *tabs)
    x1a, x1b = trade(x1a, x1b, "coarse")
    (pay,) = call(early_kernel, [SM] + [VM] * 10, [((4 * DEVICES, LANES), F32)])(
        agg_count, beside, across, zs, ic, pe, c, both, x0b, y0a, y0b
    )
    sums = everyone(pay, 4)
    y1a, y1b = call(widen_kernel, [VM] * 7, [((row_count(LATE_ROWS), CZ), F32)] * 2)(
        zs, ic, pe, both, x0b, x1a, x1b
    )
    y1a, y1b = trade(y1a, y1b, "fine")

    pe2, pe_face, e_face, xa, xb = call(
        second_solve_kernel, [SM] + [VM] * 8,
        [FIELD, ((CY, CZ), F32), ((8, LANES), F32), ((CY, CZ), F32), ((CY, CZ), F32)], flops=100_000_000,
    )(agg_count, sums, gathered, order, plan, own, at_row, at_lane, counts)
    xa, xb = trade(xa, xb, "coarse")
    z1, w1, sw, sw_beside, sw_ghost, s_ghost, w_ghost = call(
        direction_kernel, [VM] * 13, [FIELD, FIELD, FIELD, ((2, CY, CZ), F32)] + [((CY, CZ), F32)] * 3,
    )(zs, ic, pe, c, both, x0b, x1a, x1b, y0a, y0b, y1a, y1b, e_face)
    (pay,) = call(
        products_kernel, [VM] * 14, [((2 * DEVICES, LANES), F32)]
    )(s, w1, sw, pe2, c, xa, xb, sw_beside, sw_ghost, s_ghost, w_ghost, pe_face, e_face, beside)
    parts = everyone(pay, 2)
    mobile, immobile = call(
        update_kernel, [VM] * 6, [FIELD, ((RATES, CX, CY, CZ), F32)]
    )(parts, z1, sw, pe2, s_old, rate_time)
    return mobile, immobile


def solution(mesh):
    return jax.shard_map(
        local,
        mesh=mesh,
        in_specs=(
            P("coarse", "fine", None),
            P(None, "coarse", "fine", None),
            P(None, "coarse", "fine", None),
            P(),
            P(("coarse", "fine")),
            P(),
            P(None, "coarse"),
            P(None, "coarse"),
            P("coarse"),
        ),
        out_specs=(P("coarse", "fine", None), P(None, "coarse", "fine", None)),
        check_vma=False,
    )
```

```python
import jax
import jax.numpy as jnp
from jax import lax
from jax.experimental import pallas as pl
from jax.experimental.pallas import tpu as pltpu
from jax.sharding import PartitionSpec as P

BOTH = ("coarse", "fine")
CX, CY, CZ = 4, 8, 256
RATES = 16
KC = 8
DEVICES = 128
LANES = 128
SLOTS = 256
SHARDS = 8
SHARD_ROWS = 2048
FLOW = 50.0
TABLE_ROWS = 128
UNUSED = 1e30
F32, BF16, I32 = jnp.float32, jnp.bfloat16, jnp.int32
VM = pl.BlockSpec(memory_space=pltpu.VMEM)
SM = pl.BlockSpec(memory_space=pltpu.SMEM)
HB = pl.BlockSpec(memory_space=pltpu.HBM)


def places():
    return lax.axis_index("coarse").astype(I32), lax.axis_index("fine").astype(I32)


def iota(shape, dim):
    return lax.broadcasted_iota(I32, shape, dim)


def lane_take(table, index):
    return jnp.take_along_axis(table, index, axis=1, mode="promise_in_bounds")


def nt(left, right):
    return lax.dot_general(left, right, (((1,), (1,)), ((), ())), preferred_element_type=F32)


def nn(left, right):
    return jnp.dot(left, right, preferred_element_type=F32)


def split2(values):
    high = values.astype(BF16)
    return high, (values - high.astype(F32)).astype(BF16)


def slots_of(plane, half, count):
    row = (plane * CY + iota((CY, LANES), 0)) * 2 + half
    return ((row * LANES + iota((CY, LANES), 1)) * count) >> 13


def restrict_plane(values, plane, count, totals, base):
    lane = iota((CY, LANES), 1)
    for half in range(2):
        part_of = values[:, half * LANES : (half + 1) * LANES]
        row = (plane * CY + iota((CY, LANES), 0)) * 2 + half
        first = (row * count) >> 6
        member = slots_of(plane, half, count) - first
        relative = lane + (base - first)
        for k in range(5):
            part = jnp.sum(jnp.where(member == k, part_of, 0.0), axis=1, keepdims=True)
            totals = [t + jnp.where(relative == k - LANES * i, part, 0.0) for i, t in enumerate(totals)]
    return totals


def restrict(cells, count):
    totals = [jnp.zeros((CY, LANES), F32)] * 2
    for plane in range(CX):
        totals = restrict_plane(cells[plane], plane, count, totals, 0)
    return [jnp.sum(t, axis=0, keepdims=True) for t in totals]


def rim_restrict(rim, count):
    n = jnp.concatenate([count, count], axis=1)
    row = iota((CY, CZ), 0)
    cells = ((row & 3) * CY + jnp.where(row < 4, CY - 1, 0)) * CZ
    member = (((cells + iota((CY, CZ), 1)) * n) >> 13) - ((cells * n) >> 13)
    lane = iota((8, LANES), 1)
    start = iota((8, LANES), 0) * 16
    spread = jnp.zeros((8, LANES), F32)
    for k in range(9):
        part = jnp.sum(jnp.where(member == k, rim, 0.0), axis=1, keepdims=True)
        spread = spread + jnp.where(lane == start + k, part, 0.0)
    return jnp.sum(spread, axis=0, keepdims=True)


def rim_exists(index):
    return jnp.where(iota((CY, CZ), 0) < 4, index, 15 - index) > 0


def prolong(entries, count):
    low = jnp.broadcast_to(entries[:, :LANES], (CY, LANES))
    high = jnp.broadcast_to(entries[:, LANES:], (CY, LANES))
    planes = []
    for plane in range(CX):
        halves = []
        for half in range(2):
            slot = slots_of(plane, half, count)
            place = slot & 127
            halves.append(jnp.where(slot < LANES, lane_take(low, place), lane_take(high, place)))
        planes.append(jnp.concatenate(halves, axis=1))
    return planes


def couple(left, mid, right, up, down):
    length = mid.shape[1]
    lane = iota(mid.shape, 1)
    behind = jnp.where(lane == 0, 0.0, pltpu.roll(mid, 1, 1))
    ahead = jnp.where(lane == length - 1, 0.0, pltpu.roll(mid, length - 1, 1))
    return 8.0 * (left + right + up + down + ahead) + 10.0 * behind


def source_kernel(
    cap, count, c_old, s_old_hbm, rate_hbm, diag, cols, off, diag_rows, order,
    c_out, ic_out, s_out, zs_out, tab, both, xb, ya, yb, pay, s_old, rate, sems,
):
    copies = []
    for x in range(CX):
        pair = (
            pltpu.make_async_copy(rate_hbm.at[:, x], rate.at[:, x], sems.at[0, x]),
            pltpu.make_async_copy(s_old_hbm.at[:, x], s_old.at[:, x], sems.at[1, x]),
        )
        for copy in pair:
            copy.start()
        copies.append(pair)
    for j in range(SHARD_ROWS // 256):
        at = slice(256 * j, 256 * j + 256)
        part = jnp.concatenate([cols[:, at].astype(F32), off[:, at] * (0.8 / diag[:, at])], axis=0)
        tab[16 * j : 16 * j + 16, :] = part
        both[16 * j : 16 * j + 16, :] = part
    place = places()
    n = jnp.full((CY, LANES), count[0], I32)
    mine = (order[0:1, :] >> 7) == place[0] * 16 + place[1]
    low = jnp.sum(jnp.where(mine, (order[...] & 127).astype(F32), 0.0), axis=1, keepdims=True)
    spot = iota((LANES, LANES), 1).astype(F32) == low
    at_place = jnp.sum(jnp.where(spot, iota((LANES, LANES), 0).astype(F32), 0.0), axis=0, keepdims=True)
    shares = [jnp.broadcast_to(cap[0:1, k : k + 1], (CY, CZ)) for k in range(RATES)]
    smooth, inverse, sources = [], [], []
    for x in range(CX):
        for copy in copies[x]:
            copy.wait()
        mass = jnp.zeros((CY, CZ), F32)
        extra = jnp.zeros((CY, CZ), F32)
        for k in range(RATES):
            r = rate[k, x]
            weighted = shares[k] * (r / (1.0 + r))
            mass = mass + weighted
            extra = extra + weighted * s_old[k, x]
        centre = (1.0 + mass) + FLOW
        source = c_old[x] + extra
        inv = 1.0 / centre
        c_out[x] = centre
        ic_out[x] = inv
        s_out[x] = source
        zs_out[x] = 0.8 * source * inv
        smooth.append(0.8 * source * inv)
        inverse.append(inv)
        sources.append(source)
    xa, xb[...] = send_planes([(smooth, 4), (inverse, 3)])
    both[TABLE_ROWS:, :] = xa
    ya[...], yb[...] = send_rows(EARLY_ROWS, lambda f, x: (smooth, inverse)[f][x])
    slot = iota((1, LANES), 1)
    sums = [jnp.where(slot + LANES * i < n[0:1], t, UNUSED) for i, t in enumerate(restrict(sources, n))]
    repeat4(pay, [*sums, diag_rows[pl.ds(place[1], 1), :], at_place])


def send_planes(fields):
    even = (places()[0] & 1) == 0
    upper = jnp.concatenate([p for planes, depth in fields for p in planes[CX - depth :]], axis=0)
    lower = jnp.concatenate([p for planes, depth in fields for p in planes[:depth]], axis=0)
    return jnp.where(even, upper, lower), jnp.where(even, lower, upper)


def ghost_rows(field, x):
    return max(0, (4, 3, 3)[field] - max(0, -x, x - CX + 1))


EARLY_ROWS = [(f, x) for f in range(2) for x in range(CX)]
LATE_ROWS = [(f, x) for f in range(3) for x in range(-3, CX + 3) if ghost_rows(f, x) and (f, x) not in EARLY_ROWS]


def row_of(rows, which):
    return sum(ghost_rows(*w) for w in rows[: rows.index(which)])


def row_count(rows):
    return sum(ghost_rows(*w) for w in rows)


def send_rows(rows, plane):
    even = (places()[1] & 1) == 0
    upper = jnp.concatenate([plane(*w)[CY - ghost_rows(*w) :] for w in rows], axis=0)
    lower = jnp.concatenate([plane(*w)[: ghost_rows(*w)] for w in rows], axis=0)
    return jnp.where(even, upper, lower), jnp.where(even, lower, upper)


def repeat4(pay, rows):
    kind = iota((8, LANES), 0) & 3
    tile = jnp.broadcast_to(rows[3], (8, LANES))
    for k in range(3):
        tile = jnp.where(kind == k, rows[k], tile)
    for i in range(DEVICES // 2):
        pay[pl.ds(8 * i, 8), :] = tile


def read_sums(gathered):
    low = gathered[pl.ds(0, DEVICES, stride=4), :]
    high = gathered[pl.ds(1, DEVICES, stride=4), :]
    diag = gathered[pl.ds(2, DEVICES, stride=4), :]
    inverse = gathered[pl.ds(3, DEVICES, stride=4), :].astype(I32)
    used = jnp.where(low < 0.5 * UNUSED, 1.0, 0.0) + jnp.where(high < 0.5 * UNUSED, 1.0, 0.0)
    return low, high, diag, inverse, jnp.sum(used, axis=1, keepdims=True)


def offsets_of(counts):
    row, lane = iota((LANES, LANES), 0), iota((LANES, LANES), 1)
    by_lane = jnp.sum(jnp.where(row < lane, counts, 0.0), axis=0, keepdims=True)
    across = jnp.sum(jnp.where(row == lane, counts, 0.0), axis=0, keepdims=True)
    by_row = jnp.sum(jnp.where(lane < row, across, 0.0), axis=1, keepdims=True)
    return jnp.broadcast_to(by_row, (LANES, LANES)).astype(I32), by_lane.astype(I32)


def blocks_of(order):
    return (iota((LANES, LANES), 0) == (order[0:1, :] >> 7)).astype(F32).astype(BF16)


def assemble(low, high, offsets, inverse, blocks):
    by_row, by_lane = offsets
    lane = iota((LANES, LANES), 1)
    shift = by_row & 127
    place = (lane - shift) & 127
    low = lane_take(low, place)
    high = lane_take(high, place)
    kept = lane >= shift
    rows = (jnp.where(kept, low, 0.0), jnp.where(kept, high, low), jnp.where(kept, 0.0, high))
    start = by_lane >> 7
    spots = [(iota((LANES, LANES), 0) == start + j).astype(F32).astype(BF16) for j in range(3)]
    parts = [jnp.concatenate(split2(r), axis=1) for r in rows]
    table = nn(jnp.concatenate(spots, axis=1), jnp.concatenate(parts, axis=0))
    by_block = nt(blocks, jnp.concatenate([table[:, :LANES], table[:, LANES:]], axis=0).astype(BF16))
    return lane_take(by_block[:, :LANES] + by_block[:, LANES:], inverse)


def one_hot(row16, index):
    return jnp.where(row16 == index.astype(BF16), jnp.ones(row16.shape, BF16), jnp.zeros(row16.shape, BF16))


def fetch(table, unknown, coarse):
    inner = unknown & (SHARD_ROWS - 1)
    shard = (unknown >> 11) ^ coarse
    row16 = iota((256, SLOTS), 0).astype(F32).astype(BF16)
    found = jnp.zeros((SHARDS * 32, SLOTS), F32)
    for chunk in range(SHARD_ROWS // 256):
        spot = one_hot(row16, (inner - chunk * 256).astype(F32))
        found = found + nn(table[:, chunk * 256 : (chunk + 1) * 256], spot)
    found = found.reshape(SHARDS, 32, SLOTS)
    picked = found[0]
    for g in range(1, SHARDS):
        picked = jnp.where(shard == g, found[g], picked)
    return picked[0:8], picked[8:16], picked[16:24] + picked[24:32]


def gatherer(values):
    high, low = split2(values.T)
    table = jnp.concatenate([high, low], axis=1)
    row = iota((LANES, SLOTS), 0).astype(F32)
    row16 = row.astype(BF16)

    def gather(block, inner):
        spot = one_hot(row16, block)
        found = nn(table, jnp.concatenate([spot, spot], axis=0))
        kept = jnp.zeros((8, SLOTS), F32)
        for b in range(0, LANES, 8):
            kept = jnp.where(row[b : b + 8] == inner, found[b : b + 8], kept)
        return kept

    return gather


def solve_entry(gather, first, parts):
    total = -1.4 * gather(first[0], first[1])
    for j in range(KC):
        total = total + parts[2][j : j + 1] * gather(parts[0][j : j + 1], parts[1][j : j + 1])
    return first[2] * total


def coarse_solve(values, plan, own):
    gather = gatherer(values)

    def column(k, total):
        first = [plan[KC, pl.ds(8 * i + k, 1), :] for i in range(3)]
        return total + solve_entry(gather, first, [plan[k, 8 * i : 8 * i + 8, :] for i in range(3)])

    total = lax.fori_loop(0, KC, column, 1.24 * gather(own[0:1, :], own[1:2, :]), unroll=SECOND_UNROLL)
    return jnp.sum(total, axis=0, keepdims=True)


def plan_rows(ref, k, parts):
    ref[k, 0:8, :] = parts[0]
    ref[k, 8:16, :] = parts[1]
    ref[k, 16:24, :] = parts[2]


def first_kernel(
    gathered, order, tab0, tab1, tab2, tab3, tab4, tab5, tab6, tab7,
    pe_out, plan, own, own_count, beside, across, at_row, at_lane, counts_out, xa, xb, table,
):
    place = places()
    me = place[0] * 16 + place[1]
    low, high, diag, inverse, counts = read_sums(gathered)
    offsets = offsets_of(counts)
    at_row[...] = offsets[0]
    at_lane[...] = jnp.broadcast_to(offsets[1], (8, LANES))
    sums = assemble(
        jnp.where(low < 0.5 * UNUSED, low, 0.0), jnp.where(high < 0.5 * UNUSED, high, 0.0),
        offsets, inverse, blocks_of(order),
    )
    values = 0.8 * sums / diag
    counts = jnp.broadcast_to(counts, (LANES, LANES))
    counts_out[...] = counts.astype(I32)
    row = iota((LANES, LANES), 0)

    def count_of(device):
        found = jnp.sum(jnp.where(row == device, counts, 0.0), axis=0, keepdims=True)
        return jnp.broadcast_to(found, (8, LANES)).astype(I32)

    n = count_of(me)
    own_count[...] = n
    beside[...] = jnp.where(iota((8, LANES), 0) < 4, count_of(me - 1), count_of(me + 1))
    across[0] = count_of(me - 16)
    across[1] = count_of(me + 16)

    tabs = (tab0, tab1, tab2, tab3, tab4, tab5, tab6, tab7)
    for g in range(SHARDS):
        for j in range(SHARD_ROWS // 256):
            at = slice(256 * j, 256 * j + 256)
            cols = tabs[g][16 * j : 16 * j + 8, :]
            big = jnp.floor(cols * (1.0 / 128.0))
            pair = jnp.concatenate([big, cols - 128.0 * big], axis=0)
            table[32 * g : 32 * g + 16, at] = pair.astype(BF16)
            off = tabs[g][16 * j + 8 : 16 * j + 16, :]
            big = off.astype(BF16).astype(F32)
            table[32 * g + 16 : 32 * g + 32, at] = jnp.concatenate([big, off - big], axis=0).astype(BF16)

    mine = jnp.sum(jnp.where(row == me, offsets[0].astype(F32), 0.0), axis=0, keepdims=True).astype(I32)
    numbers = order[...].astype(F32)
    start = mine >> 7
    lines = []
    spread = (iota((8, LANES), 1) + mine) & 127
    for j in range(3):
        line = jnp.sum(jnp.where(row == start + j, numbers, 0.0), axis=0, keepdims=True)
        lines.append(lane_take(jnp.broadcast_to(line, (8, LANES)), spread))
    inside = iota((8, LANES), 1) + (mine & 127) < LANES
    unknown = jnp.concatenate(
        [jnp.where(inside, lines[0], lines[1]), jnp.where(inside, lines[1], lines[2])], axis=1
    )[0:1].astype(I32)
    own[0:1, :] = (unknown >> 7).astype(F32)
    own[1:2, :] = (unknown & 127).astype(F32)
    plan_rows(plan, KC, fetch(table, unknown, place[0]))

    def column(k, carry):
        col = 128.0 * plan[KC, pl.ds(k, 1), :] + plan[KC, pl.ds(8 + k, 1), :]
        plan_rows(plan, k, fetch(table, col.astype(I32), place[0]))
        return carry

    lax.fori_loop(0, KC, column, 0, unroll=FIRST_UNROLL)
    pe = prolong(coarse_solve(values, plan, own), n)
    for x in range(CX):
        pe_out[x] = pe[x]

    xa[...], xb[...] = send_planes([(pe, 3)])


def below_above(index, count, a, b):
    even = (index & 1) == 0
    inner = jnp.logical_and(index > 0, index < count - 1)

    def near(i):
        if i is not ...:
            i = slice(CY * i, CY * i + CY)
        return a[i], jnp.where(inner, b[i], 0.0)

    def below(i):
        first, second = near(i)
        return jnp.where(even, second, first)

    def above(i):
        first, second = near(i)
        return jnp.where(even, first, second)

    return below, above


def with_ghosts(own, messages):
    def plane(field, x):
        if 0 <= x < CX:
            return own[field][x]
        below, above, base, depth = messages[field]
        return below(base + depth + x) if x < 0 else above(base + x - CX)

    return plane


def widen(plane, fields, ya, yb):
    even = (places()[1] & 1) == 0
    upper, lower = [], []
    for f in fields:
        for x in range(-3, CX + 3):
            d = ghost_rows(f, x)
            if d:
                here = plane(f, x)
                upper.append(here[CY - d :])
                lower.append(here[:d])
    upper, lower = jnp.concatenate(upper, axis=0), jnp.concatenate(lower, axis=0)
    ya[...] = jnp.where(even, upper, lower)
    yb[...] = jnp.where(even, lower, upper)


def all_ghosts(own, x0a, x0b, x1a, x1b):
    early = below_above(places()[0], 8, x0a.at[TABLE_ROWS:], x0b)
    late = below_above(places()[0], 8, x1a, x1b)
    return with_ghosts(own, ((*early, 0, 4), (*early, 4, 3), (*late, 0, 3)))


def widen_kernel(zs, ic, pe, x0a, x0b, x1a, x1b, ya, yb):
    plane = all_ghosts((zs, ic, pe), x0a, x0b, x1a, x1b)
    ya[...], yb[...] = send_rows(LATE_ROWS, plane)


def early_kernel(count, beside, across, zs, ic, pe, c, xa, xb, ya, yb, pay):
    place = places()
    n = count[...]
    below, above = below_above(place[0], 8, xa.at[TABLE_ROWS:], xb)
    near, far = [side(...) for side in below_above(place[1], 16, ya, yb)]
    row = iota((CY, CZ), 0)
    z1 = []
    for x in range(CX):
        mid = zs[x]
        left = zs[x - 1] if x else below(3)
        right = zs[x + 1] if x + 1 < CX else above(0)
        at = row_of(EARLY_ROWS, (0, x))
        last = at + ghost_rows(0, x) - 1
        up = jnp.where(row == 0, near[last : last + 1], pltpu.roll(mid, 1, 0))
        down = jnp.where(row == CY - 1, far[at : at + 1], pltpu.roll(mid, CY - 1, 0))
        z1.append(1.2 * mid + 0.8 * ic[x] * couple(left, mid, right, up, down) + pe[x])
    image = []
    zero = jnp.zeros((CY, CZ), F32)
    for x in range(CX):
        mid = z1[x]
        up = jnp.where(row == 0, 0.0, pltpu.roll(mid, 1, 0))
        down = jnp.where(row == CY - 1, 0.0, pltpu.roll(mid, CY - 1, 0))
        left = z1[x - 1] if x else zero
        right = z1[x + 1] if x + 1 < CX else zero
        image.append(c[x] * mid - couple(left, mid, right, up, down))
    sums = restrict(image, n)
    blank = [jnp.zeros((CY, LANES), F32)]
    lane = iota((1, LANES), 1)
    under, over = across[0], across[1]
    (down_x,) = restrict_plane(-8.0 * z1[0], CX - 1, under, blank, (3 * under) >> 2)
    (up_x,) = restrict_plane(-8.0 * z1[CX - 1], 0, over, blank, 0)
    down_x = jnp.where(place[0] > 0, jnp.sum(down_x, axis=0, keepdims=True), 0.0)
    up_x = jnp.where(place[0] < 7, jnp.sum(up_x, axis=0, keepdims=True), 0.0)
    along_x = jnp.where(lane < 64, down_x, pltpu.roll(jnp.broadcast_to(up_x, (8, LANES)), 64, 1)[0:1])
    rims = jnp.concatenate([z[0:1] for z in z1] + [z[CY - 1 : CY] for z in z1], axis=0)
    along_y = rim_restrict(jnp.where(rim_exists(place[1]), -8.0 * rims, 0.0), beside[...])
    repeat4(pay, [*sums, along_x, along_y])


def add_neighbours(low, high, from_x, from_y, counts):
    lane = iota((DEVICES, LANES), 1)

    def place(window, base, shift, length):
        nonlocal low, high
        relative = lane - base
        moved = lane_take(window, (relative + shift) & 127)
        low = low + jnp.where(jnp.logical_and(relative >= 0, relative < length), moved, 0.0)
        relative = relative + LANES
        high = high + jnp.where(jnp.logical_and(relative >= 0, relative < length), moved, 0.0)

    low = low + jnp.where(lane < 64, pltpu.roll(pltpu.roll(from_x, 16, 0), 64, 1), 0.0)
    place(pltpu.roll(from_x, DEVICES - 16, 0), (3 * counts) >> 2, 0, 64)
    both = jnp.where(lane < 64, pltpu.roll(from_y, DEVICES - 1, 0), pltpu.roll(from_y, 1, 0))
    for g in range(2 * CX):
        cells = ((g & 3) * CY + (CY - 1 if g < CX else 0)) * CZ
        place(both, (cells * counts) >> 13, 16 * g, 9)
    return low, high


def second_solve_kernel(
    count, sums, gathered, order, plan, own, at_row, at_lane, counts, pe_out, pe_face, e_face, xa, xb
):
    n = count[...]
    low, high = add_neighbours(
        sums[pl.ds(0, DEVICES, stride=4), :], sums[pl.ds(1, DEVICES, stride=4), :],
        sums[pl.ds(2, DEVICES, stride=4), :], sums[pl.ds(3, DEVICES, stride=4), :], counts[...],
    )
    diag = gathered[pl.ds(2, DEVICES, stride=4), :]
    inverse = gathered[pl.ds(3, DEVICES, stride=4), :].astype(I32)
    values = assemble(low, high, (at_row[...], at_lane[0:1, :]), inverse, blocks_of(order))
    entries = coarse_solve(0.8 * values / diag, plan, own)
    pe = prolong(entries, n)
    for x in range(CX):
        pe_out[x] = pe[x]
        pe_face[x : x + 1, :] = pe[x][0:1]
        pe_face[CX + x : CX + x + 1, :] = pe[x][CY - 1 : CY]
    xa[...], xb[...] = send_planes([(pe, 1)])
    lane = iota((8, LANES), 1)
    group = lane >> 4
    cells = ((group & 3) * CY + jnp.where(group < 4, 0, CY - 1)) * CZ
    slot = jnp.minimum(((cells * n) >> 13) + (lane & 15), SLOTS - 1)
    low = jnp.broadcast_to(entries[:, :LANES], (8, LANES))
    high = jnp.broadcast_to(entries[:, LANES:], (8, LANES))
    e_face[...] = jnp.where(slot < LANES, lane_take(low, slot & 127), lane_take(high, slot & 127))


def direction_kernel(
    zs, ic, pe, c, x0a, x0b, x1a, x1b, y0a, y0b, y1a, y1b, after,
    z1_out, w1_out, sw_out, sw_beside, sw_ghost, s_ghost, w_ghost,
):
    place = places()
    middle = all_ghosts((zs, ic, pe), x0a, x0b, x1a, x1b)
    early = [side(...) for side in below_above(place[1], 16, y0a, y0b)]
    late = [side(...) for side in below_above(place[1], 16, y1a, y1b)]

    def plane(field, x):
        d = ghost_rows(field, x)
        here = middle(field, x)
        if not d:
            blank = jnp.zeros((8, CZ), F32)
            return jnp.concatenate([blank, here, blank], axis=0)
        rows, (near, far) = (EARLY_ROWS, early) if (field, x) in EARLY_ROWS else (LATE_ROWS, late)
        at = row_of(rows, (field, x))
        blank = jnp.zeros((8 - d, CZ), F32)
        return jnp.concatenate([blank, near[at : at + d], here, far[at : at + d], blank], axis=0)

    def neighbours(get, x):
        mid = get(x)
        count = mid.shape[0]
        return couple(get(x - 1), mid, get(x + 1), pltpu.roll(mid, 1, 0), pltpu.roll(mid, count - 1, 0))

    z = {x: plane(0, x) for x in range(-4, CX + 4)}
    inv = {x: plane(1, x) for x in range(-3, CX + 3)}
    first = {}
    for x in range(-3, CX + 3):
        first[x] = 1.2 * z[x] + 0.8 * inv[x] * neighbours(z.get, x) + plane(2, x)
    zw = {}
    for x in range(-2, CX + 2):
        beside = neighbours(first.get, x)
        zw[x] = 0.8 * (first[x] - inv[x] * beside)
        if 0 <= x < CX:
            z1_out[x] = first[x][8:16]
            w1_out[x] = c[x] * first[x][8:16] - beside[8:16]
    for x in range(-1, CX + 1):
        smooth = 1.2 * zw[x] + 0.8 * inv[x] * neighbours(zw.get, x)
        if not 0 <= x < CX:
            sw_beside[0 if x < 0 else 1] = smooth[8:16]
            continue
        sw_out[x] = smooth[8:16]
        for at, row in ((x, 7), (CX + x, 16)):
            iv = inv[x][row : row + 1]
            scale = jnp.where(iv > 0.0, 1.25 / jnp.where(iv > 0.0, iv, 1.0), 0.0)
            sw_ghost[at : at + 1, :] = smooth[row : row + 1]
            s_ghost[at : at + 1, :] = z[x][row : row + 1] * scale
            w_ghost[at : at + 1, :] = zw[x][row : row + 1] * scale


def products_kernel(
    s, w1, sw, pe2, c, xa, xb, sw_beside, sw_ghost, s_ghost, w_ghost, pe_face, e_face, beside, pay
):
    place = places()
    below, above = [side(...) for side in below_above(place[0], 8, xa, xb)]
    sums = [jnp.zeros((CY, CZ), F32) for _ in range(6)]
    row = iota((CY, CZ), 0)
    rims = [None] * (2 * CX)
    p = [below + sw_beside[0], *(sw[x] + pe2[x] for x in range(CX)), above + sw_beside[1]]
    for x in range(CX):
        left, mid, right = p[x : x + 3]
        up = jnp.where(row == 0, sw_ghost[x : x + 1, :], pltpu.roll(mid, 1, 0))
        down = jnp.where(row == CY - 1, sw_ghost[CX + x : CX + x + 1, :], pltpu.roll(mid, CY - 1, 0))
        q = c[x] * mid - couple(left, mid, right, up, down)
        rims[x], rims[CX + x] = q[0:1], q[CY - 1 : CY]
        a, b = s[x], w1[x]
        for k, term in enumerate((a * a, a * b, a * q, b * b, b * q, q * q)):
            sums[k] = sums[k] + term
    exists = rim_exists(place[1])
    face = pe_face[...]
    sums[2] = sums[2] - 8.0 * face * s_ghost[...]
    sums[4] = sums[4] - 8.0 * face * w_ghost[...]
    sums[5] = sums[5] + jnp.where(exists, 64.0 * face * face, 0.0)
    rim = jnp.where(exists, jnp.concatenate(rims, axis=0), 0.0)
    lane = iota((8, LANES), 1)
    top = jnp.broadcast_to(rim_restrict(rim, beside[...]), (8, LANES))
    for k in range(6):
        top = top + jnp.where(lane == 9 + k, jnp.sum(sums[k], keepdims=True), 0.0)
    tile = jnp.where((iota((8, LANES), 0) & 1) == 0, top, e_face[...])
    for i in range(DEVICES // 4):
        pay[pl.ds(8 * i, 8), :] = tile


def update_kernel(parts, z1, smooth, pe2, s_old, rate, mobile, immobile):
    top = parts[pl.ds(0, DEVICES, stride=2), :]
    face = pltpu.roll(parts[pl.ds(1, DEVICES, stride=2), :], LANES // 2, 1)
    lane = iota((DEVICES, LANES), 1)
    other = jnp.where(lane < LANES // 2, pltpu.roll(face, 1, 0), pltpu.roll(face, DEVICES - 1, 0))
    cross = jnp.sum(jnp.where((lane & 15) < 9, top * other, 0.0), keepdims=True)
    total = jnp.sum(top, axis=0, keepdims=True)
    ss, sw, sq, ww, wq, qq = [total[:, 9 + k : 10 + k] for k in range(6)]
    qq = qq - 16.0 * cross
    factor = wq / ww
    y2 = (sq - factor * sw) / (qq - factor * wq)
    y1 = (sw - wq * y2) / ww
    for x in range(CX):
        new = y1 * z1[x] + y2 * (smooth[x] + pe2[x])
        mobile[x] = new
        for k in range(RATES):
            r = rate[k, x]
            immobile[k, x] = (s_old[k, x] + r * new) / (1.0 + r)


def call(kernel, ins, outs, scratch=(), flops=10_000, vmem=48 << 20):
    shapes = [jax.ShapeDtypeStruct(shape, dtype) for shape, dtype in outs]
    return pl.pallas_call(
        kernel,
        out_shape=shapes,
        in_specs=ins,
        out_specs=[VM] * len(shapes),
        scratch_shapes=list(scratch),
        cost_estimate=pl.CostEstimate(flops=flops, bytes_accessed=100_000, transcendentals=0),
        compiler_params=pltpu.CompilerParams(vmem_limit_bytes=vmem),
    )


FIELD = ((CX, CY, CZ), F32)
SOURCE_VMEM = 63 << 20
FIRST_UNROLL = 8
SECOND_UNROLL = 8


def swap_pairs(axis):
    n, m = lax.axis_size("coarse"), lax.axis_size("fine")
    inside, between = [], []
    for c in range(n):
        for f in range(m):
            me = c * m + f
            at, count, step = (c, n, m) if axis == "coarse" else (f, m, 1)
            inside.append((me, me + ((at ^ 1) - at) * step))
            if 0 < at < count - 1:
                between.append((me, me + (((at - 1) ^ 1) + 1 - at) * step))
            elif axis == "fine":
                between.append((me, (c ^ 1) * m + f))
            else:
                between.append((me, (n - 1 - c) * m + f))
    return inside, between


def swap_between(b, axis):
    return lax.ppermute(b, BOTH, swap_pairs(axis)[1])


def trade(a, b, axis):
    b = swap_between(b, axis)
    return lax.ppermute(a, BOTH, swap_pairs(axis)[0]), b


def everyone(pay, rows):
    moved = lax.all_to_all(pay.reshape(DEVICES, rows, LANES), BOTH, 0, 0)
    return moved.reshape(DEVICES * rows, LANES)


def local(
    c_old, s_old, rate_time, capacity, agg_count, coarse_order, coarse_cols, coarse_off, coarse_diag
):
    order = coarse_order.reshape(LANES, LANES)
    c, ic, s, zs, tab, both, x0b, y0a, y0b, pay = call(
        source_kernel, [VM, SM, VM, HB, HB] + [VM] * 5,
        [
            FIELD, FIELD, FIELD, FIELD, ((TABLE_ROWS, 256), F32), ((TABLE_ROWS + 7 * CY, 256), F32),
            ((7 * CY, CZ), F32), ((row_count(EARLY_ROWS), CZ), F32), ((row_count(EARLY_ROWS), CZ), F32),
            ((4 * DEVICES, LANES), F32),
        ],
        scratch=[
            pltpu.VMEM((RATES, CX, CY, CZ), F32),
            pltpu.VMEM((RATES, CX, CY, CZ), F32),
            pltpu.SemaphoreType.DMA((2, CX)),
        ],
        vmem=SOURCE_VMEM,
    )(
        capacity.reshape(1, RATES), agg_count, c_old, s_old, rate_time, coarse_diag.reshape(1, SHARD_ROWS), coarse_cols, coarse_off,
        coarse_diag.reshape(16, LANES), order,
    )
    other_core = [(i, i ^ 1) for i in range(8)]
    both = lax.ppermute(both, "coarse", other_core)
    tabs = [tab, both]
    for hop in (2, 4, 6):
        shard = lax.ppermute(tab, "coarse", [(i, i ^ hop) for i in range(8)])
        tabs += [shard, lax.ppermute(shard, "coarse", other_core)]
    x0b = swap_between(x0b, "coarse")
    y0a, y0b = trade(y0a, y0b, "fine")
    pay, x0b = lax.optimization_barrier((pay, x0b))
    gathered = everyone(pay, 4)

    pe, plan, own, own_count, beside, across, at_row, at_lane, counts, x1a, x1b = call(
        first_kernel, [VM] * 10,
        [
            FIELD, ((KC + 1, 24, SLOTS), F32), ((8, SLOTS), F32), ((8, LANES), I32), ((8, LANES), I32), ((2, 8, LANES), I32),
            ((LANES, LANES), I32), ((8, LANES), I32), ((LANES, LANES), I32),
            ((3 * CY, CZ), F32), ((3 * CY, CZ), F32),
        ],
        scratch=[pltpu.VMEM((SHARDS * 32, SHARD_ROWS), BF16)],
    )(gathered, order, *tabs)
    x1a, x1b = trade(x1a, x1b, "coarse")
    (pay,) = call(early_kernel, [VM] * 11, [((4 * DEVICES, LANES), F32)])(
        own_count, beside, across, zs, ic, pe, c, both, x0b, y0a, y0b
    )
    sums = everyone(pay, 4)
    y1a, y1b = call(widen_kernel, [VM] * 7, [((row_count(LATE_ROWS), CZ), F32)] * 2)(
        zs, ic, pe, both, x0b, x1a, x1b
    )
    y1a, y1b = trade(y1a, y1b, "fine")

    pe2, pe_face, e_face, xa, xb = call(
        second_solve_kernel, [VM] * 9,
        [FIELD, ((CY, CZ), F32), ((8, LANES), F32), ((CY, CZ), F32), ((CY, CZ), F32)], flops=100_000_000,
    )(own_count, sums, gathered, order, plan, own, at_row, at_lane, counts)
    xa, xb = trade(xa, xb, "coarse")
    z1, w1, sw, sw_beside, sw_ghost, s_ghost, w_ghost = call(
        direction_kernel, [VM] * 13, [FIELD, FIELD, FIELD, ((2, CY, CZ), F32)] + [((CY, CZ), F32)] * 3,
    )(zs, ic, pe, c, both, x0b, x1a, x1b, y0a, y0b, y1a, y1b, e_face)
    (pay,) = call(
        products_kernel, [VM] * 14, [((2 * DEVICES, LANES), F32)]
    )(s, w1, sw, pe2, c, xa, xb, sw_beside, sw_ghost, s_ghost, w_ghost, pe_face, e_face, beside)
    parts = everyone(pay, 2)
    mobile, immobile = call(
        update_kernel, [VM] * 6, [FIELD, ((RATES, CX, CY, CZ), F32)]
    )(parts, z1, sw, pe2, s_old, rate_time)
    return mobile, immobile


def solution(mesh):
    return jax.shard_map(
        local,
        mesh=mesh,
        in_specs=(
            P("coarse", "fine", None),
            P(None, "coarse", "fine", None),
            P(None, "coarse", "fine", None),
            P(),
            P(("coarse", "fine")),
            P(),
            P(None, "coarse"),
            P(None, "coarse"),
            P("coarse"),
        ),
        out_specs=(P("coarse", "fine", None), P(None, "coarse", "fine", None)),
        check_vma=False,
    )
```

```python
import jax
import jax.numpy as jnp
from jax import lax
from jax.experimental import pallas as pl
from jax.experimental.pallas import tpu as pltpu
from jax.sharding import PartitionSpec as P

BOTH = ("coarse", "fine")
CX, CY, CZ = 4, 8, 256
RATES = 16
KC = 8
DEVICES = 128
LANES = 128
SLOTS = 256
SHARDS = 8
SHARD_ROWS = 2048
FLOW = 50.0
TABLE_ROWS = 128
UNUSED = 1e30
F32, BF16, I32 = jnp.float32, jnp.bfloat16, jnp.int32
VM = pl.BlockSpec(memory_space=pltpu.VMEM)
SM = pl.BlockSpec(memory_space=pltpu.SMEM)
HB = pl.BlockSpec(memory_space=pltpu.HBM)


def places():
    return lax.axis_index("coarse").astype(I32), lax.axis_index("fine").astype(I32)


def iota(shape, dim):
    return lax.broadcasted_iota(I32, shape, dim)


def lane_take(table, index):
    return jnp.take_along_axis(table, index, axis=1, mode="promise_in_bounds")


def nt(left, right):
    return lax.dot_general(left, right, (((1,), (1,)), ((), ())), preferred_element_type=F32)


def nn(left, right):
    return jnp.dot(left, right, preferred_element_type=F32)


def split2(values):
    high = values.astype(BF16)
    return high, (values - high.astype(F32)).astype(BF16)


def slots_of(plane, half, count):
    row = (plane * CY + iota((CY, LANES), 0)) * 2 + half
    return ((row * LANES + iota((CY, LANES), 1)) * count) >> 13


def restrict_plane(values, plane, count, totals, base):
    lane = iota((CY, LANES), 1)
    for half in range(2):
        part_of = values[:, half * LANES : (half + 1) * LANES]
        row = (plane * CY + iota((CY, LANES), 0)) * 2 + half
        first = (row * count) >> 6
        member = slots_of(plane, half, count) - first
        relative = lane + (base - first)
        for k in range(5):
            part = jnp.sum(jnp.where(member == k, part_of, 0.0), axis=1, keepdims=True)
            totals = [t + jnp.where(relative == k - LANES * i, part, 0.0) for i, t in enumerate(totals)]
    return totals


def restrict(cells, count):
    totals = [jnp.zeros((CY, LANES), F32)] * 2
    for plane in range(CX):
        totals = restrict_plane(cells[plane], plane, count, totals, 0)
    return [jnp.sum(t, axis=0, keepdims=True) for t in totals]


def rim_restrict(rim, count):
    n = jnp.concatenate([count, count], axis=1)
    row = iota((CY, CZ), 0)
    cells = ((row & 3) * CY + jnp.where(row < 4, CY - 1, 0)) * CZ
    member = (((cells + iota((CY, CZ), 1)) * n) >> 13) - ((cells * n) >> 13)
    lane = iota((8, LANES), 1)
    start = iota((8, LANES), 0) * 16
    spread = jnp.zeros((8, LANES), F32)
    for k in range(9):
        part = jnp.sum(jnp.where(member == k, rim, 0.0), axis=1, keepdims=True)
        spread = spread + jnp.where(lane == start + k, part, 0.0)
    return jnp.sum(spread, axis=0, keepdims=True)


def rim_exists(index):
    return jnp.where(iota((CY, CZ), 0) < 4, index, 15 - index) > 0


def prolong(entries, count):
    low = jnp.broadcast_to(entries[:, :LANES], (CY, LANES))
    high = jnp.broadcast_to(entries[:, LANES:], (CY, LANES))
    planes = []
    for plane in range(CX):
        halves = []
        for half in range(2):
            slot = slots_of(plane, half, count)
            place = slot & 127
            halves.append(jnp.where(slot < LANES, lane_take(low, place), lane_take(high, place)))
        planes.append(jnp.concatenate(halves, axis=1))
    return planes


def couple(left, mid, right, up, down):
    length = mid.shape[1]
    lane = iota(mid.shape, 1)
    behind = jnp.where(lane == 0, 0.0, pltpu.roll(mid, 1, 1))
    ahead = jnp.where(lane == length - 1, 0.0, pltpu.roll(mid, length - 1, 1))
    return 8.0 * (left + right + up + down + ahead) + 10.0 * behind


def source_kernel(
    cap, count, c_old, s_old_hbm, rate_hbm, diag, cols, off, diag_rows, order,
    c_out, ic_out, s_out, zs_out, tab, both, xb, ya, yb, pay, s_old, rate, sems,
):
    copies = []
    for x in range(CX):
        pair = (
            pltpu.make_async_copy(rate_hbm.at[:, x], rate.at[:, x], sems.at[0, x]),
            pltpu.make_async_copy(s_old_hbm.at[:, x], s_old.at[:, x], sems.at[1, x]),
        )
        for copy in pair:
            copy.start()
        copies.append(pair)
    for j in range(SHARD_ROWS // 256):
        at = slice(256 * j, 256 * j + 256)
        part = jnp.concatenate([cols[:, at].astype(F32), off[:, at] * (0.8 / diag[:, at])], axis=0)
        tab[16 * j : 16 * j + 16, :] = part
        both[16 * j : 16 * j + 16, :] = part
    place = places()
    n = jnp.full((CY, LANES), count[0], I32)
    mine = (order[0:1, :] >> 7) == place[0] * 16 + place[1]
    low = jnp.sum(jnp.where(mine, (order[...] & 127).astype(F32), 0.0), axis=1, keepdims=True)
    spot = iota((LANES, LANES), 1).astype(F32) == low
    at_place = jnp.sum(jnp.where(spot, iota((LANES, LANES), 0).astype(F32), 0.0), axis=0, keepdims=True)
    shares = [jnp.broadcast_to(cap[0:1, k : k + 1], (CY, CZ)) for k in range(RATES)]
    smooth, inverse, sources = [], [], []
    for x in range(CX):
        for copy in copies[x]:
            copy.wait()
        mass = jnp.zeros((CY, CZ), F32)
        extra = jnp.zeros((CY, CZ), F32)
        for k in range(RATES):
            r = rate[k, x]
            weighted = shares[k] * (r / (1.0 + r))
            mass = mass + weighted
            extra = extra + weighted * s_old[k, x]
        centre = (1.0 + mass) + FLOW
        source = c_old[x] + extra
        inv = 1.0 / centre
        c_out[x] = centre
        ic_out[x] = inv
        s_out[x] = source
        zs_out[x] = 0.8 * source * inv
        smooth.append(0.8 * source * inv)
        inverse.append(inv)
        sources.append(source)
    xa, xb[...] = send_planes([(smooth, 4), (inverse, 3)])
    both[TABLE_ROWS:, :] = xa
    ya[...], yb[...] = send_rows(EARLY_ROWS, lambda f, x: (smooth, inverse)[f][x])
    slot = iota((1, LANES), 1)
    sums = [jnp.where(slot + LANES * i < n[0:1], t, UNUSED) for i, t in enumerate(restrict(sources, n))]
    repeat4(pay, [*sums, diag_rows[pl.ds(place[1], 1), :], at_place])


def send_planes(fields):
    even = (places()[0] & 1) == 0
    upper = jnp.concatenate([p for planes, depth in fields for p in planes[CX - depth :]], axis=0)
    lower = jnp.concatenate([p for planes, depth in fields for p in planes[:depth]], axis=0)
    return jnp.where(even, upper, lower), jnp.where(even, lower, upper)


def ghost_rows(field, x):
    return max(0, (4, 3, 3)[field] - max(0, -x, x - CX + 1))


EARLY_ROWS = [(f, x) for f in range(2) for x in range(CX)]
LATE_ROWS = [(f, x) for f in range(3) for x in range(-3, CX + 3) if ghost_rows(f, x) and (f, x) not in EARLY_ROWS]


def row_of(rows, which):
    return sum(ghost_rows(*w) for w in rows[: rows.index(which)])


def row_count(rows):
    return sum(ghost_rows(*w) for w in rows)


def send_rows(rows, plane):
    even = (places()[1] & 1) == 0
    upper = jnp.concatenate([plane(*w)[CY - ghost_rows(*w) :] for w in rows], axis=0)
    lower = jnp.concatenate([plane(*w)[: ghost_rows(*w)] for w in rows], axis=0)
    return jnp.where(even, upper, lower), jnp.where(even, lower, upper)


def repeat4(pay, rows):
    kind = iota((8, LANES), 0) & 3
    tile = jnp.broadcast_to(rows[3], (8, LANES))
    for k in range(3):
        tile = jnp.where(kind == k, rows[k], tile)
    for i in range(DEVICES // 2):
        pay[pl.ds(8 * i, 8), :] = tile


def read_sums(gathered):
    low = gathered[pl.ds(0, DEVICES, stride=4), :]
    high = gathered[pl.ds(1, DEVICES, stride=4), :]
    diag = gathered[pl.ds(2, DEVICES, stride=4), :]
    inverse = gathered[pl.ds(3, DEVICES, stride=4), :].astype(I32)
    used = jnp.where(low < 0.5 * UNUSED, 1.0, 0.0) + jnp.where(high < 0.5 * UNUSED, 1.0, 0.0)
    return low, high, diag, inverse, jnp.sum(used, axis=1, keepdims=True)


def offsets_of(counts):
    row, lane = iota((LANES, LANES), 0), iota((LANES, LANES), 1)
    by_lane = jnp.sum(jnp.where(row < lane, counts, 0.0), axis=0, keepdims=True)
    across = jnp.sum(jnp.where(row == lane, counts, 0.0), axis=0, keepdims=True)
    by_row = jnp.sum(jnp.where(lane < row, across, 0.0), axis=1, keepdims=True)
    return jnp.broadcast_to(by_row, (LANES, LANES)).astype(I32), by_lane.astype(I32)


def blocks_of(order):
    return (iota((LANES, LANES), 0) == (order[0:1, :] >> 7)).astype(F32).astype(BF16)


def assemble(low, high, offsets, inverse, blocks):
    by_row, by_lane = offsets
    lane = iota((LANES, LANES), 1)
    shift = by_row & 127
    place = (lane - shift) & 127
    low = lane_take(low, place)
    high = lane_take(high, place)
    kept = lane >= shift
    rows = (jnp.where(kept, low, 0.0), jnp.where(kept, high, low), jnp.where(kept, 0.0, high))
    start = by_lane >> 7
    spots = [(iota((LANES, LANES), 0) == start + j).astype(F32).astype(BF16) for j in range(3)]
    parts = [jnp.concatenate(split2(r), axis=1) for r in rows]
    table = nn(jnp.concatenate(spots, axis=1), jnp.concatenate(parts, axis=0))
    by_block = nt(blocks, jnp.concatenate([table[:, :LANES], table[:, LANES:]], axis=0).astype(BF16))
    return lane_take(by_block[:, :LANES] + by_block[:, LANES:], inverse)


def one_hot(row16, index):
    return jnp.where(row16 == index.astype(BF16), jnp.ones(row16.shape, BF16), jnp.zeros(row16.shape, BF16))


def fetch(table, unknown, coarse):
    inner = unknown & (SHARD_ROWS - 1)
    shard = (unknown >> 11) ^ coarse
    row16 = iota((256, SLOTS), 0).astype(F32).astype(BF16)
    found = jnp.zeros((SHARDS * 32, SLOTS), F32)
    for chunk in range(SHARD_ROWS // 256):
        spot = one_hot(row16, (inner - chunk * 256).astype(F32))
        found = found + nn(table[:, chunk * 256 : (chunk + 1) * 256], spot)
    found = found.reshape(SHARDS, 32, SLOTS)
    picked = found[0]
    for g in range(1, SHARDS):
        picked = jnp.where(shard == g, found[g], picked)
    return picked[0:8], picked[8:16], picked[16:24] + picked[24:32]


def gatherer(values):
    high, low = split2(values.T)
    table = jnp.concatenate([high, low], axis=1)
    row = iota((LANES, SLOTS), 0).astype(F32)
    row16 = row.astype(BF16)

    def gather(block, inner):
        spot = one_hot(row16, block)
        found = nn(table, jnp.concatenate([spot, spot], axis=0))
        kept = jnp.zeros((8, SLOTS), F32)
        for b in range(0, LANES, 8):
            kept = jnp.where(row[b : b + 8] == inner, found[b : b + 8], kept)
        return kept

    return gather


def solve_entry(gather, first, parts):
    total = -1.4 * gather(first[0], first[1])
    for j in range(KC):
        total = total + parts[2][j : j + 1] * gather(parts[0][j : j + 1], parts[1][j : j + 1])
    return first[2] * total


def coarse_solve(values, plan, own):
    gather = gatherer(values)

    def column(k, total):
        first = [plan[KC, pl.ds(8 * i + k, 1), :] for i in range(3)]
        return total + solve_entry(gather, first, [plan[k, 8 * i : 8 * i + 8, :] for i in range(3)])

    total = lax.fori_loop(0, KC, column, 1.24 * gather(own[0:1, :], own[1:2, :]), unroll=SECOND_UNROLL)
    return jnp.sum(total, axis=0, keepdims=True)


def plan_rows(ref, k, parts):
    ref[k, 0:8, :] = parts[0]
    ref[k, 8:16, :] = parts[1]
    ref[k, 16:24, :] = parts[2]


def first_kernel(
    gathered, order, tab0, tab1, tab2, tab3, tab4, tab5, tab6, tab7,
    pe_out, plan, own, own_count, beside, across, at_row, at_lane, counts_out, xa, xb, table,
):
    place = places()
    me = place[0] * 16 + place[1]
    low, high, diag, inverse, counts = read_sums(gathered)
    offsets = offsets_of(counts)
    at_row[...] = offsets[0]
    at_lane[...] = jnp.broadcast_to(offsets[1], (8, LANES))
    sums = assemble(
        jnp.where(low < 0.5 * UNUSED, low, 0.0), jnp.where(high < 0.5 * UNUSED, high, 0.0),
        offsets, inverse, blocks_of(order),
    )
    values = 0.8 * sums / diag
    counts = jnp.broadcast_to(counts, (LANES, LANES))
    counts_out[...] = counts.astype(I32)
    row = iota((LANES, LANES), 0)

    def count_of(device):
        found = jnp.sum(jnp.where(row == device, counts, 0.0), axis=0, keepdims=True)
        return jnp.broadcast_to(found, (8, LANES)).astype(I32)

    n = count_of(me)
    own_count[...] = n
    beside[...] = jnp.where(iota((8, LANES), 0) < 4, count_of(me - 1), count_of(me + 1))
    across[0] = count_of(me - 16)
    across[1] = count_of(me + 16)

    tabs = (tab0, tab1, tab2, tab3, tab4, tab5, tab6, tab7)
    for g in range(SHARDS):
        for j in range(SHARD_ROWS // 256):
            at = slice(256 * j, 256 * j + 256)
            cols = tabs[g][16 * j : 16 * j + 8, :]
            big = jnp.floor(cols * (1.0 / 128.0))
            pair = jnp.concatenate([big, cols - 128.0 * big], axis=0)
            table[32 * g : 32 * g + 16, at] = pair.astype(BF16)
            off = tabs[g][16 * j + 8 : 16 * j + 16, :]
            big = off.astype(BF16).astype(F32)
            table[32 * g + 16 : 32 * g + 32, at] = jnp.concatenate([big, off - big], axis=0).astype(BF16)

    mine = jnp.sum(jnp.where(row == me, offsets[0].astype(F32), 0.0), axis=0, keepdims=True).astype(I32)
    numbers = order[...].astype(F32)
    start = mine >> 7
    lines = []
    spread = (iota((8, LANES), 1) + mine) & 127
    for j in range(3):
        line = jnp.sum(jnp.where(row == start + j, numbers, 0.0), axis=0, keepdims=True)
        lines.append(lane_take(jnp.broadcast_to(line, (8, LANES)), spread))
    inside = iota((8, LANES), 1) + (mine & 127) < LANES
    unknown = jnp.concatenate(
        [jnp.where(inside, lines[0], lines[1]), jnp.where(inside, lines[1], lines[2])], axis=1
    )[0:1].astype(I32)
    own[0:1, :] = (unknown >> 7).astype(F32)
    own[1:2, :] = (unknown & 127).astype(F32)
    plan_rows(plan, KC, fetch(table, unknown, place[0]))

    def column(k, carry):
        col = 128.0 * plan[KC, pl.ds(k, 1), :] + plan[KC, pl.ds(8 + k, 1), :]
        plan_rows(plan, k, fetch(table, col.astype(I32), place[0]))
        return carry

    lax.fori_loop(0, KC, column, 0, unroll=FIRST_UNROLL)
    pe = prolong(coarse_solve(values, plan, own), n)
    for x in range(CX):
        pe_out[x] = pe[x]

    xa[...], xb[...] = send_planes([(pe, 3)])


def below_above(index, count, a, b):
    even = (index & 1) == 0
    inner = jnp.logical_and(index > 0, index < count - 1)

    def near(i):
        if i is not ...:
            i = slice(CY * i, CY * i + CY)
        return a[i], jnp.where(inner, b[i], 0.0)

    def below(i):
        first, second = near(i)
        return jnp.where(even, second, first)

    def above(i):
        first, second = near(i)
        return jnp.where(even, first, second)

    return below, above


def with_ghosts(own, messages):
    def plane(field, x):
        if 0 <= x < CX:
            return own[field][x]
        below, above, base, depth = messages[field]
        return below(base + depth + x) if x < 0 else above(base + x - CX)

    return plane


def widen(plane, fields, ya, yb):
    even = (places()[1] & 1) == 0
    upper, lower = [], []
    for f in fields:
        for x in range(-3, CX + 3):
            d = ghost_rows(f, x)
            if d:
                here = plane(f, x)
                upper.append(here[CY - d :])
                lower.append(here[:d])
    upper, lower = jnp.concatenate(upper, axis=0), jnp.concatenate(lower, axis=0)
    ya[...] = jnp.where(even, upper, lower)
    yb[...] = jnp.where(even, lower, upper)


def all_ghosts(own, x0a, x0b, x1a, x1b):
    early = below_above(places()[0], 8, x0a.at[TABLE_ROWS:], x0b)
    late = below_above(places()[0], 8, x1a, x1b)
    return with_ghosts(own, ((*early, 0, 4), (*early, 4, 3), (*late, 0, 3)))


def widen_kernel(zs, ic, pe, x0a, x0b, x1a, x1b, ya, yb):
    plane = all_ghosts((zs, ic, pe), x0a, x0b, x1a, x1b)
    ya[...], yb[...] = send_rows(LATE_ROWS, plane)


def early_kernel(count, beside, across, zs, ic, pe, c, xa, xb, ya, yb, pay):
    place = places()
    n = count[...]
    below, above = below_above(place[0], 8, xa.at[TABLE_ROWS:], xb)
    near, far = [side(...) for side in below_above(place[1], 16, ya, yb)]
    row = iota((CY, CZ), 0)
    z1 = []
    for x in range(CX):
        mid = zs[x]
        left = zs[x - 1] if x else below(3)
        right = zs[x + 1] if x + 1 < CX else above(0)
        at = row_of(EARLY_ROWS, (0, x))
        last = at + ghost_rows(0, x) - 1
        up = jnp.where(row == 0, near[last : last + 1], pltpu.roll(mid, 1, 0))
        down = jnp.where(row == CY - 1, far[at : at + 1], pltpu.roll(mid, CY - 1, 0))
        z1.append(1.2 * mid + 0.8 * ic[x] * couple(left, mid, right, up, down) + pe[x])
    image = []
    zero = jnp.zeros((CY, CZ), F32)
    for x in range(CX):
        mid = z1[x]
        up = jnp.where(row == 0, 0.0, pltpu.roll(mid, 1, 0))
        down = jnp.where(row == CY - 1, 0.0, pltpu.roll(mid, CY - 1, 0))
        left = z1[x - 1] if x else zero
        right = z1[x + 1] if x + 1 < CX else zero
        image.append(c[x] * mid - couple(left, mid, right, up, down))
    sums = restrict(image, n)
    blank = [jnp.zeros((CY, LANES), F32)]
    lane = iota((1, LANES), 1)
    under, over = across[0], across[1]
    (down_x,) = restrict_plane(-8.0 * z1[0], CX - 1, under, blank, (3 * under) >> 2)
    (up_x,) = restrict_plane(-8.0 * z1[CX - 1], 0, over, blank, 0)
    down_x = jnp.where(place[0] > 0, jnp.sum(down_x, axis=0, keepdims=True), 0.0)
    up_x = jnp.where(place[0] < 7, jnp.sum(up_x, axis=0, keepdims=True), 0.0)
    along_x = jnp.where(lane < 64, down_x, pltpu.roll(jnp.broadcast_to(up_x, (8, LANES)), 64, 1)[0:1])
    rims = jnp.concatenate([z[0:1] for z in z1] + [z[CY - 1 : CY] for z in z1], axis=0)
    along_y = rim_restrict(jnp.where(rim_exists(place[1]), -8.0 * rims, 0.0), beside[...])
    repeat4(pay, [*sums, along_x, along_y])


def add_neighbours(low, high, from_x, from_y, counts):
    lane = iota((DEVICES, LANES), 1)

    def place(window, base, shift, length):
        nonlocal low, high
        relative = lane - base
        moved = lane_take(window, (relative + shift) & 127)
        low = low + jnp.where(jnp.logical_and(relative >= 0, relative < length), moved, 0.0)
        relative = relative + LANES
        high = high + jnp.where(jnp.logical_and(relative >= 0, relative < length), moved, 0.0)

    low = low + jnp.where(lane < 64, pltpu.roll(pltpu.roll(from_x, 16, 0), 64, 1), 0.0)
    place(pltpu.roll(from_x, DEVICES - 16, 0), (3 * counts) >> 2, 0, 64)
    both = jnp.where(lane < 64, pltpu.roll(from_y, DEVICES - 1, 0), pltpu.roll(from_y, 1, 0))
    for g in range(2 * CX):
        cells = ((g & 3) * CY + (CY - 1 if g < CX else 0)) * CZ
        place(both, (cells * counts) >> 13, 16 * g, 9)
    return low, high


def second_solve_kernel(
    count, sums, gathered, order, plan, own, at_row, at_lane, counts, pe_out, pe_face, e_face, xa, xb
):
    n = count[...]
    low, high = add_neighbours(
        sums[pl.ds(0, DEVICES, stride=4), :], sums[pl.ds(1, DEVICES, stride=4), :],
        sums[pl.ds(2, DEVICES, stride=4), :], sums[pl.ds(3, DEVICES, stride=4), :], counts[...],
    )
    diag = gathered[pl.ds(2, DEVICES, stride=4), :]
    inverse = gathered[pl.ds(3, DEVICES, stride=4), :].astype(I32)
    values = assemble(low, high, (at_row[...], at_lane[0:1, :]), inverse, blocks_of(order))
    entries = coarse_solve(0.8 * values / diag, plan, own)
    pe = prolong(entries, n)
    for x in range(CX):
        pe_out[x] = pe[x]
        pe_face[x : x + 1, :] = pe[x][0:1]
        pe_face[CX + x : CX + x + 1, :] = pe[x][CY - 1 : CY]
    xa[...], xb[...] = send_planes([(pe, 1)])
    lane = iota((8, LANES), 1)
    group = lane >> 4
    cells = ((group & 3) * CY + jnp.where(group < 4, 0, CY - 1)) * CZ
    slot = jnp.minimum(((cells * n) >> 13) + (lane & 15), SLOTS - 1)
    low = jnp.broadcast_to(entries[:, :LANES], (8, LANES))
    high = jnp.broadcast_to(entries[:, LANES:], (8, LANES))
    e_face[...] = jnp.where(slot < LANES, lane_take(low, slot & 127), lane_take(high, slot & 127))


def direction_kernel(
    zs, ic, pe, c, x0a, x0b, x1a, x1b, y0a, y0b, y1a, y1b, after,
    z1_out, w1_out, sw_out, sw_beside, sw_ghost, s_ghost, w_ghost,
):
    place = places()
    middle = all_ghosts((zs, ic, pe), x0a, x0b, x1a, x1b)
    early = [side(...) for side in below_above(place[1], 16, y0a, y0b)]
    late = [side(...) for side in below_above(place[1], 16, y1a, y1b)]

    def plane(field, x):
        d = ghost_rows(field, x)
        here = middle(field, x)
        if not d:
            blank = jnp.zeros((8, CZ), F32)
            return jnp.concatenate([blank, here, blank], axis=0)
        rows, (near, far) = (EARLY_ROWS, early) if (field, x) in EARLY_ROWS else (LATE_ROWS, late)
        at = row_of(rows, (field, x))
        blank = jnp.zeros((8 - d, CZ), F32)
        return jnp.concatenate([blank, near[at : at + d], here, far[at : at + d], blank], axis=0)

    def neighbours(get, x):
        mid = get(x)
        count = mid.shape[0]
        return couple(get(x - 1), mid, get(x + 1), pltpu.roll(mid, 1, 0), pltpu.roll(mid, count - 1, 0))

    z = {x: plane(0, x) for x in range(-4, CX + 4)}
    inv = {x: plane(1, x) for x in range(-3, CX + 3)}
    first = {}
    for x in range(-3, CX + 3):
        first[x] = 1.2 * z[x] + 0.8 * inv[x] * neighbours(z.get, x) + plane(2, x)
    zw = {}
    for x in range(-2, CX + 2):
        beside = neighbours(first.get, x)
        zw[x] = 0.8 * (first[x] - inv[x] * beside)
        if 0 <= x < CX:
            z1_out[x] = first[x][8:16]
            w1_out[x] = c[x] * first[x][8:16] - beside[8:16]
    for x in range(-1, CX + 1):
        smooth = 1.2 * zw[x] + 0.8 * inv[x] * neighbours(zw.get, x)
        if not 0 <= x < CX:
            sw_beside[0 if x < 0 else 1] = smooth[8:16]
            continue
        sw_out[x] = smooth[8:16]
        for at, row in ((x, 7), (CX + x, 16)):
            iv = inv[x][row : row + 1]
            scale = jnp.where(iv > 0.0, 1.25 / jnp.where(iv > 0.0, iv, 1.0), 0.0)
            sw_ghost[at : at + 1, :] = smooth[row : row + 1]
            s_ghost[at : at + 1, :] = z[x][row : row + 1] * scale
            w_ghost[at : at + 1, :] = zw[x][row : row + 1] * scale


def products_kernel(
    s, w1, sw, pe2, c, xa, xb, sw_beside, sw_ghost, s_ghost, w_ghost, pe_face, e_face, beside, pay
):
    place = places()
    below, above = [side(...) for side in below_above(place[0], 8, xa, xb)]
    sums = [jnp.zeros((CY, CZ), F32) for _ in range(6)]
    row = iota((CY, CZ), 0)
    rims = [None] * (2 * CX)
    p = [below + sw_beside[0], *(sw[x] + pe2[x] for x in range(CX)), above + sw_beside[1]]
    for x in range(CX):
        left, mid, right = p[x : x + 3]
        up = jnp.where(row == 0, sw_ghost[x : x + 1, :], pltpu.roll(mid, 1, 0))
        down = jnp.where(row == CY - 1, sw_ghost[CX + x : CX + x + 1, :], pltpu.roll(mid, CY - 1, 0))
        q = c[x] * mid - couple(left, mid, right, up, down)
        rims[x], rims[CX + x] = q[0:1], q[CY - 1 : CY]
        a, b = s[x], w1[x]
        for k, term in enumerate((a * a, a * b, a * q, b * b, b * q, q * q)):
            sums[k] = sums[k] + term
    exists = rim_exists(place[1])
    face = pe_face[...]
    sums[2] = sums[2] - 8.0 * face * s_ghost[...]
    sums[4] = sums[4] - 8.0 * face * w_ghost[...]
    sums[5] = sums[5] + jnp.where(exists, 64.0 * face * face, 0.0)
    rim = jnp.where(exists, jnp.concatenate(rims, axis=0), 0.0)
    lane = iota((8, LANES), 1)
    top = jnp.broadcast_to(rim_restrict(rim, beside[...]), (8, LANES))
    for k in range(6):
        top = top + jnp.where(lane == 9 + k, jnp.sum(sums[k], keepdims=True), 0.0)
    tile = jnp.where((iota((8, LANES), 0) & 1) == 0, top, e_face[...])
    for i in range(DEVICES // 4):
        pay[pl.ds(8 * i, 8), :] = tile


def update_kernel(parts, z1, smooth, pe2, s_old, rate, mobile, immobile):
    top = parts[pl.ds(0, DEVICES, stride=2), :]
    face = pltpu.roll(parts[pl.ds(1, DEVICES, stride=2), :], LANES // 2, 1)
    lane = iota((DEVICES, LANES), 1)
    other = jnp.where(lane < LANES // 2, pltpu.roll(face, 1, 0), pltpu.roll(face, DEVICES - 1, 0))
    cross = jnp.sum(jnp.where((lane & 15) < 9, top * other, 0.0), keepdims=True)
    total = jnp.sum(top, axis=0, keepdims=True)
    ss, sw, sq, ww, wq, qq = [total[:, 9 + k : 10 + k] for k in range(6)]
    qq = qq - 16.0 * cross
    factor = wq / ww
    y2 = (sq - factor * sw) / (qq - factor * wq)
    y1 = (sw - wq * y2) / ww
    for x in range(CX):
        new = y1 * z1[x] + y2 * (smooth[x] + pe2[x])
        mobile[x] = new
        for k in range(RATES):
            r = rate[k, x]
            immobile[k, x] = (s_old[k, x] + r * new) / (1.0 + r)


def call(kernel, ins, outs, scratch=(), flops=10_000, vmem=48 << 20):
    shapes = [jax.ShapeDtypeStruct(shape, dtype) for shape, dtype in outs]
    return pl.pallas_call(
        kernel,
        out_shape=shapes,
        in_specs=ins,
        out_specs=[VM] * len(shapes),
        scratch_shapes=list(scratch),
        cost_estimate=pl.CostEstimate(flops=flops, bytes_accessed=100_000, transcendentals=0),
        compiler_params=pltpu.CompilerParams(vmem_limit_bytes=vmem),
    )


FIELD = ((CX, CY, CZ), F32)
SOURCE_VMEM = 63 << 20
FIRST_UNROLL = 8
SECOND_UNROLL = 8


def swap_pairs(axis):
    n, m = lax.axis_size("coarse"), lax.axis_size("fine")
    inside, between = [], []
    for c in range(n):
        for f in range(m):
            me = c * m + f
            at, count, step = (c, n, m) if axis == "coarse" else (f, m, 1)
            inside.append((me, me + ((at ^ 1) - at) * step))
            if 0 < at < count - 1:
                between.append((me, me + (((at - 1) ^ 1) + 1 - at) * step))
            elif axis == "fine":
                between.append((me, (c ^ 1) * m + f))
            else:
                between.append((me, (n - 1 - c) * m + f))
    return inside, between


def swap_between(b, axis):
    return lax.ppermute(b, BOTH, swap_pairs(axis)[1])


def trade(a, b, axis):
    b = swap_between(b, axis)
    return lax.ppermute(a, BOTH, swap_pairs(axis)[0]), b


def everyone(pay, rows):
    moved = lax.all_to_all(pay.reshape(DEVICES, rows, LANES), BOTH, 0, 0)
    return moved.reshape(DEVICES * rows, LANES)


def local(
    c_old, s_old, rate_time, capacity, agg_count, coarse_order, coarse_cols, coarse_off, coarse_diag
):
    order = coarse_order.reshape(LANES, LANES)
    c, ic, s, zs, tab, both, x0b, y0a, y0b, pay = call(
        source_kernel, [VM, SM, VM, HB, HB] + [VM] * 5,
        [
            FIELD, FIELD, FIELD, FIELD, ((TABLE_ROWS, 256), F32), ((TABLE_ROWS + 7 * CY, 256), F32),
            ((7 * CY, CZ), F32), ((row_count(EARLY_ROWS), CZ), F32), ((row_count(EARLY_ROWS), CZ), F32),
            ((4 * DEVICES, LANES), F32),
        ],
        scratch=[
            pltpu.VMEM((RATES, CX, CY, CZ), F32),
            pltpu.VMEM((RATES, CX, CY, CZ), F32),
            pltpu.SemaphoreType.DMA((2, CX)),
        ],
        vmem=SOURCE_VMEM,
    )(
        capacity.reshape(1, RATES), agg_count, c_old, s_old, rate_time, coarse_diag.reshape(1, SHARD_ROWS), coarse_cols, coarse_off,
        coarse_diag.reshape(16, LANES), order,
    )
    other_core = [(i, i ^ 1) for i in range(8)]
    both = lax.ppermute(both, "coarse", other_core)
    tabs = []
    for hop in (2, 4, 6):
        shard = lax.ppermute(tab, "coarse", [(i, i ^ hop) for i in range(8)])
        tabs += [shard, lax.ppermute(shard, "coarse", other_core)]
    x0b = swap_between(x0b, "coarse")
    y0a, y0b = trade(y0a, y0b, "fine")
    pay, both = lax.optimization_barrier((pay, both))
    tabs = [tab, both] + tabs
    gathered = everyone(pay, 4)

    pe, plan, own, own_count, beside, across, at_row, at_lane, counts, x1a, x1b = call(
        first_kernel, [VM] * 10,
        [
            FIELD, ((KC + 1, 24, SLOTS), F32), ((8, SLOTS), F32), ((8, LANES), I32), ((8, LANES), I32), ((2, 8, LANES), I32),
            ((LANES, LANES), I32), ((8, LANES), I32), ((LANES, LANES), I32),
            ((3 * CY, CZ), F32), ((3 * CY, CZ), F32),
        ],
        scratch=[pltpu.VMEM((SHARDS * 32, SHARD_ROWS), BF16)],
    )(gathered, order, *tabs)
    x1a, x1b = trade(x1a, x1b, "coarse")
    (pay,) = call(early_kernel, [VM] * 11, [((4 * DEVICES, LANES), F32)])(
        own_count, beside, across, zs, ic, pe, c, both, x0b, y0a, y0b
    )
    sums = everyone(pay, 4)
    y1a, y1b = call(widen_kernel, [VM] * 7, [((row_count(LATE_ROWS), CZ), F32)] * 2)(
        zs, ic, pe, both, x0b, x1a, x1b
    )
    y1a, y1b = trade(y1a, y1b, "fine")

    pe2, pe_face, e_face, xa, xb = call(
        second_solve_kernel, [VM] * 9,
        [FIELD, ((CY, CZ), F32), ((8, LANES), F32), ((CY, CZ), F32), ((CY, CZ), F32)], flops=100_000_000,
    )(own_count, sums, gathered, order, plan, own, at_row, at_lane, counts)
    xa, xb = trade(xa, xb, "coarse")
    z1, w1, sw, sw_beside, sw_ghost, s_ghost, w_ghost = call(
        direction_kernel, [VM] * 13, [FIELD, FIELD, FIELD, ((2, CY, CZ), F32)] + [((CY, CZ), F32)] * 3,
    )(zs, ic, pe, c, both, x0b, x1a, x1b, y0a, y0b, y1a, y1b, e_face)
    (pay,) = call(
        products_kernel, [VM] * 14, [((2 * DEVICES, LANES), F32)]
    )(s, w1, sw, pe2, c, xa, xb, sw_beside, sw_ghost, s_ghost, w_ghost, pe_face, e_face, beside)
    parts = everyone(pay, 2)
    mobile, immobile = call(
        update_kernel, [VM] * 6, [FIELD, ((RATES, CX, CY, CZ), F32)]
    )(parts, z1, sw, pe2, s_old, rate_time)
    return mobile, immobile


def solution(mesh):
    return jax.shard_map(
        local,
        mesh=mesh,
        in_specs=(
            P("coarse", "fine", None),
            P(None, "coarse", "fine", None),
            P(None, "coarse", "fine", None),
            P(),
            P(("coarse", "fine")),
            P(),
            P(None, "coarse"),
            P(None, "coarse"),
            P("coarse"),
        ),
        out_specs=(P("coarse", "fine", None), P(None, "coarse", "fine", None)),
        check_vma=False,
    )
```

```python
import jax
import jax.numpy as jnp
from jax import lax
from jax.experimental import pallas as pl
from jax.experimental.pallas import tpu as pltpu
from jax.sharding import PartitionSpec as P

BOTH = ("coarse", "fine")
CX, CY, CZ = 4, 8, 256
RATES = 16
KC = 8
DEVICES = 128
LANES = 128
SLOTS = 256
SHARDS = 8
SHARD_ROWS = 2048
FLOW = 50.0
TABLE_ROWS = 128
UNUSED = 1e30
F32, BF16, I32 = jnp.float32, jnp.bfloat16, jnp.int32
VM = pl.BlockSpec(memory_space=pltpu.VMEM)
SM = pl.BlockSpec(memory_space=pltpu.SMEM)
HB = pl.BlockSpec(memory_space=pltpu.HBM)


def places():
    return lax.axis_index("coarse").astype(I32), lax.axis_index("fine").astype(I32)


def iota(shape, dim):
    return lax.broadcasted_iota(I32, shape, dim)


def lane_take(table, index):
    return jnp.take_along_axis(table, index, axis=1, mode="promise_in_bounds")


def nt(left, right):
    return lax.dot_general(left, right, (((1,), (1,)), ((), ())), preferred_element_type=F32)


def nn(left, right):
    return jnp.dot(left, right, preferred_element_type=F32)


def split2(values):
    high = values.astype(BF16)
    return high, (values - high.astype(F32)).astype(BF16)


def slots_of(plane, half, count):
    row = (plane * CY + iota((CY, LANES), 0)) * 2 + half
    return ((row * LANES + iota((CY, LANES), 1)) * count) >> 13


def restrict_plane(values, plane, count, totals, base):
    lane = iota((CY, LANES), 1)
    for half in range(2):
        part_of = values[:, half * LANES : (half + 1) * LANES]
        row = (plane * CY + iota((CY, LANES), 0)) * 2 + half
        first = (row * count) >> 6
        member = slots_of(plane, half, count) - first
        relative = lane + (base - first)
        for k in range(5):
            part = jnp.sum(jnp.where(member == k, part_of, 0.0), axis=1, keepdims=True)
            totals = [t + jnp.where(relative == k - LANES * i, part, 0.0) for i, t in enumerate(totals)]
    return totals


def restrict(cells, count):
    totals = [jnp.zeros((CY, LANES), F32)] * 2
    for plane in range(CX):
        totals = restrict_plane(cells[plane], plane, count, totals, 0)
    return [jnp.sum(t, axis=0, keepdims=True) for t in totals]


def rim_restrict(rim, count):
    n = jnp.concatenate([count, count], axis=1)
    row = iota((CY, CZ), 0)
    cells = ((row & 3) * CY + jnp.where(row < 4, CY - 1, 0)) * CZ
    member = (((cells + iota((CY, CZ), 1)) * n) >> 13) - ((cells * n) >> 13)
    lane = iota((8, LANES), 1)
    start = iota((8, LANES), 0) * 16
    spread = jnp.zeros((8, LANES), F32)
    for k in range(9):
        part = jnp.sum(jnp.where(member == k, rim, 0.0), axis=1, keepdims=True)
        spread = spread + jnp.where(lane == start + k, part, 0.0)
    return jnp.sum(spread, axis=0, keepdims=True)


def rim_exists(index):
    return jnp.where(iota((CY, CZ), 0) < 4, index, 15 - index) > 0


def prolong(entries, count):
    low = jnp.broadcast_to(entries[:, :LANES], (CY, LANES))
    high = jnp.broadcast_to(entries[:, LANES:], (CY, LANES))
    planes = []
    for plane in range(CX):
        halves = []
        for half in range(2):
            slot = slots_of(plane, half, count)
            place = slot & 127
            halves.append(jnp.where(slot < LANES, lane_take(low, place), lane_take(high, place)))
        planes.append(jnp.concatenate(halves, axis=1))
    return planes


def couple(left, mid, right, up, down):
    length = mid.shape[1]
    lane = iota(mid.shape, 1)
    behind = jnp.where(lane == 0, 0.0, pltpu.roll(mid, 1, 1))
    ahead = jnp.where(lane == length - 1, 0.0, pltpu.roll(mid, length - 1, 1))
    return 8.0 * (left + right + up + down + ahead) + 10.0 * behind


def source_kernel(
    cap, count, c_old, s_old_hbm, rate_hbm, diag, cols, off, diag_rows, order,
    c_out, ic_out, s_out, zs_out, tab, both, xb, ya, yb, pay, s_old, rate, sems,
):
    copies = []
    for x in range(CX):
        pair = (
            pltpu.make_async_copy(rate_hbm.at[:, x], rate.at[:, x], sems.at[0, x]),
            pltpu.make_async_copy(s_old_hbm.at[:, x], s_old.at[:, x], sems.at[1, x]),
        )
        for copy in pair:
            copy.start()
        copies.append(pair)
    for j in range(SHARD_ROWS // 256):
        at = slice(256 * j, 256 * j + 256)
        part = jnp.concatenate([cols[:, at].astype(F32), off[:, at] * (0.8 / diag[:, at])], axis=0)
        tab[16 * j : 16 * j + 16, :] = part
        both[16 * j : 16 * j + 16, :] = part
    place = places()
    n = jnp.full((CY, LANES), count[0], I32)
    mine = (order[0:1, :] >> 7) == place[0] * 16 + place[1]
    low = jnp.sum(jnp.where(mine, (order[...] & 127).astype(F32), 0.0), axis=1, keepdims=True)
    spot = iota((LANES, LANES), 1).astype(F32) == low
    at_place = jnp.sum(jnp.where(spot, iota((LANES, LANES), 0).astype(F32), 0.0), axis=0, keepdims=True)
    shares = [jnp.broadcast_to(cap[0:1, k : k + 1], (CY, CZ)) for k in range(RATES)]
    smooth, inverse, sources = [], [], []
    for x in range(CX):
        for copy in copies[x]:
            copy.wait()
        mass = jnp.zeros((CY, CZ), F32)
        extra = jnp.zeros((CY, CZ), F32)
        for k in range(RATES):
            r = rate[k, x]
            weighted = shares[k] * (r / (1.0 + r))
            mass = mass + weighted
            extra = extra + weighted * s_old[k, x]
        centre = (1.0 + mass) + FLOW
        source = c_old[x] + extra
        inv = 1.0 / centre
        c_out[x] = centre
        ic_out[x] = inv
        s_out[x] = source
        zs_out[x] = 0.8 * source * inv
        smooth.append(0.8 * source * inv)
        inverse.append(inv)
        sources.append(source)
    xa, xb[...] = send_planes([(smooth, 4), (inverse, 3)])
    both[TABLE_ROWS:, :] = xa
    ya[...], yb[...] = send_rows(EARLY_ROWS, lambda f, x: (smooth, inverse)[f][x])
    slot = iota((1, LANES), 1)
    sums = [jnp.where(slot + LANES * i < n[0:1], t, UNUSED) for i, t in enumerate(restrict(sources, n))]
    repeat4(pay, [*sums, diag_rows[pl.ds(place[1], 1), :], at_place])


def send_planes(fields):
    even = (places()[0] & 1) == 0
    upper = jnp.concatenate([p for planes, depth in fields for p in planes[CX - depth :]], axis=0)
    lower = jnp.concatenate([p for planes, depth in fields for p in planes[:depth]], axis=0)
    return jnp.where(even, upper, lower), jnp.where(even, lower, upper)


def ghost_rows(field, x):
    return max(0, (4, 3, 3)[field] - max(0, -x, x - CX + 1))


EARLY_ROWS = [(f, x) for f in range(2) for x in range(CX)]
LATE_ROWS = [(f, x) for f in range(3) for x in range(-3, CX + 3) if ghost_rows(f, x) and (f, x) not in EARLY_ROWS]


def row_of(rows, which):
    return sum(ghost_rows(*w) for w in rows[: rows.index(which)])


def row_count(rows):
    return sum(ghost_rows(*w) for w in rows)


def send_rows(rows, plane):
    even = (places()[1] & 1) == 0
    upper = jnp.concatenate([plane(*w)[CY - ghost_rows(*w) :] for w in rows], axis=0)
    lower = jnp.concatenate([plane(*w)[: ghost_rows(*w)] for w in rows], axis=0)
    return jnp.where(even, upper, lower), jnp.where(even, lower, upper)


def repeat4(pay, rows):
    kind = iota((8, LANES), 0) & 3
    tile = jnp.broadcast_to(rows[3], (8, LANES))
    for k in range(3):
        tile = jnp.where(kind == k, rows[k], tile)
    for i in range(DEVICES // 2):
        pay[pl.ds(8 * i, 8), :] = tile


def read_sums(gathered):
    low = gathered[pl.ds(0, DEVICES, stride=4), :]
    high = gathered[pl.ds(1, DEVICES, stride=4), :]
    diag = gathered[pl.ds(2, DEVICES, stride=4), :]
    inverse = gathered[pl.ds(3, DEVICES, stride=4), :].astype(I32)
    used = jnp.where(low < 0.5 * UNUSED, 1.0, 0.0) + jnp.where(high < 0.5 * UNUSED, 1.0, 0.0)
    return low, high, diag, inverse, jnp.sum(used, axis=1, keepdims=True)


def offsets_of(counts):
    row, lane = iota((LANES, LANES), 0), iota((LANES, LANES), 1)
    by_lane = jnp.sum(jnp.where(row < lane, counts, 0.0), axis=0, keepdims=True)
    across = jnp.sum(jnp.where(row == lane, counts, 0.0), axis=0, keepdims=True)
    by_row = jnp.sum(jnp.where(lane < row, across, 0.0), axis=1, keepdims=True)
    return jnp.broadcast_to(by_row, (LANES, LANES)).astype(I32), by_lane.astype(I32)


def blocks_of(order):
    return (iota((LANES, LANES), 0) == (order[0:1, :] >> 7)).astype(F32).astype(BF16)


def assemble(low, high, offsets, inverse, blocks):
    by_row, by_lane = offsets
    lane = iota((LANES, LANES), 1)
    shift = by_row & 127
    place = (lane - shift) & 127
    low = lane_take(low, place)
    high = lane_take(high, place)
    kept = lane >= shift
    rows = (jnp.where(kept, low, 0.0), jnp.where(kept, high, low), jnp.where(kept, 0.0, high))
    start = by_lane >> 7
    spots = [(iota((LANES, LANES), 0) == start + j).astype(F32).astype(BF16) for j in range(3)]
    parts = [jnp.concatenate(split2(r), axis=1) for r in rows]
    table = nn(jnp.concatenate(spots, axis=1), jnp.concatenate(parts, axis=0))
    by_block = nt(blocks, jnp.concatenate([table[:, :LANES], table[:, LANES:]], axis=0).astype(BF16))
    return lane_take(by_block[:, :LANES] + by_block[:, LANES:], inverse)


def one_hot(row16, index):
    return jnp.where(row16 == index.astype(BF16), jnp.ones(row16.shape, BF16), jnp.zeros(row16.shape, BF16))


def fetch(table, unknown, coarse):
    inner = unknown & (SHARD_ROWS - 1)
    shard = (unknown >> 11) ^ coarse
    row16 = iota((256, SLOTS), 0).astype(F32).astype(BF16)
    found = jnp.zeros((SHARDS * 32, SLOTS), F32)
    for chunk in range(SHARD_ROWS // 256):
        spot = one_hot(row16, (inner - chunk * 256).astype(F32))
        found = found + nn(table[:, chunk * 256 : (chunk + 1) * 256], spot)
    found = found.reshape(SHARDS, 32, SLOTS)
    picked = found[0]
    for g in range(1, SHARDS):
        picked = jnp.where(shard == g, found[g], picked)
    return picked[0:8], picked[8:16], picked[16:24] + picked[24:32]


def gatherer(values):
    high, low = split2(values.T)
    table = jnp.concatenate([high, low], axis=1)
    row = iota((LANES, SLOTS), 0).astype(F32)
    row16 = row.astype(BF16)

    def gather(block, inner):
        spot = one_hot(row16, block)
        found = nn(table, jnp.concatenate([spot, spot], axis=0))
        kept = jnp.zeros((8, SLOTS), F32)
        for b in range(0, LANES, 8):
            kept = jnp.where(row[b : b + 8] == inner, found[b : b + 8], kept)
        return kept

    return gather


def solve_entry(gather, first, parts):
    total = -1.4 * gather(first[0], first[1])
    for j in range(KC):
        total = total + parts[2][j : j + 1] * gather(parts[0][j : j + 1], parts[1][j : j + 1])
    return first[2] * total


def coarse_solve(values, plan, own):
    gather = gatherer(values)

    def column(k, total):
        first = [plan[KC, pl.ds(8 * i + k, 1), :] for i in range(3)]
        return total + solve_entry(gather, first, [plan[k, 8 * i : 8 * i + 8, :] for i in range(3)])

    total = lax.fori_loop(0, KC, column, 1.24 * gather(own[0:1, :], own[1:2, :]), unroll=SECOND_UNROLL)
    return jnp.sum(total, axis=0, keepdims=True)


def plan_rows(ref, k, parts):
    ref[k, 0:8, :] = parts[0]
    ref[k, 8:16, :] = parts[1]
    ref[k, 16:24, :] = parts[2]


def first_kernel(
    gathered, order, tab0, tab1, tab2, tab3, tab4, tab5, tab6, tab7,
    pe_out, plan, own, own_count, beside, across, at_row, at_lane, counts_out, xa, xb, table,
):
    place = places()
    me = place[0] * 16 + place[1]
    low, high, diag, inverse, counts = read_sums(gathered)
    offsets = offsets_of(counts)
    at_row[...] = offsets[0]
    at_lane[...] = jnp.broadcast_to(offsets[1], (8, LANES))
    sums = assemble(
        jnp.where(low < 0.5 * UNUSED, low, 0.0), jnp.where(high < 0.5 * UNUSED, high, 0.0),
        offsets, inverse, blocks_of(order),
    )
    values = 0.8 * sums / diag
    counts = jnp.broadcast_to(counts, (LANES, LANES))
    counts_out[...] = counts.astype(I32)
    row = iota((LANES, LANES), 0)

    def count_of(device):
        found = jnp.sum(jnp.where(row == device, counts, 0.0), axis=0, keepdims=True)
        return jnp.broadcast_to(found, (8, LANES)).astype(I32)

    n = count_of(me)
    own_count[...] = n
    beside[...] = jnp.where(iota((8, LANES), 0) < 4, count_of(me - 1), count_of(me + 1))
    across[0] = count_of(me - 16)
    across[1] = count_of(me + 16)

    tabs = (tab0, tab1, tab2, tab3, tab4, tab5, tab6, tab7)
    for g in range(SHARDS):
        for j in range(SHARD_ROWS // 256):
            at = slice(256 * j, 256 * j + 256)
            cols = tabs[g][16 * j : 16 * j + 8, :]
            big = jnp.floor(cols * (1.0 / 128.0))
            pair = jnp.concatenate([big, cols - 128.0 * big], axis=0)
            table[32 * g : 32 * g + 16, at] = pair.astype(BF16)
            off = tabs[g][16 * j + 8 : 16 * j + 16, :]
            big = off.astype(BF16).astype(F32)
            table[32 * g + 16 : 32 * g + 32, at] = jnp.concatenate([big, off - big], axis=0).astype(BF16)

    mine = jnp.sum(jnp.where(row == me, offsets[0].astype(F32), 0.0), axis=0, keepdims=True).astype(I32)
    numbers = order[...].astype(F32)
    start = mine >> 7
    lines = []
    spread = (iota((8, LANES), 1) + mine) & 127
    for j in range(3):
        line = jnp.sum(jnp.where(row == start + j, numbers, 0.0), axis=0, keepdims=True)
        lines.append(lane_take(jnp.broadcast_to(line, (8, LANES)), spread))
    inside = iota((8, LANES), 1) + (mine & 127) < LANES
    unknown = jnp.concatenate(
        [jnp.where(inside, lines[0], lines[1]), jnp.where(inside, lines[1], lines[2])], axis=1
    )[0:1].astype(I32)
    own[0:1, :] = (unknown >> 7).astype(F32)
    own[1:2, :] = (unknown & 127).astype(F32)
    plan_rows(plan, KC, fetch(table, unknown, place[0]))

    def column(k, carry):
        col = 128.0 * plan[KC, pl.ds(k, 1), :] + plan[KC, pl.ds(8 + k, 1), :]
        plan_rows(plan, k, fetch(table, col.astype(I32), place[0]))
        return carry

    lax.fori_loop(0, KC, column, 0, unroll=FIRST_UNROLL)
    pe = prolong(coarse_solve(values, plan, own), n)
    for x in range(CX):
        pe_out[x] = pe[x]

    xa[...], xb[...] = send_planes([(pe, 3)])


def below_above(index, count, a, b):
    even = (index & 1) == 0
    inner = jnp.logical_and(index > 0, index < count - 1)

    def near(i):
        if i is not ...:
            i = slice(CY * i, CY * i + CY)
        return a[i], jnp.where(inner, b[i], 0.0)

    def below(i):
        first, second = near(i)
        return jnp.where(even, second, first)

    def above(i):
        first, second = near(i)
        return jnp.where(even, first, second)

    return below, above


def with_ghosts(own, messages):
    def plane(field, x):
        if 0 <= x < CX:
            return own[field][x]
        below, above, base, depth = messages[field]
        return below(base + depth + x) if x < 0 else above(base + x - CX)

    return plane


def widen(plane, fields, ya, yb):
    even = (places()[1] & 1) == 0
    upper, lower = [], []
    for f in fields:
        for x in range(-3, CX + 3):
            d = ghost_rows(f, x)
            if d:
                here = plane(f, x)
                upper.append(here[CY - d :])
                lower.append(here[:d])
    upper, lower = jnp.concatenate(upper, axis=0), jnp.concatenate(lower, axis=0)
    ya[...] = jnp.where(even, upper, lower)
    yb[...] = jnp.where(even, lower, upper)


def all_ghosts(own, x0a, x0b, x1a, x1b):
    early = below_above(places()[0], 8, x0a.at[TABLE_ROWS:], x0b)
    late = below_above(places()[0], 8, x1a, x1b)
    return with_ghosts(own, ((*early, 0, 4), (*early, 4, 3), (*late, 0, 3)))


def widen_kernel(zs, ic, pe, x0a, x0b, x1a, x1b, ya, yb):
    plane = all_ghosts((zs, ic, pe), x0a, x0b, x1a, x1b)
    ya[...], yb[...] = send_rows(LATE_ROWS, plane)


def early_kernel(count, beside, across, zs, ic, pe, c, xa, xb, ya, yb, pay):
    place = places()
    n = count[...]
    below, above = below_above(place[0], 8, xa.at[TABLE_ROWS:], xb)
    near, far = [side(...) for side in below_above(place[1], 16, ya, yb)]
    row = iota((CY, CZ), 0)
    z1 = []
    for x in range(CX):
        mid = zs[x]
        left = zs[x - 1] if x else below(3)
        right = zs[x + 1] if x + 1 < CX else above(0)
        at = row_of(EARLY_ROWS, (0, x))
        last = at + ghost_rows(0, x) - 1
        up = jnp.where(row == 0, near[last : last + 1], pltpu.roll(mid, 1, 0))
        down = jnp.where(row == CY - 1, far[at : at + 1], pltpu.roll(mid, CY - 1, 0))
        z1.append(1.2 * mid + 0.8 * ic[x] * couple(left, mid, right, up, down) + pe[x])
    image = []
    zero = jnp.zeros((CY, CZ), F32)
    for x in range(CX):
        mid = z1[x]
        up = jnp.where(row == 0, 0.0, pltpu.roll(mid, 1, 0))
        down = jnp.where(row == CY - 1, 0.0, pltpu.roll(mid, CY - 1, 0))
        left = z1[x - 1] if x else zero
        right = z1[x + 1] if x + 1 < CX else zero
        image.append(c[x] * mid - couple(left, mid, right, up, down))
    sums = restrict(image, n)
    blank = [jnp.zeros((CY, LANES), F32)]
    lane = iota((1, LANES), 1)
    under, over = across[0], across[1]
    (down_x,) = restrict_plane(-8.0 * z1[0], CX - 1, under, blank, (3 * under) >> 2)
    (up_x,) = restrict_plane(-8.0 * z1[CX - 1], 0, over, blank, 0)
    down_x = jnp.where(place[0] > 0, jnp.sum(down_x, axis=0, keepdims=True), 0.0)
    up_x = jnp.where(place[0] < 7, jnp.sum(up_x, axis=0, keepdims=True), 0.0)
    along_x = jnp.where(lane < 64, down_x, pltpu.roll(jnp.broadcast_to(up_x, (8, LANES)), 64, 1)[0:1])
    rims = jnp.concatenate([z[0:1] for z in z1] + [z[CY - 1 : CY] for z in z1], axis=0)
    along_y = rim_restrict(jnp.where(rim_exists(place[1]), -8.0 * rims, 0.0), beside[...])
    repeat4(pay, [*sums, along_x, along_y])


def add_neighbours(low, high, from_x, from_y, counts):
    lane = iota((DEVICES, LANES), 1)

    def place(window, base, shift, length):
        nonlocal low, high
        relative = lane - base
        moved = lane_take(window, (relative + shift) & 127)
        low = low + jnp.where(jnp.logical_and(relative >= 0, relative < length), moved, 0.0)
        relative = relative + LANES
        high = high + jnp.where(jnp.logical_and(relative >= 0, relative < length), moved, 0.0)

    low = low + jnp.where(lane < 64, pltpu.roll(pltpu.roll(from_x, 16, 0), 64, 1), 0.0)
    place(pltpu.roll(from_x, DEVICES - 16, 0), (3 * counts) >> 2, 0, 64)
    both = jnp.where(lane < 64, pltpu.roll(from_y, DEVICES - 1, 0), pltpu.roll(from_y, 1, 0))
    for g in range(2 * CX):
        cells = ((g & 3) * CY + (CY - 1 if g < CX else 0)) * CZ
        place(both, (cells * counts) >> 13, 16 * g, 9)
    return low, high


def second_solve_kernel(
    count, sums, gathered, order, plan, own, at_row, at_lane, counts, pe_out, pe_face, e_face, xa, xb
):
    n = count[...]
    low, high = add_neighbours(
        sums[pl.ds(0, DEVICES, stride=4), :], sums[pl.ds(1, DEVICES, stride=4), :],
        sums[pl.ds(2, DEVICES, stride=4), :], sums[pl.ds(3, DEVICES, stride=4), :], counts[...],
    )
    diag = gathered[pl.ds(2, DEVICES, stride=4), :]
    inverse = gathered[pl.ds(3, DEVICES, stride=4), :].astype(I32)
    values = assemble(low, high, (at_row[...], at_lane[0:1, :]), inverse, blocks_of(order))
    entries = coarse_solve(0.8 * values / diag, plan, own)
    pe = prolong(entries, n)
    for x in range(CX):
        pe_out[x] = pe[x]
        pe_face[x : x + 1, :] = pe[x][0:1]
        pe_face[CX + x : CX + x + 1, :] = pe[x][CY - 1 : CY]
    xa[...], xb[...] = send_planes([(pe, 1)])
    lane = iota((8, LANES), 1)
    group = lane >> 4
    cells = ((group & 3) * CY + jnp.where(group < 4, 0, CY - 1)) * CZ
    slot = jnp.minimum(((cells * n) >> 13) + (lane & 15), SLOTS - 1)
    low = jnp.broadcast_to(entries[:, :LANES], (8, LANES))
    high = jnp.broadcast_to(entries[:, LANES:], (8, LANES))
    e_face[...] = jnp.where(slot < LANES, lane_take(low, slot & 127), lane_take(high, slot & 127))


def direction_kernel(
    zs, ic, pe, c, x0a, x0b, x1a, x1b, y0a, y0b, y1a, y1b, after,
    z1_out, w1_out, sw_out, sw_beside, sw_ghost, s_ghost, w_ghost,
):
    place = places()
    middle = all_ghosts((zs, ic, pe), x0a, x0b, x1a, x1b)
    early = [side(...) for side in below_above(place[1], 16, y0a, y0b)]
    late = [side(...) for side in below_above(place[1], 16, y1a, y1b)]

    def plane(field, x):
        d = ghost_rows(field, x)
        here = middle(field, x)
        if not d:
            blank = jnp.zeros((8, CZ), F32)
            return jnp.concatenate([blank, here, blank], axis=0)
        rows, (near, far) = (EARLY_ROWS, early) if (field, x) in EARLY_ROWS else (LATE_ROWS, late)
        at = row_of(rows, (field, x))
        blank = jnp.zeros((8 - d, CZ), F32)
        return jnp.concatenate([blank, near[at : at + d], here, far[at : at + d], blank], axis=0)

    def neighbours(get, x):
        mid = get(x)
        count = mid.shape[0]
        return couple(get(x - 1), mid, get(x + 1), pltpu.roll(mid, 1, 0), pltpu.roll(mid, count - 1, 0))

    z = {x: plane(0, x) for x in range(-4, CX + 4)}
    inv = {x: plane(1, x) for x in range(-3, CX + 3)}
    first = {}
    for x in range(-3, CX + 3):
        first[x] = 1.2 * z[x] + 0.8 * inv[x] * neighbours(z.get, x) + plane(2, x)
    zw = {}
    for x in range(-2, CX + 2):
        beside = neighbours(first.get, x)
        zw[x] = 0.8 * (first[x] - inv[x] * beside)
        if 0 <= x < CX:
            z1_out[x] = first[x][8:16]
            w1_out[x] = c[x] * first[x][8:16] - beside[8:16]
    for x in range(-1, CX + 1):
        smooth = 1.2 * zw[x] + 0.8 * inv[x] * neighbours(zw.get, x)
        if not 0 <= x < CX:
            sw_beside[0 if x < 0 else 1] = smooth[8:16]
            continue
        sw_out[x] = smooth[8:16]
        for at, row in ((x, 7), (CX + x, 16)):
            iv = inv[x][row : row + 1]
            scale = jnp.where(iv > 0.0, 1.25 / jnp.where(iv > 0.0, iv, 1.0), 0.0)
            sw_ghost[at : at + 1, :] = smooth[row : row + 1]
            s_ghost[at : at + 1, :] = z[x][row : row + 1] * scale
            w_ghost[at : at + 1, :] = zw[x][row : row + 1] * scale


def products_kernel(
    s, w1, sw, pe2, c, xa, xb, sw_beside, sw_ghost, s_ghost, w_ghost, pe_face, e_face, beside, pay
):
    place = places()
    below, above = [side(...) for side in below_above(place[0], 8, xa, xb)]
    sums = [jnp.zeros((CY, CZ), F32) for _ in range(6)]
    row = iota((CY, CZ), 0)
    rims = [None] * (2 * CX)
    p = [below + sw_beside[0], *(sw[x] + pe2[x] for x in range(CX)), above + sw_beside[1]]
    for x in range(CX):
        left, mid, right = p[x : x + 3]
        up = jnp.where(row == 0, sw_ghost[x : x + 1, :], pltpu.roll(mid, 1, 0))
        down = jnp.where(row == CY - 1, sw_ghost[CX + x : CX + x + 1, :], pltpu.roll(mid, CY - 1, 0))
        q = c[x] * mid - couple(left, mid, right, up, down)
        rims[x], rims[CX + x] = q[0:1], q[CY - 1 : CY]
        a, b = s[x], w1[x]
        for k, term in enumerate((a * a, a * b, a * q, b * b, b * q, q * q)):
            sums[k] = sums[k] + term
    exists = rim_exists(place[1])
    face = pe_face[...]
    sums[2] = sums[2] - 8.0 * face * s_ghost[...]
    sums[4] = sums[4] - 8.0 * face * w_ghost[...]
    sums[5] = sums[5] + jnp.where(exists, 64.0 * face * face, 0.0)
    rim = jnp.where(exists, jnp.concatenate(rims, axis=0), 0.0)
    lane = iota((8, LANES), 1)
    top = jnp.broadcast_to(rim_restrict(rim, beside[...]), (8, LANES))
    for k in range(6):
        top = top + jnp.where(lane == 9 + k, jnp.sum(sums[k], keepdims=True), 0.0)
    tile = jnp.where((iota((8, LANES), 0) & 1) == 0, top, e_face[...])
    for i in range(DEVICES // 4):
        pay[pl.ds(8 * i, 8), :] = tile


def update_kernel(parts, z1, smooth, pe2, s_old, rate, mobile, immobile):
    top = parts[pl.ds(0, DEVICES, stride=2), :]
    face = pltpu.roll(parts[pl.ds(1, DEVICES, stride=2), :], LANES // 2, 1)
    lane = iota((DEVICES, LANES), 1)
    other = jnp.where(lane < LANES // 2, pltpu.roll(face, 1, 0), pltpu.roll(face, DEVICES - 1, 0))
    cross = jnp.sum(jnp.where((lane & 15) < 9, top * other, 0.0), keepdims=True)
    total = jnp.sum(top, axis=0, keepdims=True)
    ss, sw, sq, ww, wq, qq = [total[:, 9 + k : 10 + k] for k in range(6)]
    qq = qq - 16.0 * cross
    factor = wq / ww
    y2 = (sq - factor * sw) / (qq - factor * wq)
    y1 = (sw - wq * y2) / ww
    for x in range(CX):
        new = y1 * z1[x] + y2 * (smooth[x] + pe2[x])
        mobile[x] = new
        for k in range(RATES):
            r = rate[k, x]
            immobile[k, x] = (s_old[k, x] + r * new) / (1.0 + r)


def call(kernel, ins, outs, scratch=(), flops=10_000, vmem=48 << 20):
    shapes = [jax.ShapeDtypeStruct(shape, dtype) for shape, dtype in outs]
    return pl.pallas_call(
        kernel,
        out_shape=shapes,
        in_specs=ins,
        out_specs=[VM] * len(shapes),
        scratch_shapes=list(scratch),
        cost_estimate=pl.CostEstimate(flops=flops, bytes_accessed=100_000, transcendentals=0),
        compiler_params=pltpu.CompilerParams(vmem_limit_bytes=vmem),
    )


FIELD = ((CX, CY, CZ), F32)
SOURCE_VMEM = 63 << 20
FIRST_UNROLL = 8
SECOND_UNROLL = 8


def swap_pairs(axis):
    n, m = lax.axis_size("coarse"), lax.axis_size("fine")
    inside, between = [], []
    for c in range(n):
        for f in range(m):
            me = c * m + f
            at, count, step = (c, n, m) if axis == "coarse" else (f, m, 1)
            inside.append((me, me + ((at ^ 1) - at) * step))
            if 0 < at < count - 1:
                between.append((me, me + (((at - 1) ^ 1) + 1 - at) * step))
            elif axis == "fine":
                between.append((me, (c ^ 1) * m + f))
            else:
                between.append((me, (n - 1 - c) * m + f))
    return inside, between


def swap_between(b, axis):
    return lax.ppermute(b, BOTH, swap_pairs(axis)[1])


def trade(a, b, axis):
    b = swap_between(b, axis)
    return lax.ppermute(a, BOTH, swap_pairs(axis)[0]), b


def everyone(pay, rows):
    moved = lax.all_to_all(pay.reshape(DEVICES, rows, LANES), BOTH, 0, 0)
    return moved.reshape(DEVICES * rows, LANES)


def local(
    c_old, s_old, rate_time, capacity, agg_count, coarse_order, coarse_cols, coarse_off, coarse_diag
):
    order = coarse_order.reshape(LANES, LANES)
    c, ic, s, zs, tab, both, x0b, y0a, y0b, pay = call(
        source_kernel, [VM, SM, VM, HB, HB] + [VM] * 5,
        [
            FIELD, FIELD, FIELD, FIELD, ((TABLE_ROWS, 256), F32), ((TABLE_ROWS + 7 * CY, 256), F32),
            ((7 * CY, CZ), F32), ((row_count(EARLY_ROWS), CZ), F32), ((row_count(EARLY_ROWS), CZ), F32),
            ((4 * DEVICES, LANES), F32),
        ],
        scratch=[
            pltpu.VMEM((RATES, CX, CY, CZ), F32),
            pltpu.VMEM((RATES, CX, CY, CZ), F32),
            pltpu.SemaphoreType.DMA((2, CX)),
        ],
        vmem=SOURCE_VMEM,
    )(
        capacity.reshape(1, RATES), agg_count, c_old, s_old, rate_time, coarse_diag.reshape(1, SHARD_ROWS), coarse_cols, coarse_off,
        coarse_diag.reshape(16, LANES), order,
    )
    other_core = [(i, i ^ 1) for i in range(8)]
    both = lax.ppermute(both, "coarse", other_core)
    tabs = []
    for hop in (2, 4, 6):
        shard = lax.ppermute(tab, "coarse", [(i, i ^ hop) for i in range(8)])
        tabs += [shard, lax.ppermute(shard, "coarse", other_core)]
    x0b = swap_between(x0b, "coarse")
    y0a, y0b = trade(y0a, y0b, "fine")
    pay, both = lax.optimization_barrier((pay, both))
    tabs = [tab, both] + tabs
    gathered = everyone(pay, 4)

    pe, plan, own, own_count, beside, across, at_row, at_lane, counts, x1a, x1b = call(
        first_kernel, [VM] * 10,
        [
            FIELD, ((KC + 1, 24, SLOTS), F32), ((8, SLOTS), F32), ((8, LANES), I32), ((8, LANES), I32), ((2, 8, LANES), I32),
            ((LANES, LANES), I32), ((8, LANES), I32), ((LANES, LANES), I32),
            ((3 * CY, CZ), F32), ((3 * CY, CZ), F32),
        ],
        scratch=[pltpu.VMEM((SHARDS * 32, SHARD_ROWS), BF16)],
    )(gathered, order, *tabs)
    x1a, x1b = trade(x1a, x1b, "coarse")
    (pay,) = call(early_kernel, [VM] * 11, [((4 * DEVICES, LANES), F32)])(
        own_count, beside, across, zs, ic, pe, c, both, x0b, y0a, y0b
    )
    pay, x1a = lax.optimization_barrier((pay, x1a))
    sums = everyone(pay, 4)
    y1a, y1b = call(widen_kernel, [VM] * 7, [((row_count(LATE_ROWS), CZ), F32)] * 2)(
        zs, ic, pe, both, x0b, x1a, x1b
    )
    y1a, y1b = trade(y1a, y1b, "fine")

    pe2, pe_face, e_face, xa, xb = call(
        second_solve_kernel, [VM] * 9,
        [FIELD, ((CY, CZ), F32), ((8, LANES), F32), ((CY, CZ), F32), ((CY, CZ), F32)], flops=100_000_000,
    )(own_count, sums, gathered, order, plan, own, at_row, at_lane, counts)
    xa, xb = trade(xa, xb, "coarse")
    z1, w1, sw, sw_beside, sw_ghost, s_ghost, w_ghost = call(
        direction_kernel, [VM] * 13, [FIELD, FIELD, FIELD, ((2, CY, CZ), F32)] + [((CY, CZ), F32)] * 3,
    )(zs, ic, pe, c, both, x0b, x1a, x1b, y0a, y0b, y1a, y1b, e_face)
    (pay,) = call(
        products_kernel, [VM] * 14, [((2 * DEVICES, LANES), F32)]
    )(s, w1, sw, pe2, c, xa, xb, sw_beside, sw_ghost, s_ghost, w_ghost, pe_face, e_face, beside)
    parts = everyone(pay, 2)
    mobile, immobile = call(
        update_kernel, [VM] * 6, [FIELD, ((RATES, CX, CY, CZ), F32)]
    )(parts, z1, sw, pe2, s_old, rate_time)
    return mobile, immobile


def solution(mesh):
    return jax.shard_map(
        local,
        mesh=mesh,
        in_specs=(
            P("coarse", "fine", None),
            P(None, "coarse", "fine", None),
            P(None, "coarse", "fine", None),
            P(),
            P(("coarse", "fine")),
            P(),
            P(None, "coarse"),
            P(None, "coarse"),
            P("coarse"),
        ),
        out_specs=(P("coarse", "fine", None), P(None, "coarse", "fine", None)),
        check_vma=False,
    )
```
